32 devices in a mesh: grp: 8 (over z, x), sub: 4 (over y, core).
Axes of the slice: x: 2, y: 2, z: 4, core: 2. Of those that a mesh axis runs over, the one named last changes fastest.
Arguments:
- field: bfloat16 [64, 64, 32, 128], P('grp', 'sub'), may hold values from -6 to 6
- cotangent: bfloat16 [64, 64, 32, 128], P('grp', 'sub'), may hold values from -0.0390625 to 0.0390625
- fine_kernel: bfloat16 [3, 3, 3, 128, 128], replicated, may hold values from -0.109375 to 0.109375
- fine_bias: float32 [128], replicated, may hold values from -3 to 3
- coarse_kernel: bfloat16 [3, 3, 3, 128, 256], replicated, may hold values from -0.109375 to 0.109375
- coarse_bias: float32 [256], replicated, may hold values from -3 to 3
- merge_weight: bfloat16 [256, 128], replicated, may hold values from -0.375 to 0.375
Outputs:
- output: bfloat16 [64, 64, 32, 128], P('grp', 'sub')
- grad_fine_kernel: float32 [3, 3, 3, 128, 128], P(None, None, None, None, 'sub')
- grad_fine_bias: float32 [128], P('sub')
- grad_coarse_kernel: float32 [3, 3, 3, 128, 256], P(None, None, None, None, 'sub')
- grad_coarse_bias: float32 [256], P('sub')
- grad_merge_weight: float32 [256, 128], P('sub')
The draws below stay inside these ranges and needn't reach their ends.
All inputs are finite; a program needn't handle non-finite values.
Results may differ from the reference program's by a relative error of at most 0.02.
Values may be sent and summed in bfloat16 or wider, within the bound.
No kernel may reach another device: no remote copies, remote signals or barrier semaphores. Data moves between devices by JAX's collectives and lax.ppermute only.
A program may use at most 64 MiB of HBM per device.

```python
import jax
import jax.numpy as jnp
from jax import lax

C1 = 128
C2 = 256
BX = 8
BY = 16
BZ = 32
X = 64
Y = 64
Z = 32
N_GRP = 8
N_SUB = 4


def block_scale(key, extent, split, least, high):
    loudness = 1.0
    for position, parts in split:
        draws = jax.random.uniform(jax.random.fold_in(jax.random.fold_in(key, 6), position), (parts,), jnp.float32, least / len(split), high / len(split))
        loudness = loudness * jnp.repeat(jnp.exp(draws), extent[position] // parts).reshape((-1,) + (1,) * (len(extent) - 1 - position))
    return loudness


def normal_values(rng, extent, scale, limit, cuts=(), kind=jnp.bfloat16):
    factor_of = block_scale(rng, extent, cuts, -0.22, 0.18) if cuts else 1.0
    entries = jax.random.normal(rng, extent, jnp.float32) * scale * factor_of
    return jnp.minimum(jnp.maximum(entries, -limit), limit).astype(kind)


def setup_inputs(seed: int = 0) -> dict:
    seeds = jax.random.split(jax.random.key(seed), 8)
    return {
        "field": normal_values(seeds[0], (X, Y, Z, C1), 1.0, 6.0, ((0, 8), (1, 4))),
        "cotangent": normal_values(seeds[1], (X, Y, Z, C1), ((BX * BY * BZ * N_GRP * N_SUB) ** -0.5), 0.0390625, ((0, 8), (1, 4))),
        "fine_kernel": normal_values(seeds[2], (3, 3, 3, C1, C1), (27 * C1) ** -0.5, 0.109375),
        "fine_bias": normal_values(seeds[3], (C1,), 0.5, 3.0, (), jnp.float32),
        "coarse_kernel": normal_values(seeds[4], (3, 3, 3, C1, C2), (27 * C1) ** -0.5, 0.109375),
        "coarse_bias": normal_values(seeds[5], (C2,), 0.5, 3.0, (), jnp.float32),
        "merge_weight": normal_values(seeds[6], (C2, C1), C2 ** -0.5, 0.375),
    }


def conv_valid(padded, kernel):
    return lax.conv_general_dilated(padded[None], kernel, (1, 1, 1), 'VALID', dimension_numbers=('NDHWC', 'DHWIO', 'NDHWC'), preferred_element_type=jnp.float32)[0]

def pad_three(volume):
    return jnp.pad(volume, ((1, 1), (1, 1), (1, 1), (0, 0)))

def cube_sum(volume):
    sx, sy, sz, chans = volume.shape
    shaped = volume.astype(jnp.float32).reshape(sx // 2, 2, sy // 2, 2, sz // 2, 2, chans)
    return lax.optimization_barrier(jnp.sum(shaped, axis=(1, 3, 5)))

def upsample(volume):
    return jnp.repeat(jnp.repeat(jnp.repeat(volume, 2, 0), 2, 1), 2, 2)

def dsilu(value):
    sig = jax.nn.sigmoid(value)
    return sig * (1.0 + value * (1.0 - sig))

def kernel_grad(padded, slope):
    sx, sy, sz, cout = slope.shape
    flat_slope = slope.reshape(-1, cout)
    pieces = []
    for i in range(3):
        for j in range(3):
            for k in range(3):
                piece = padded[i:i + sx, j:j + sy, k:k + sz].reshape(-1, padded.shape[3])
                pieces.append(lax.dot_general(piece, flat_slope, (((0,), (0,)), ((), ())), preferred_element_type=jnp.float32))
    return jnp.stack(pieces).reshape(3, 3, 3, padded.shape[3], cout)

def reference(field, cotangent, fine_kernel, fine_bias, coarse_kernel, coarse_bias, merge_weight):
    field_pad = pad_three(field)
    pre_fine = conv_valid(field_pad, fine_kernel) + fine_bias
    hidden = jax.nn.silu(pre_fine).astype(jnp.bfloat16)
    pooled = (cube_sum(hidden) / 8.0).astype(jnp.bfloat16)
    pooled_pad = pad_three(pooled)
    pre_coarse = conv_valid(pooled_pad, coarse_kernel) + coarse_bias
    coarse = jax.nn.silu(pre_coarse).astype(jnp.bfloat16)
    cshape = coarse.shape
    projected = jnp.dot(coarse.reshape(-1, cshape[3]), merge_weight, preferred_element_type=jnp.float32).reshape(cshape[0], cshape[1], cshape[2], -1)
    output = (hidden.astype(jnp.float32) + upsample(projected)).astype(jnp.bfloat16)
    pooled_grad = cube_sum(cotangent).astype(jnp.bfloat16)
    flat_grad = pooled_grad.reshape(-1, pooled_grad.shape[3])
    grad_merge = lax.dot_general(coarse.reshape(-1, cshape[3]), flat_grad, (((0,), (0,)), ((), ())), preferred_element_type=jnp.float32)
    back = lax.dot_general(flat_grad, merge_weight, (((1,), (1,)), ((), ())), preferred_element_type=jnp.float32).reshape(cshape)
    coarse_slope = (back * dsilu(pre_coarse)).astype(jnp.bfloat16)
    grad_coarse_bias = lax.optimization_barrier(jnp.sum(coarse_slope.astype(jnp.float32), axis=(0, 1, 2)))
    grad_coarse = kernel_grad(pooled_pad, coarse_slope)
    flipped = jnp.transpose(coarse_kernel[::-1, ::-1, ::-1], (0, 1, 2, 4, 3))
    pooled_back = conv_valid(pad_three(coarse_slope), flipped)
    fine_back = cotangent.astype(jnp.float32) + upsample(pooled_back) / 8.0
    fine_slope = (fine_back * dsilu(pre_fine)).astype(jnp.bfloat16)
    grad_fine_bias = lax.optimization_barrier(jnp.sum(fine_slope.astype(jnp.float32), axis=(0, 1, 2)))
    grad_fine = kernel_grad(field_pad, fine_slope)
    return (output, grad_fine, grad_fine_bias, grad_coarse, grad_coarse_bias, grad_merge)
```

```python
import functools

import jax
import jax.numpy as jnp
from jax import lax
from jax.experimental import pallas as pl
from jax.experimental.pallas import tpu as pltpu
from jax.sharding import PartitionSpec as P

F32 = jnp.float32
BF16 = jnp.bfloat16
VMEM_LIMIT = 48 * 1024 * 1024


def call(body, name, args, outs, scratch=(), flops=0, nbytes=0):
    specs = [pl.BlockSpec(memory_space=pltpu.SMEM)]
    specs += [pl.BlockSpec(memory_space=pltpu.VMEM) for _ in args[1:]]
    return pl.pallas_call(
        body,
        name=name,
        out_shape=[jax.ShapeDtypeStruct(s, t) for s, t in outs],
        in_specs=specs,
        out_specs=[pl.BlockSpec(memory_space=pltpu.VMEM) for _ in outs],
        scratch_shapes=list(scratch),
        compiler_params=pltpu.CompilerParams(vmem_limit_bytes=VMEM_LIMIT),
        cost_estimate=pl.CostEstimate(flops=flops, bytes_accessed=nbytes, transcendentals=0),
    )(*args)


def put_faces(odd, first, second, low, high):
    first[...] = jnp.where(odd, low, high)
    second[...] = jnp.where(odd, high, low)


def get_faces(odd, first, second):
    a, b = first[...], second[...]
    return jnp.where(odd, a, b), jnp.where(odd, b, a)


def sum_cube(rows, planes, ref):
    half = rows // 2
    ref[pl.ds(0, rows), :] = planes
    return ref[pl.ds(0, half, stride=2), :] + ref[pl.ds(1, half, stride=2), :]


def shift_rows(value, step, depth):
    rows = value.shape[0]
    moved = pltpu.roll(value, step % rows, 0)
    place = lax.broadcasted_iota(jnp.int32, value.shape, 0) % depth
    edge = 0 if step == 1 else depth - 1
    return jnp.where(place == edge, 0.0, moved)


def sigmoid(value):
    return 1.0 / (1.0 + jnp.exp(-value))


def prep_body(par, lo, hi, cot, pg, out_a, out_b, tmp):
    bx, by, bz, c = cot.shape
    cx, cy, cz = bx // 2, by // 2, bz // 2
    total = jnp.sum(cot[...].astype(F32).reshape(cx, 2, cy, 2, bz, c), axis=(1, 3))
    grad = sum_cube(cx * cy * bz, total.reshape(cx * cy * bz, c), tmp).astype(BF16)
    pg[...] = grad.reshape(cx, cy, cz, c)
    face = cy * cz
    low = jnp.concatenate([lo[0].reshape(by * bz, c), grad[:face]], axis=0)
    high = jnp.concatenate([hi[0].reshape(by * bz, c), grad[-face:]], axis=0)
    put_faces(par[0] == 1, out_a, out_b, low, high)


def turn_body(par, lo, hi, pg, ra, rb, out_a, out_b):
    bx, _, bz, c = lo.shape
    cx, cy, cz, _ = pg.shape
    xlo, xhi = get_faces(par[0] == 1, ra, rb)
    fine = 2 * cy * bz

    def side(face, row, coarse, crow):
        return jnp.concatenate(
            [
                xlo[row : row + bz],
                face[...].reshape(bx * bz, c),
                xhi[row : row + bz],
                xlo[fine + crow : fine + crow + cz],
                coarse.reshape(cx * cz, c),
                xhi[fine + crow : fine + crow + cz],
            ],
            axis=0,
        )

    low = side(lo, 0, pg[:, 0], 0)
    high = side(hi, fine - bz, pg[:, cy - 1], (cy - 1) * cz)
    put_faces(par[1] == 1, out_a, out_b, low, high)


def fine_body(par, field, ra, rb, ua, ub, w, bias, fpad, hidden, ds, pooled, out_a, out_b, wb, tmp):
    bx, by, bz, c = field.shape
    cx, cy, cz = bx // 2, by // 2, bz // 2
    rows = by * bz
    xlo, xhi = get_faces(par[0] == 1, ra, rb)
    ylo, yhi = get_faces(par[1] == 1, ua, ub)
    fpad[1 : bx + 1, 1 : by + 1] = field[...]
    fpad[0, 1 : by + 1] = xlo[:rows].reshape(by, bz, c)
    fpad[bx + 1, 1 : by + 1] = xhi[:rows].reshape(by, bz, c)
    fpad[:, 0] = ylo[: (bx + 2) * bz].reshape(bx + 2, bz, c)
    fpad[:, by + 1] = yhi[: (bx + 2) * bz].reshape(bx + 2, bz, c)
    for i in range(3):
        for j in range(3):
            for k in range(3):
                wb[pl.ds((3 * i + j) * c, c), pl.ds(k * c, c)] = w[i, j, k]

    def plane(x):
        taps = [fpad[x + i, j : j + by].reshape(rows, c) for i in range(3) for j in range(3)]
        part = jnp.dot(jnp.concatenate(taps, axis=1), wb[...], preferred_element_type=F32)
        pre = (
            part[:, c : 2 * c]
            + shift_rows(part[:, :c], 1, bz)
            + shift_rows(part[:, 2 * c :], -1, bz)
            + bias[...]
        )
        sig = sigmoid(pre)
        hid = (pre * sig).astype(BF16)
        hidden[x] = hid.reshape(by, bz, c)
        ds[x] = (sig * (1.0 + pre * (1.0 - sig))).reshape(by, bz, c)
        return hid.astype(F32)

    def pair(q, carry):
        both = plane(2 * q) + plane(2 * q + 1)
        both = jnp.sum(both.reshape(cy, 2, bz, c), axis=1).reshape(cy * bz, c)
        pooled[q] = (sum_cube(cy * bz, both, tmp) / 8.0).astype(BF16).reshape(cy, cz, c)
        return carry

    lax.fori_loop(0, cx, pair, 0)
    low = pooled[0:2].reshape(2 * cy * cz, c)
    high = pooled[cx - 2 : cx].reshape(2 * cy * cz, c)
    put_faces(par[0] == 1, out_a, out_b, low, high)


def turn2_body(par, pooled, ra, rb, out_a, out_b):
    cx, cy, cz, c = pooled.shape
    xlo, xhi = get_faces(par[0] == 1, ra, rb)
    xlo, xhi = xlo.reshape(2, cy, cz, c), xhi.reshape(2, cy, cz, c)

    def side(y):
        parts = [xlo[:, y : y + 2], pooled[:, y : y + 2], xhi[:, y : y + 2]]
        return jnp.concatenate([p.reshape(-1, c) for p in parts], axis=0)

    put_faces(par[1] == 1, out_a, out_b, side(0), side(cy - 2))


def reverse_bits(value, count):
    out = 0
    for _ in range(count):
        out, value = out * 2 + value % 2, value // 2
    return out


def spread(par, keep, send, n, blocks, piece):
    bits = n.bit_length() - 1
    half = n // 2
    for b in (0, 1):

        @pl.when(par == b)
        def _():
            for s in range(n):
                target = keep if s % 2 == b else send
                for t in range(blocks):
                    value = piece(s, t)
                    size = value.shape[0]
                    target[reverse_bits(s, bits) % half, pl.ds(t * size, size)] = value


def coarse_body(
    n, par, pooled, ra, rb, ua, ub, pg, fa, fb, ga, gb, w, bias, wm,
    slope, coarse, keep, send, cbias, qpad, gpad, wb, st, rhs, acc, ct,
):
    cx, cy, cz, c = pooled.shape
    c2 = wm.shape[0]
    xlo, xhi = get_faces(par[0] == 1, ra, rb)
    ylo, yhi = get_faces(par[1] == 1, ua, ub)
    qpad[2 : cx + 2, 2 : cy + 2] = pooled[...]
    qpad[0:2, 2 : cy + 2] = xlo.reshape(2, cy, cz, c)
    qpad[cx + 2 : cx + 4, 2 : cy + 2] = xhi.reshape(2, cy, cz, c)
    qpad[:, 0:2] = ylo.reshape(cx + 4, 2, cz, c)
    qpad[:, cy + 2 : cy + 4] = yhi.reshape(cx + 4, 2, cz, c)
    face = cy * cz
    glo, ghi = get_faces(par[0] == 1, fa, fb)
    hlo, hhi = get_faces(par[1] == 1, ga, gb)
    gpad[1 : cx + 1, 1 : cy + 1] = pg[...]
    gpad[0, 1 : cy + 1] = glo[-face:].reshape(cy, cz, c)
    gpad[cx + 1, 1 : cy + 1] = ghi[-face:].reshape(cy, cz, c)
    edge = (cx + 2) * cz
    gpad[:, 0] = hlo[-edge:].reshape(cx + 2, cz, c)
    gpad[:, cy + 1] = hhi[-edge:].reshape(cx + 2, cz, c)
    for i in range(3):
        for j in range(3):
            for k in range(3):
                wb[pl.ds((3 * i + j) * c, c), pl.ds(k * c2, c2)] = w[i, j, k]
    wide = cy + 2
    rows = wide * cz

    def plane(x, carry):
        taps = [qpad[x + i, j : j + wide].reshape(rows, c) for i in range(3) for j in range(3)]
        part = jnp.dot(jnp.concatenate(taps, axis=1), wb[...], preferred_element_type=F32)
        pre = (
            part[:, c2 : 2 * c2]
            + shift_rows(part[:, :c2], 1, cz)
            + shift_rows(part[:, 2 * c2 :], -1, cz)
            + bias[...]
        )
        sig = sigmoid(pre)
        back = lax.dot_general(
            gpad[x].reshape(rows, c), wm[...], (((1,), (1,)), ((), ())), preferred_element_type=F32
        )
        slope[x] = (back * (sig * (1.0 + pre * (1.0 - sig)))).astype(BF16).reshape(wide, cz, c2)

        @pl.when((x >= 1) & (x <= cx))
        def _():
            coarse[x - 1] = (pre * sig).astype(BF16).reshape(wide, cz, c2)[1 : cy + 1]

        return carry

    lax.fori_loop(0, cx + 2, plane, 0)
    cells = cx * cy * cz
    mid = slope[1 : cx + 1, 1 : cy + 1].reshape(cells, c2)
    wide_mid = mid.astype(F32)
    st[pl.ds(0, c2), :] = shift_rows(wide_mid, -1, cz).astype(BF16).T
    st[pl.ds(c2, c2), :] = mid.T
    st[pl.ds(2 * c2, c2), :] = shift_rows(wide_mid, 1, cz).astype(BF16).T
    for i in range(3):
        for j in range(3):
            rhs[:, pl.ds((3 * i + j) * c, c)] = qpad[
                1 + i : 1 + i + cx, 1 + j : 1 + j + cy
            ].reshape(cells, c)
    rhs[:, pl.ds(9 * c, c)] = jnp.ones((cells, c), BF16)
    acc[...] = jnp.dot(st[...], rhs[...], preferred_element_type=F32).astype(BF16)
    ct[...] = jnp.dot(
        coarse[...].reshape(cells, c2).T, pg[...].reshape(cells, c), preferred_element_type=F32
    ).astype(BF16)
    cbias[...] = acc[pl.ds(c2, c2), pl.ds(9 * c, c)]
    per = c2 // n

    def piece(s, t):
        if t == 27:
            return ct[pl.ds(s * per, per), :]
        k, tap = t // 9, t % 9
        return acc[pl.ds(k * c2 + s * per, per), pl.ds(tap * c, c)]

    spread(par[2], keep, send, n, 28, piece)


def back_body(n, par, slope, w, cot, ds, fpad, cbias, keep, send, up, st, rhs, acc, wt):
    bx, by, bz, c = cot.shape
    cx, cy, cz = bx // 2, by // 2, bz // 2
    c2 = slope.shape[3]
    cells = cx * cy * cz
    total = jnp.zeros((cells, 3 * c), F32)
    for i in range(3):
        for j in range(3):
            tap = slope[2 - i : 2 - i + cx, 2 - j : 2 - j + cy].reshape(cells, c2)
            total = total + lax.dot_general(
                tap,
                w[i, j].reshape(3 * c, c2),
                (((1,), (1,)), ((), ())),
                preferred_element_type=F32,
            )
    pooled = (
        total[:, c : 2 * c]
        + shift_rows(total[:, :c], -1, cz)
        + shift_rows(total[:, 2 * c :], 1, cz)
    ) * 0.125
    up[pl.ds(0, cells, stride=2), :] = pooled
    up[pl.ds(1, cells, stride=2), :] = pooled
    rows = by * bz
    for x in range(bx):
        base = up[pl.ds((x // 2) * cy * bz, cy * bz), :].reshape(cy, 1, bz, c)
        fine = cot[x].astype(F32).reshape(cy, 2, bz, c) + base
        fs = (fine.reshape(rows, c) * ds[x].reshape(rows, c)).astype(BF16)
        wide = fs.astype(F32)
        st[pl.ds(0, c), pl.ds(x * rows, rows)] = shift_rows(wide, -1, bz).astype(BF16).T
        st[pl.ds(c, c), pl.ds(x * rows, rows)] = fs.T
        st[pl.ds(2 * c, c), pl.ds(x * rows, rows)] = shift_rows(wide, 1, bz).astype(BF16).T
    voxels = bx * rows
    for t in range(0, 10, 2):
        for h in (0, 1):
            i, j = (t + h) // 3, (t + h) % 3
            if t + h == 9:
                rhs[:, pl.ds(h * c, c)] = jnp.ones((voxels, c), BF16)
            else:
                rhs[:, pl.ds(h * c, c)] = fpad[i : i + bx, j : j + by].reshape(voxels, c)
        acc[:, pl.ds(t * c, 2 * c)] = jnp.dot(
            st[...], rhs[...], preferred_element_type=F32
        ).astype(BF16)
    per, cper = c // n, c2 // n
    lane = lax.broadcasted_iota(jnp.int32, (per, c), 1)

    def piece(s, t):
        if t == 27:
            bias = acc[pl.ds(c + s * per, per), pl.ds(9 * c, c)].astype(F32)
            one = cbias[pl.ds(s * cper, per), :].astype(F32)
            two = cbias[pl.ds(s * cper + per, per), :].astype(F32)
            return jnp.where(lane == 0, bias, jnp.where(lane == 1, one, two)).astype(BF16)
        k, tap = t // 9, t % 9
        return acc[pl.ds(k * c + s * per, per), pl.ds(tap * c, c)]

    spread(par[2], keep, send, n, 28, piece)


def merge_body(par, hidden, coarse, wm, out, tmp):
    bx, by, bz, c = hidden.shape
    cx, cy, cz = bx // 2, by // 2, bz // 2
    c2 = coarse.shape[3]
    cells = cx * cy * cz
    proj = jnp.dot(coarse[...].reshape(cells, c2), wm[...], preferred_element_type=F32)
    tmp[pl.ds(0, cells, stride=2), :] = proj
    tmp[pl.ds(1, cells, stride=2), :] = proj
    for x in range(bx):
        base = tmp[pl.ds((x // 2) * cy * bz, cy * bz), :].reshape(cy, 1, bz, c)
        total = hidden[x].astype(F32).reshape(cy, 2, bz, c) + base
        out[x] = total.astype(BF16).reshape(by, bz, c)


def swap(value, axis, bit):
    n = lax.axis_size(axis)
    return lax.ppermute(value, axis, [(i, i ^ (1 << bit)) for i in range(n)])


def swap_faces(first, second, axis):
    n = lax.axis_size(axis)
    one = [p for i in range(0, n - 1, 2) for p in ((i, i + 1), (i + 1, i))]
    two = [p for i in range(1, n - 1, 2) for p in ((i, i + 1), (i + 1, i))]
    return lax.ppermute(first, axis, one), lax.ppermute(second, axis, two)


def add(a, b):
    return (a.astype(F32) + b.astype(F32)).astype(BF16)


def half_of(value, which):
    size = value.shape[0] // 2
    return lax.dynamic_slice_in_dim(value, which * size, size, 0)


def reduce_all(keep, send, sub, grp):
    got = swap(send, "sub", 0)
    for bit in range(1, lax.axis_size("sub").bit_length() - 1):
        mine = (sub >> bit) & 1
        send = add(half_of(keep, 1 - mine), half_of(got, 1 - mine))
        keep = add(half_of(keep, mine), half_of(got, mine))
        got = swap(send, "sub", bit)
    total = add(keep, got)[0]
    order = []
    for bit in range(lax.axis_size("grp").bit_length() - 1):
        mine = (grp >> bit) & 1
        if total.shape[0] % 32:
            total = add(total, swap(total, "grp", bit))
            continue
        got = swap(half_of(total, 1 - mine), "grp", bit)
        total = add(half_of(total, mine), got)
        order.append((bit, mine))
    for bit, mine in reversed(order):
        got = swap(total, "grp", bit)
        first, second = jnp.where(mine == 0, total, got), jnp.where(mine == 0, got, total)
        total = jnp.concatenate([first, second], axis=0)
    return total


def per_device(field, cotangent, fine_kernel, fine_bias, coarse_kernel, coarse_bias, merge_weight):
    grp, sub = lax.axis_index("grp"), lax.axis_index("sub")
    n = lax.axis_size("sub")
    bx, by, bz, c = field.shape
    cx, cy, cz = bx // 2, by // 2, bz // 2
    c2 = merge_weight.shape[0]
    par = jnp.stack([grp % 2, sub % 2, sub % 2]).astype(jnp.int32)
    face = by * bz + cy * cz
    pg, sa, sb = call(
        prep_body,
        "prep",
        (par, field[:1], field[bx - 1 :], cotangent),
        [((cx, cy, cz, c), BF16), ((face, c), BF16), ((face, c), BF16)],
        [pltpu.VMEM((cx * cy * bz, c), F32)],
    )
    xa, xb = swap_faces(sa, sb, "grp")
    edge = (bx + 2) * bz + (cx + 2) * cz
    ta, tb = call(
        turn_body,
        "turn",
        (par, field[:, :1], field[:, by - 1 :], pg, xa, xb),
        [((edge, c), BF16), ((edge, c), BF16)],
    )
    ya, yb = swap_faces(ta, tb, "sub")
    side = 2 * cy * cz
    fpad, hidden, ds, pooled, pa, pb = call(
        fine_body,
        "fine",
        (par, field, xa, xb, ya, yb, fine_kernel, fine_bias.reshape(1, c)),
        [
            ((bx + 2, by + 2, bz, c), BF16),
            ((bx, by, bz, c), BF16),
            ((bx, by, bz, c), F32),
            ((cx, cy, cz, c), BF16),
            ((side, c), BF16),
            ((side, c), BF16),
        ],
        [pltpu.VMEM((9 * c, 3 * c), BF16), pltpu.VMEM((cy * bz, c), F32)],
    )
    pxa, pxb = swap_faces(pa, pb, "grp")
    side = (cx + 4) * 2 * cz
    qa, qb = call(
        turn2_body,
        "turn2",
        (par, pooled, pxa, pxb),
        [((side, c), BF16), ((side, c), BF16)],
    )
    pya, pyb = swap_faces(qa, qb, "sub")
    cells = cx * cy * cz
    part = (n // 2, 28 * (c2 // n), c)
    slope, coarse, ckeep, csend, cbias = call(
        functools.partial(coarse_body, n),
        "coarse",
        (par, pooled, pxa, pxb, pya, pyb, pg, xa, xb, ya, yb, coarse_kernel, coarse_bias.reshape(1, c2), merge_weight),
        [
            ((cx + 2, cy + 2, cz, c2), BF16),
            ((cx, cy, cz, c2), BF16),
            (part, BF16),
            (part, BF16),
            ((c2, c), BF16),
        ],
        [
            pltpu.VMEM((cx + 4, cy + 4, cz, c), BF16),
            pltpu.VMEM((cx + 2, cy + 2, cz, c), BF16),
            pltpu.VMEM((9 * c, 3 * c2), BF16),
            pltpu.VMEM((3 * c2, cells), BF16),
            pltpu.VMEM((cells, 10 * c), BF16),
            pltpu.VMEM((3 * c2, 10 * c), BF16),
            pltpu.VMEM((c2, c), BF16),
        ],
    )
    coarse_sum = reduce_all(ckeep, csend, sub, grp)
    part = (n // 2, 28 * (c // n), c)
    fkeep, fsend = call(
        functools.partial(back_body, n),
        "back",
        (par, slope, coarse_kernel, cotangent, ds, fpad, cbias),
        [(part, BF16), (part, BF16)],
        [
            pltpu.VMEM((cx * cy * bz, c), F32),
            pltpu.VMEM((3 * c, bx * by * bz), BF16),
            pltpu.VMEM((bx * by * bz, 2 * c), BF16),
            pltpu.VMEM((3 * c, 10 * c), BF16),
            pltpu.VMEM((16, 128), BF16),
        ],
    )
    fine_sum = reduce_all(fkeep, fsend, sub, grp)
    (output,) = call(
        merge_body,
        "merge",
        (par, hidden, coarse, merge_weight),
        [((bx, by, bz, c), BF16)],
        [pltpu.VMEM((cx * cy * bz, c), F32)],
    )
    per, cper = c // n, c2 // n
    fine_sum = fine_sum.reshape(28, per, c)
    coarse_sum = coarse_sum.reshape(28, cper, c)

    def kernel_of(total, size):
        shaped = total[:27].reshape(3, 3, 3, size, c)
        return jnp.transpose(shaped, (1, 2, 0, 4, 3)).astype(F32)

    grad_coarse_bias = jnp.concatenate([fine_sum[27, :, 1], fine_sum[27, :, 2]]).astype(F32)
    return (
        output,
        kernel_of(fine_sum, per),
        fine_sum[27, :, 0].astype(F32),
        kernel_of(coarse_sum, cper),
        grad_coarse_bias,
        coarse_sum[27].astype(F32),
    )


def solution(mesh):
    in_specs = (P("grp", "sub", None, None), P("grp", "sub", None, None), P(), P(), P(), P(), P())
    out_specs = (
        P("grp", "sub", None, None),
        P(None, None, None, None, "sub"),
        P("sub"),
        P(None, None, None, None, "sub"),
        P("sub"),
        P("sub", None),
    )
    return jax.shard_map(
        per_device, mesh=mesh, in_specs=in_specs, out_specs=out_specs, check_vma=False
    )
```

```python
import functools

import jax
import jax.numpy as jnp
from jax import lax
from jax.experimental import pallas as pl
from jax.experimental.pallas import tpu as pltpu
from jax.sharding import PartitionSpec as P

F32 = jnp.float32
BF16 = jnp.bfloat16
VMEM_LIMIT = 48 * 1024 * 1024


def call(body, name, args, outs, scratch=(), micros=1):
    specs = [pl.BlockSpec(memory_space=pltpu.SMEM)]
    arrays = [args[0]]
    for arg in args[1:]:
        if isinstance(arg, tuple):
            arrays.append(arg[0])
            specs.append(pl.BlockSpec(arg[1], functools.partial(lambda at, _: at, arg[2])))
        else:
            arrays.append(arg)
            specs.append(pl.BlockSpec(memory_space=pltpu.VMEM))
    return pl.pallas_call(
        body,
        name=name,
        out_shape=[jax.ShapeDtypeStruct(s, t) for s, t in outs],
        grid=(1,) if any(isinstance(arg, tuple) for arg in args) else (),
        in_specs=specs,
        out_specs=[pl.BlockSpec(memory_space=pltpu.VMEM) for _ in outs],
        scratch_shapes=list(scratch),
        compiler_params=pltpu.CompilerParams(vmem_limit_bytes=VMEM_LIMIT),
        cost_estimate=pl.CostEstimate(
            flops=int(micros * 1e9), bytes_accessed=0, transcendentals=0
        ),
    )(*arrays)


def put_faces(odd, first, second, low, high):
    first[...] = jnp.where(odd, low, high)
    second[...] = jnp.where(odd, high, low)


def get_faces(odd, first, second):
    a, b = first[...], second[...]
    return jnp.where(odd, a, b), jnp.where(odd, b, a)


def sum_cube(rows, planes, ref):
    half = rows // 2
    ref[pl.ds(0, rows), :] = planes
    return ref[pl.ds(0, half, stride=2), :] + ref[pl.ds(1, half, stride=2), :]


def shift_rows(value, step, depth):
    rows = value.shape[0]
    moved = pltpu.roll(value, step % rows, 0)
    place = lax.broadcasted_iota(jnp.int32, value.shape, 0) % depth
    edge = 0 if step == 1 else depth - 1
    return jnp.where(place == edge, 0.0, moved)


def sigmoid(value):
    return 1.0 / (1.0 + jnp.exp(-value))


def prep_body(par, lo, hi, cot, pg, out_a, out_b, tmp):
    bx, by, bz, c = cot.shape
    cx, cy, cz = bx // 2, by // 2, bz // 2
    total = jnp.sum(cot[...].astype(F32).reshape(cx, 2, cy, 2, bz, c), axis=(1, 3))
    grad = sum_cube(cx * cy * bz, total.reshape(cx * cy * bz, c), tmp).astype(BF16)
    pg[...] = grad.reshape(cx, cy, cz, c)
    face = cy * cz
    low = jnp.concatenate([lo[0].reshape(by * bz, c), grad[:face]], axis=0)
    high = jnp.concatenate([hi[0].reshape(by * bz, c), grad[-face:]], axis=0)
    put_faces(par[0] == 1, out_a, out_b, low, high)


def turn_body(par, lo, hi, pg, ra, rb, out_a, out_b):
    bx, _, bz, c = lo.shape
    cx, cy, cz, _ = pg.shape
    xlo, xhi = get_faces(par[0] == 1, ra, rb)
    fine = 2 * cy * bz

    def side(face, row, coarse, crow):
        return jnp.concatenate(
            [
                xlo[row : row + bz],
                face[...].reshape(bx * bz, c),
                xhi[row : row + bz],
                xlo[fine + crow : fine + crow + cz],
                coarse.reshape(cx * cz, c),
                xhi[fine + crow : fine + crow + cz],
            ],
            axis=0,
        )

    low = side(lo, 0, pg[:, 0], 0)
    high = side(hi, fine - bz, pg[:, cy - 1], (cy - 1) * cz)
    put_faces(par[1] == 1, out_a, out_b, low, high)


def fine_body(par, field, ra, rb, ua, ub, w, bias, fpad, hidden, ds, pooled, out_a, out_b, wb, tmp):
    bx, by, bz, c = field.shape
    cx, cy, cz = bx // 2, by // 2, bz // 2
    rows = by * bz
    xlo, xhi = get_faces(par[0] == 1, ra, rb)
    ylo, yhi = get_faces(par[1] == 1, ua, ub)
    fpad[1 : bx + 1, 1 : by + 1] = field[...]
    fpad[0, 1 : by + 1] = xlo[:rows].reshape(by, bz, c)
    fpad[bx + 1, 1 : by + 1] = xhi[:rows].reshape(by, bz, c)
    fpad[:, 0] = ylo[: (bx + 2) * bz].reshape(bx + 2, bz, c)
    fpad[:, by + 1] = yhi[: (bx + 2) * bz].reshape(bx + 2, bz, c)
    for i in range(3):
        for j in range(3):
            for k in range(3):
                wb[pl.ds((3 * i + j) * c, c), pl.ds(k * c, c)] = w[i, j, k]

    def plane(x):
        taps = [fpad[x + i, j : j + by].reshape(rows, c) for i in range(3) for j in range(3)]
        part = jnp.dot(jnp.concatenate(taps, axis=1), wb[...], preferred_element_type=F32)
        pre = (
            part[:, c : 2 * c]
            + shift_rows(part[:, :c], 1, bz)
            + shift_rows(part[:, 2 * c :], -1, bz)
            + bias[...]
        )
        sig = sigmoid(pre)
        hid = (pre * sig).astype(BF16)
        hidden[x] = hid.reshape(by, bz, c)
        ds[x] = (sig * (1.0 + pre * (1.0 - sig))).reshape(by, bz, c)
        return hid.astype(F32)

    def pair(q, carry):
        both = plane(2 * q) + plane(2 * q + 1)
        both = jnp.sum(both.reshape(cy, 2, bz, c), axis=1).reshape(cy * bz, c)
        pooled[q] = (sum_cube(cy * bz, both, tmp) / 8.0).astype(BF16).reshape(cy, cz, c)
        return carry

    lax.fori_loop(0, cx, pair, 0)
    low = pooled[0:2].reshape(2 * cy * cz, c)
    high = pooled[cx - 2 : cx].reshape(2 * cy * cz, c)
    put_faces(par[0] == 1, out_a, out_b, low, high)


def turn2_body(par, pooled, ra, rb, out_a, out_b):
    cx, cy, cz, c = pooled.shape
    xlo, xhi = get_faces(par[0] == 1, ra, rb)
    xlo, xhi = xlo.reshape(2, cy, cz, c), xhi.reshape(2, cy, cz, c)

    def side(y):
        parts = [xlo[:, y : y + 2], pooled[:, y : y + 2], xhi[:, y : y + 2]]
        return jnp.concatenate([p.reshape(-1, c) for p in parts], axis=0)

    put_faces(par[1] == 1, out_a, out_b, side(0), side(cy - 2))


def reverse_bits(value, count):
    out = 0
    for _ in range(count):
        out, value = out * 2 + value % 2, value // 2
    return out


def spread(par, keep, send, n, blocks, piece):
    bits = n.bit_length() - 1
    half = n // 2
    for b in (0, 1):

        @pl.when(par == b)
        def _():
            for s in range(n):
                target = keep if s % 2 == b else send
                for t in range(blocks):
                    value = piece(s, t)
                    size = value.shape[0]
                    target[reverse_bits(s, bits) % half, pl.ds(t * size, size)] = value


def coarse_body(
    n, par, pooled, ra, rb, ua, ub, pg, fa, fb, ga, gb, w, bias, wm,
    slope, coarse, keep, send, cbias, qpad, gpad, wb, st, rhs, acc, ct,
):
    cx, cy, cz, c = pooled.shape
    c2 = wm.shape[0]
    xlo, xhi = get_faces(par[0] == 1, ra, rb)
    ylo, yhi = get_faces(par[1] == 1, ua, ub)
    qpad[2 : cx + 2, 2 : cy + 2] = pooled[...]
    qpad[0:2, 2 : cy + 2] = xlo.reshape(2, cy, cz, c)
    qpad[cx + 2 : cx + 4, 2 : cy + 2] = xhi.reshape(2, cy, cz, c)
    qpad[:, 0:2] = ylo.reshape(cx + 4, 2, cz, c)
    qpad[:, cy + 2 : cy + 4] = yhi.reshape(cx + 4, 2, cz, c)
    face = cy * cz
    glo, ghi = get_faces(par[0] == 1, fa, fb)
    hlo, hhi = get_faces(par[1] == 1, ga, gb)
    gpad[1 : cx + 1, 1 : cy + 1] = pg[...]
    gpad[0, 1 : cy + 1] = glo[-face:].reshape(cy, cz, c)
    gpad[cx + 1, 1 : cy + 1] = ghi[-face:].reshape(cy, cz, c)
    edge = (cx + 2) * cz
    gpad[:, 0] = hlo[-edge:].reshape(cx + 2, cz, c)
    gpad[:, cy + 1] = hhi[-edge:].reshape(cx + 2, cz, c)
    for i in range(3):
        for j in range(3):
            for k in range(3):
                wb[pl.ds((3 * i + j) * c, c), pl.ds(k * c2, c2)] = w[i, j, k]
    wide = cy + 2
    rows = wide * cz

    def plane(x, carry):
        taps = [qpad[x + i, j : j + wide].reshape(rows, c) for i in range(3) for j in range(3)]
        part = jnp.dot(jnp.concatenate(taps, axis=1), wb[...], preferred_element_type=F32)
        pre = (
            part[:, c2 : 2 * c2]
            + shift_rows(part[:, :c2], 1, cz)
            + shift_rows(part[:, 2 * c2 :], -1, cz)
            + bias[...]
        )
        sig = sigmoid(pre)
        back = lax.dot_general(
            gpad[x].reshape(rows, c), wm[...], (((1,), (1,)), ((), ())), preferred_element_type=F32
        )
        slope[x] = (back * (sig * (1.0 + pre * (1.0 - sig)))).astype(BF16).reshape(wide, cz, c2)

        @pl.when((x >= 1) & (x <= cx))
        def _():
            coarse[x - 1] = (pre * sig).astype(BF16).reshape(wide, cz, c2)[1 : cy + 1]

        return carry

    lax.fori_loop(0, cx + 2, plane, 0)
    cells = cx * cy * cz
    mid = slope[1 : cx + 1, 1 : cy + 1].reshape(cells, c2)
    wide_mid = mid.astype(F32)
    st[pl.ds(0, c2), :] = shift_rows(wide_mid, -1, cz).astype(BF16).T
    st[pl.ds(c2, c2), :] = mid.T
    st[pl.ds(2 * c2, c2), :] = shift_rows(wide_mid, 1, cz).astype(BF16).T
    for i in range(3):
        for j in range(3):
            rhs[:, pl.ds((3 * i + j) * c, c)] = qpad[
                1 + i : 1 + i + cx, 1 + j : 1 + j + cy
            ].reshape(cells, c)
    rhs[:, pl.ds(9 * c, c)] = jnp.ones((cells, c), BF16)
    acc[...] = jnp.dot(st[...], rhs[...], preferred_element_type=F32).astype(BF16)
    ct[...] = jnp.dot(
        coarse[...].reshape(cells, c2).T, pg[...].reshape(cells, c), preferred_element_type=F32
    ).astype(BF16)
    cbias[...] = acc[pl.ds(c2, c2), pl.ds(9 * c, c)]
    per = c2 // n

    def piece(s, t):
        if t == 27:
            return ct[pl.ds(s * per, per), :]
        k, tap = t // 9, t % 9
        return acc[pl.ds(k * c2 + s * per, per), pl.ds(tap * c, c)]

    spread(par[2], keep, send, n, 28, piece)


def slope_body(par, slope, w, cot, ds, st, up):
    bx, by, bz, c = cot.shape
    cx, cy, cz = bx // 2, by // 2, bz // 2
    c2 = slope.shape[3]
    cells = cx * cy * cz
    total = jnp.zeros((cells, 3 * c), F32)
    for i in range(3):
        for j in range(3):
            tap = slope[2 - i : 2 - i + cx, 2 - j : 2 - j + cy].reshape(cells, c2)
            total = total + lax.dot_general(
                tap,
                w[i, j].reshape(3 * c, c2),
                (((1,), (1,)), ((), ())),
                preferred_element_type=F32,
            )
    pooled = (
        total[:, c : 2 * c]
        + shift_rows(total[:, :c], -1, cz)
        + shift_rows(total[:, 2 * c :], 1, cz)
    ) * 0.125
    up[pl.ds(0, cells, stride=2), :] = pooled
    up[pl.ds(1, cells, stride=2), :] = pooled
    rows = by * bz
    for x in range(bx):
        base = up[pl.ds((x // 2) * cy * bz, cy * bz), :].reshape(cy, 1, bz, c)
        fine = cot[x].astype(F32).reshape(cy, 2, bz, c) + base
        fs = (fine.reshape(rows, c) * ds[x].reshape(rows, c)).astype(BF16)
        wide = fs.astype(F32)
        st[pl.ds(0, c), pl.ds(x * rows, rows)] = shift_rows(wide, -1, bz).astype(BF16).T
        st[pl.ds(c, c), pl.ds(x * rows, rows)] = fs.T
        st[pl.ds(2 * c, c), pl.ds(x * rows, rows)] = shift_rows(wide, 1, bz).astype(BF16).T


def grad_body(n, par, st, fpad, cbias, keep, send, rhs, acc):
    bx, by, bz, c = fpad.shape[0] - 2, fpad.shape[1] - 2, fpad.shape[2], fpad.shape[3]
    voxels = bx * by * bz
    c2 = cbias.shape[0]
    for t in range(0, 10, 2):
        for h in (0, 1):
            i, j = (t + h) // 3, (t + h) % 3
            if t + h == 9:
                rhs[:, pl.ds(h * c, c)] = jnp.ones((voxels, c), BF16)
            else:
                rhs[:, pl.ds(h * c, c)] = fpad[i : i + bx, j : j + by].reshape(voxels, c)
        acc[:, pl.ds(t * c, 2 * c)] = jnp.dot(
            st[...], rhs[...], preferred_element_type=F32
        ).astype(BF16)
    per, cper = c // n, c2 // n
    lane = lax.broadcasted_iota(jnp.int32, (per, c), 1)

    def piece(s, t):
        if t == 27:
            bias = acc[pl.ds(c + s * per, per), pl.ds(9 * c, c)].astype(F32)
            one = cbias[pl.ds(s * cper, per), :].astype(F32)
            two = cbias[pl.ds(s * cper + per, per), :].astype(F32)
            return jnp.where(lane == 0, bias, jnp.where(lane == 1, one, two)).astype(BF16)
        k, tap = t // 9, t % 9
        return acc[pl.ds(k * c + s * per, per), pl.ds(tap * c, c)]

    spread(par[2], keep, send, n, 28, piece)


def merge_body(par, hidden, coarse, wm, out, tmp):
    bx, by, bz, c = hidden.shape
    cx, cy, cz = bx // 2, by // 2, bz // 2
    c2 = coarse.shape[3]
    cells = cx * cy * cz
    proj = jnp.dot(coarse[...].reshape(cells, c2), wm[...], preferred_element_type=F32)
    tmp[pl.ds(0, cells, stride=2), :] = proj
    tmp[pl.ds(1, cells, stride=2), :] = proj
    for x in range(bx):
        base = tmp[pl.ds((x // 2) * cy * bz, cy * bz), :].reshape(cy, 1, bz, c)
        total = hidden[x].astype(F32).reshape(cy, 2, bz, c) + base
        out[x] = total.astype(BF16).reshape(by, bz, c)


def swap_faces(first, second, axis):
    n = lax.axis_size(axis)
    one = [p for i in range(0, n - 1, 2) for p in ((i, i + 1), (i + 1, i))]
    two = [p for i in range(1, n - 1, 2) for p in ((i, i + 1), (i + 1, i))]
    return lax.ppermute(first, axis, one), lax.ppermute(second, axis, two)


def split4_body(par, keep, got, own, over_sub, over_grp, over_both):
    g, s = par[0], par[1]

    def part(a, b):
        return (keep[a, :, b].astype(F32) + got[a, :, b].astype(F32)).astype(BF16)

    over_both[...] = part(1 - s, 1 - g)
    over_sub[...] = part(1 - s, g)
    over_grp[...] = part(s, 1 - g)
    own[...] = part(s, g)


def split_body(count, par, *refs):
    parts, keep, send = refs[:count], refs[count], refs[count + 1]

    def part(at):
        return sum(p[at].astype(F32) for p in parts).astype(BF16)

    send[...] = part(1 - par[0])
    keep[...] = part(par[0])


def sum_body(count, par, *refs):
    refs[count][...] = sum(p[...].astype(F32) for p in refs[:count]).astype(BF16)


def partners(value, grp_mask, sub_mask):
    n_grp, n_sub = lax.axis_size("grp"), lax.axis_size("sub")
    pairs = [
        (g * n_sub + s, (g ^ grp_mask) * n_sub + (s ^ sub_mask))
        for g in range(n_grp)
        for s in range(n_sub)
    ]
    return lax.ppermute(value, ("grp", "sub"), pairs)


def split_sum(parts, bit, name):
    rows, c = parts[0].shape
    half = ((rows // 2, c), BF16)
    shaped = [p.reshape(2, rows // 2, c) for p in parts]
    return call(
        functools.partial(split_body, len(parts)), name, (bit.reshape(1), *shaped), [half, half], (), 0.8
    )


def cores(send):
    return partners(send, 0, 1)


def spread_sum(keep, got, bits, name):
    half, rows, c = keep.shape
    rest = half // 2
    shape = (2, rest, 2, rows // 2, c)
    out = ((rest, rows // 2, c), BF16)
    own, over_sub, over_grp, over_both = call(
        split4_body, name, (bits, keep.reshape(shape), got.reshape(shape)), [out] * 4, (), 1
    )
    return own, over_sub, over_grp, over_both


def cross(own, over_sub, over_grp, over_both):
    return [own, partners(over_both, 1, 2), partners(over_sub, 0, 2), partners(over_grp, 1, 0)]


def finish_sum(parts, sub, grp, name):
    rest, rows, c = parts[0].shape
    parts = [p.reshape(rest * rows, c) for p in parts]
    for bit in range(2, lax.axis_size("sub").bit_length() - 1):
        keep, send = split_sum(parts, (sub >> bit) & 1, name + f"_sub{bit}")
        parts = [keep, partners(send, 0, 1 << bit)]
    bits = [0]
    last = lax.axis_size("grp").bit_length() - 2
    for bit in range(1, last + 1):
        mask = 1 << bit
        if bit == 1 and bit < last and parts[0].shape[0] % 32 == 0:
            keep, send = split_sum(parts, (grp >> bit) & 1, name + "_half")
            parts = [keep, partners(send, mask, 0)]
            bits.append(bit)
            continue
        out = [(parts[0].shape, BF16)]
        (total,) = call(
            functools.partial(sum_body, len(parts)), name + f"_sum{bit}", (sub.reshape(1), *parts), out, (), 0.5
        )
        parts = [total, partners(total, mask, 0)]
    (total,) = call(
        functools.partial(sum_body, len(parts)), name + "_total", (sub.reshape(1), *parts), [(parts[0].shape, BF16)], (), 0.5
    )
    pieces = [total]
    for which in range(1, 2 ** len(bits)):
        pieces.append(partners(total, sum(1 << bits[b] for b in range(len(bits)) if which >> b & 1), 0))
    return pieces, bits


def last_body(count, per, par, *refs):
    pieces, rest, rows = refs[:count], refs[count:-1], refs[-1]
    size = pieces[0].shape[0]
    mine = par[0] if count == 2 else 2 * par[0] + par[1]
    for which in range(count):
        mask = which if count == 2 else 2 * (which & 1) + (which >> 1)
        rows[mine ^ mask] = pieces[which][...]
    kernel, extra = rest[0], rest[1]

    def block(t):
        at, off = t * per // size, t * per % size
        if off + per <= size:
            return rows[at, pl.ds(off, per)]
        first = size - off
        return jnp.concatenate([rows[at, pl.ds(off, first)], rows[at + 1, pl.ds(0, per - first)]], axis=0)

    for t in range(27):
        kernel[(t // 3) % 3, t % 3, t // 9] = block(t).astype(F32).T
    extra[...] = block(27).astype(F32)


def last(pieces, bits, grp, per, name):
    count = len(pieces)
    size, c = pieces[0].shape
    order = jnp.stack([(grp >> b) & 1 for b in (bits + bits)[:2]]).astype(jnp.int32)
    return call(
        functools.partial(last_body, count, per),
        name,
        (order, *pieces),
        [((3, 3, 3, c, per), F32), ((per, c), F32)],
        [pltpu.VMEM((count, size, c), BF16)],
        2,
    )


def per_device(field, cotangent, fine_kernel, fine_bias, coarse_kernel, coarse_bias, merge_weight):
    grp, sub = lax.axis_index("grp"), lax.axis_index("sub")
    n = lax.axis_size("sub")
    bx, by, bz, c = field.shape
    cx, cy, cz = bx // 2, by // 2, bz // 2
    c2 = merge_weight.shape[0]
    par = jnp.stack([grp & 1, sub & 1, sub & 1]).astype(jnp.int32)
    cross_bits = jnp.stack([grp & 1, (sub >> 1) & 1]).astype(jnp.int32)
    face = by * bz + cy * cz
    xlo = (field, (1, by, bz, c), (0, 0, 0, 0))
    xhi = (field, (1, by, bz, c), (bx - 1, 0, 0, 0))
    ylo = (field, (bx, 1, bz, c), (0, 0, 0, 0))
    yhi = (field, (bx, 1, bz, c), (0, by - 1, 0, 0))
    pg, sa, sb = call(
        prep_body,
        "prep",
        (par, xlo, xhi, cotangent),
        [((cx, cy, cz, c), BF16), ((face, c), BF16), ((face, c), BF16)],
        [pltpu.VMEM((cx * cy * bz, c), F32)],
    )
    xa, xb = swap_faces(sa, sb, "grp")
    edge = (bx + 2) * bz + (cx + 2) * cz
    ta, tb = call(
        turn_body,
        "turn",
        (par, ylo, yhi, pg, xa, xb),
        [((edge, c), BF16), ((edge, c), BF16)],
    )
    ya, yb = swap_faces(ta, tb, "sub")
    side = 2 * cy * cz
    fpad, hidden, ds, pooled, pa, pb = call(
        fine_body,
        "fine",
        (par, field, xa, xb, ya, yb, fine_kernel, fine_bias.reshape(1, c)),
        [
            ((bx + 2, by + 2, bz, c), BF16),
            ((bx, by, bz, c), BF16),
            ((bx, by, bz, c), F32),
            ((cx, cy, cz, c), BF16),
            ((side, c), BF16),
            ((side, c), BF16),
        ],
        [pltpu.VMEM((9 * c, 3 * c), BF16), pltpu.VMEM((cy * bz, c), F32)],
        8,
    )
    pxa, pxb = swap_faces(pa, pb, "grp")
    side = (cx + 4) * 2 * cz
    qa, qb = call(
        turn2_body,
        "turn2",
        (par, pooled, pxa, pxb),
        [((side, c), BF16), ((side, c), BF16)],
    )
    pya, pyb = swap_faces(qa, qb, "sub")
    cells = cx * cy * cz
    part = (n // 2, 28 * (c2 // n), c)
    slope, coarse, ckeep, csend, cbias = call(
        functools.partial(coarse_body, n),
        "coarse",
        (par, pooled, pxa, pxb, pya, pyb, pg, xa, xb, ya, yb, coarse_kernel, coarse_bias.reshape(1, c2), merge_weight),
        [
            ((cx + 2, cy + 2, cz, c2), BF16),
            ((cx, cy, cz, c2), BF16),
            (part, BF16),
            (part, BF16),
            ((c2, c), BF16),
        ],
        [
            pltpu.VMEM((cx + 4, cy + 4, cz, c), BF16),
            pltpu.VMEM((cx + 2, cy + 2, cz, c), BF16),
            pltpu.VMEM((9 * c, 3 * c2), BF16),
            pltpu.VMEM((3 * c2, cells), BF16),
            pltpu.VMEM((cells, 10 * c), BF16),
            pltpu.VMEM((3 * c2, 10 * c), BF16),
            pltpu.VMEM((c2, c), BF16),
        ],
        6,
    )
    cgot = cores(csend)
    voxels = bx * by * bz
    (st,) = call(
        slope_body,
        "slope",
        (par, slope, coarse_kernel, cotangent, ds),
        [((3 * c, voxels), BF16)],
        [pltpu.VMEM((cx * cy * bz, c), F32)],
        4,
    )
    st, cgot = lax.optimization_barrier((st, cgot))
    csent = spread_sum(ckeep, cgot, cross_bits, "coarse_split")
    st, csent = lax.optimization_barrier((st, csent))
    cparts = cross(*csent)
    part = (n // 2, 28 * (c // n), c)
    fkeep, fsend = call(
        functools.partial(grad_body, n),
        "grad",
        (par, st, fpad, cbias),
        [(part, BF16), (part, BF16)],
        [pltpu.VMEM((voxels, 2 * c), BF16), pltpu.VMEM((3 * c, 10 * c), BF16)],
        6,
    )
    fgot = cores(fsend)
    fparts = cross(*spread_sum(fkeep, fgot, cross_bits, "fine_split"))
    coarse_sum = finish_sum(cparts, sub, grp, "coarse")
    fine_sum = finish_sum(fparts, sub, grp, "fine")
    (output,) = call(
        merge_body,
        "merge",
        (par, hidden, coarse, merge_weight),
        [((bx, by, bz, c), BF16)],
        [pltpu.VMEM((cx * cy * bz, c), F32)],
        2,
    )
    grad_coarse, grad_merge = last(*coarse_sum, grp, c2 // n, "coarse_last")
    grad_fine, extra = last(*fine_sum, grp, c // n, "fine_last")
    return (
        output,
        grad_fine,
        extra[:, 0],
        grad_coarse,
        jnp.concatenate([extra[:, 1], extra[:, 2]]),
        grad_merge,
    )


def solution(mesh):
    in_specs = (P("grp", "sub", None, None), P("grp", "sub", None, None), P(), P(), P(), P(), P())
    out_specs = (
        P("grp", "sub", None, None),
        P(None, None, None, None, "sub"),
        P("sub"),
        P(None, None, None, None, "sub"),
        P("sub"),
        P("sub", None),
    )
    return jax.shard_map(
        per_device, mesh=mesh, in_specs=in_specs, out_specs=out_specs, check_vma=False
    )
```

```python
import functools

import jax
import jax.numpy as jnp
from jax import lax
from jax.experimental import pallas as pl
from jax.experimental.pallas import tpu as pltpu
from jax.sharding import PartitionSpec as P

F32 = jnp.float32
BF16 = jnp.bfloat16
VMEM_LIMIT = 32 * 1024 * 1024


def call(body, name, args, outs, scratch=(), micros=1):
    specs = [pl.BlockSpec(memory_space=pltpu.SMEM)]
    arrays = [args[0]]
    for arg in args[1:]:
        if isinstance(arg, tuple) and arg[1] is None:
            arrays.append(arg[0])
            specs.append(pl.BlockSpec(memory_space=pltpu.HBM))
        elif isinstance(arg, tuple):
            arrays.append(arg[0])
            specs.append(pl.BlockSpec(arg[1], functools.partial(lambda at, _: at, arg[2])))
        else:
            arrays.append(arg)
            specs.append(pl.BlockSpec(memory_space=pltpu.VMEM))
    return pl.pallas_call(
        body,
        name=name,
        out_shape=[jax.ShapeDtypeStruct(s, t) for s, t in outs],
        grid=(1,) if any(isinstance(arg, tuple) and arg[1] for arg in args) else (),
        in_specs=specs,
        out_specs=[pl.BlockSpec(memory_space=pltpu.VMEM) for _ in outs],
        scratch_shapes=list(scratch),
        compiler_params=pltpu.CompilerParams(vmem_limit_bytes=VMEM_LIMIT),
        cost_estimate=pl.CostEstimate(
            flops=int(micros * 1e9), bytes_accessed=0, transcendentals=0
        ),
    )(*arrays)


def put_faces(odd, first, second, low, high):
    first[...] = jnp.where(odd, low, high)
    second[...] = jnp.where(odd, high, low)


def get_faces(odd, first, second):
    a, b = first[...], second[...]
    return jnp.where(odd, a, b), jnp.where(odd, b, a)


def sum_cube(rows, planes, ref):
    half = rows // 2
    ref[pl.ds(0, rows), :] = planes
    return ref[pl.ds(0, half, stride=2), :] + ref[pl.ds(1, half, stride=2), :]


def shift_rows(value, step, depth):
    rows = value.shape[0]
    moved = pltpu.roll(value, step % rows, 0)
    place = lax.broadcasted_iota(jnp.int32, value.shape, 0) % depth
    edge = 0 if step == 1 else depth - 1
    return jnp.where(place == edge, 0.0, moved)


def sigmoid(value):
    return 1.0 / (1.0 + jnp.exp(-value))


def prep_body(par, field, out_a, out_b, sems):
    odd, end = par[0], field.shape[0] - 1
    one = pltpu.make_async_copy(field.at[(1 - odd) * end], out_a, sems.at[0])
    two = pltpu.make_async_copy(field.at[odd * end], out_b, sems.at[1])
    one.start()
    two.start()
    one.wait()
    two.wait()


def turn_body(par, lo, hi, ra, rb, out_a, out_b):
    bx, _, bz, c = lo.shape
    xlo, xhi = get_faces(par[0] == 1, ra, rb)

    def side(face, y):
        return jnp.concatenate([xlo[y : y + 1], face[:, 0], xhi[y : y + 1]], axis=0)

    put_faces(par[1] == 1, out_a, out_b, side(lo, 0), side(hi, xlo.shape[0] - 1))


def fine_body(par, field, ra, rb, ua, ub, w, bias, pg, fpad, hidden, ds, pooled, out_a, out_b, wb, tmp):
    bx, by, bz, c = field.shape
    cx, cy, cz = bx // 2, by // 2, bz // 2
    rows = by * bz
    xlo, xhi = get_faces(par[0] == 1, ra, rb)
    ylo, yhi = get_faces(par[1] == 1, ua, ub)
    fpad[1 : bx + 1, 1 : by + 1] = field[...]
    fpad[0, 1 : by + 1] = xlo
    fpad[bx + 1, 1 : by + 1] = xhi
    fpad[:, 0] = ylo
    fpad[:, by + 1] = yhi
    for i in range(3):
        for j in range(3):
            for k in range(3):
                wb[pl.ds((3 * i + j) * c, c), pl.ds(k * c, c)] = w[i, j, k]

    def plane(x):
        taps = [fpad[x + i, j : j + by].reshape(rows, c) for i in range(3) for j in range(3)]
        part = jnp.dot(jnp.concatenate(taps, axis=1), wb[...], preferred_element_type=F32)
        pre = (
            part[:, c : 2 * c]
            + shift_rows(part[:, :c], 1, bz)
            + shift_rows(part[:, 2 * c :], -1, bz)
            + bias[...]
        )
        sig = sigmoid(pre)
        hid = (pre * sig).astype(BF16)
        hidden[x] = hid.reshape(by, bz, c)
        ds[x] = (sig * (1.0 + pre * (1.0 - sig))).reshape(by, bz, c)
        return hid.astype(F32)

    def pair(q, carry):
        both = plane(2 * q) + plane(2 * q + 1)
        both = jnp.sum(both.reshape(cy, 2, bz, c), axis=1).reshape(cy * bz, c)
        pooled[q] = (sum_cube(cy * bz, both, tmp) / 8.0).astype(BF16).reshape(cy, cz, c)
        return carry

    lax.fori_loop(0, cx, pair, 0)
    low = jnp.concatenate([pooled[0:2], pg[0:1]], axis=0)
    high = jnp.concatenate([pooled[cx - 2 : cx], pg[cx - 1 : cx]], axis=0)
    put_faces(par[0] == 1, out_a, out_b, low, high)


def cubes_body(par, cot, pg, tmp):
    bx, by, bz, c = cot.shape
    cx, cy, cz = bx // 2, by // 2, bz // 2
    total = jnp.sum(cot[...].astype(F32).reshape(cx, 2, cy, 2, bz, c), axis=(1, 3))
    grad = sum_cube(cx * cy * bz, total.reshape(cx * cy * bz, c), tmp).astype(BF16)
    pg[...] = grad.reshape(cx, cy, cz, c)


def turn2_body(par, pooled, pg, ra, rb, out_a, out_b):
    cy = pooled.shape[1]
    xlo, xhi = get_faces(par[0] == 1, ra, rb)

    def side(y, last):
        two = [jnp.concatenate([xlo[0:2, at], pooled[:, at], xhi[0:2, at]], axis=0) for at in (y, y + 1)]
        one = jnp.concatenate([xlo[2:3, last], pg[:, last], xhi[2:3, last]], axis=0)
        return jnp.concatenate([*two, one], axis=0)

    put_faces(par[1] == 1, out_a, out_b, side(0, 0), side(cy - 2, cy - 1))


def reverse_bits(value, count):
    out = 0
    for _ in range(count):
        out, value = out * 2 + value % 2, value // 2
    return out


def spread(par, keep, send, n, blocks, piece):
    bits = n.bit_length() - 1
    half = n // 2
    for b in (0, 1):

        @pl.when(par == b)
        def _():
            for s in range(n):
                target = keep if s % 2 == b else send
                for t in range(blocks):
                    value = piece(s, t)
                    size = value.shape[0]
                    target[reverse_bits(s, bits) % half, pl.ds(t * size, size)] = value


def coarse_body(
    n, par, pooled, ra, rb, ua, ub, pg, w, bias, wm,
    slope, coarse, keep, send, cbias, qpad, gpad, wb, st, rhs, acc, ct,
):
    cx, cy, cz, c = pooled.shape
    c2 = wm.shape[0]
    xlo, xhi = get_faces(par[0] == 1, ra, rb)
    ylo, yhi = get_faces(par[1] == 1, ua, ub)
    qpad[2 : cx + 2, 2 : cy + 2] = pooled[...]
    qpad[0:2, 2 : cy + 2] = xlo[0:2]
    qpad[cx + 2 : cx + 4, 2 : cy + 2] = xhi[0:2]
    wide = cx + 4
    for t in (0, 1):
        qpad[:, t] = ylo[t * wide : (t + 1) * wide]
        qpad[:, cy + 2 + t] = yhi[t * wide : (t + 1) * wide]
    gpad[1 : cx + 1, 1 : cy + 1] = pg[...]
    gpad[0, 1 : cy + 1] = xlo[2]
    gpad[cx + 1, 1 : cy + 1] = xhi[2]
    gpad[:, 0] = ylo[2 * wide :]
    gpad[:, cy + 1] = yhi[2 * wide :]
    for i in range(3):
        for j in range(3):
            for k in range(3):
                wb[pl.ds((3 * i + j) * c, c), pl.ds(k * c2, c2)] = w[i, j, k]
    wide = cy + 2
    rows = wide * cz

    def plane(x, carry):
        taps = [qpad[x + i, j : j + wide].reshape(rows, c) for i in range(3) for j in range(3)]
        part = jnp.dot(jnp.concatenate(taps, axis=1), wb[...], preferred_element_type=F32)
        pre = (
            part[:, c2 : 2 * c2]
            + shift_rows(part[:, :c2], 1, cz)
            + shift_rows(part[:, 2 * c2 :], -1, cz)
            + bias[...]
        )
        sig = sigmoid(pre)
        back = lax.dot_general(
            gpad[x].reshape(rows, c), wm[...], (((1,), (1,)), ((), ())), preferred_element_type=F32
        )
        slope[x] = (back * (sig * (1.0 + pre * (1.0 - sig)))).astype(BF16).reshape(wide, cz, c2)

        @pl.when((x >= 1) & (x <= cx))
        def _():
            coarse[x - 1] = (pre * sig).astype(BF16).reshape(wide, cz, c2)[1 : cy + 1]

        return carry

    lax.fori_loop(0, cx + 2, plane, 0)
    cells = cx * cy * cz
    mid = slope[1 : cx + 1, 1 : cy + 1].reshape(cells, c2)
    wide_mid = mid.astype(F32)
    st[pl.ds(0, c2), :] = shift_rows(wide_mid, -1, cz).astype(BF16).T
    st[pl.ds(c2, c2), :] = mid.T
    st[pl.ds(2 * c2, c2), :] = shift_rows(wide_mid, 1, cz).astype(BF16).T
    for i in range(3):
        for j in range(3):
            rhs[:, pl.ds((3 * i + j) * c, c)] = qpad[
                1 + i : 1 + i + cx, 1 + j : 1 + j + cy
            ].reshape(cells, c)
    rhs[:, pl.ds(9 * c, c)] = jnp.ones((cells, c), BF16)
    acc[...] = jnp.dot(st[...], rhs[...], preferred_element_type=F32).astype(BF16)
    ct[...] = jnp.dot(
        coarse[...].reshape(cells, c2).T, pg[...].reshape(cells, c), preferred_element_type=F32
    ).astype(BF16)
    cbias[...] = acc[pl.ds(c2, c2), pl.ds(9 * c, c)]
    per = c2 // n

    def piece(s, t):
        if t == 27:
            return ct[pl.ds(s * per, per), :]
        k, tap = t // 9, t % 9
        return acc[pl.ds(k * c2 + s * per, per), pl.ds(tap * c, c)]

    spread(par[2], keep, send, n, 28, piece)


def back_body(n, par, slope, w, cot, ds, fpad, cbias, keep, send, up, st, rhs, acc):
    bx, by, bz, c = cot.shape
    cx, cy, cz = bx // 2, by // 2, bz // 2
    c2 = slope.shape[3]
    cells = cx * cy * cz
    total = jnp.zeros((cells, 3 * c), F32)
    for i in range(3):
        for j in range(3):
            tap = slope[2 - i : 2 - i + cx, 2 - j : 2 - j + cy].reshape(cells, c2)
            total = total + lax.dot_general(
                tap,
                w[i, j].reshape(3 * c, c2),
                (((1,), (1,)), ((), ())),
                preferred_element_type=F32,
            )
    pooled = (
        total[:, c : 2 * c]
        + shift_rows(total[:, :c], -1, cz)
        + shift_rows(total[:, 2 * c :], 1, cz)
    ) * 0.125
    up[pl.ds(0, cells, stride=2), :] = pooled
    up[pl.ds(1, cells, stride=2), :] = pooled
    rows = by * bz
    for x in range(bx):
        base = up[pl.ds((x // 2) * cy * bz, cy * bz), :].reshape(cy, 1, bz, c)
        fine = cot[x].astype(F32).reshape(cy, 2, bz, c) + base
        fs = (fine.reshape(rows, c) * ds[x].reshape(rows, c)).astype(BF16)
        wide = fs.astype(F32)
        st[pl.ds(0, c), pl.ds(x * rows, rows)] = shift_rows(wide, -1, bz).astype(BF16).T
        st[pl.ds(c, c), pl.ds(x * rows, rows)] = fs.T
        st[pl.ds(2 * c, c), pl.ds(x * rows, rows)] = shift_rows(wide, 1, bz).astype(BF16).T
    voxels = bx * rows
    for t in range(0, 10, 2):
        for h in (0, 1):
            i, j = (t + h) // 3, (t + h) % 3
            if t + h == 9:
                rhs[:, pl.ds(h * c, c)] = jnp.ones((voxels, c), BF16)
            else:
                rhs[:, pl.ds(h * c, c)] = fpad[i : i + bx, j : j + by].reshape(voxels, c)
        acc[:, pl.ds(t * c, 2 * c)] = jnp.dot(
            st[...], rhs[...], preferred_element_type=F32
        ).astype(BF16)
    per, cper = c // n, c2 // n
    lane = lax.broadcasted_iota(jnp.int32, (per, c), 1)

    def piece(s, t):
        if t == 27:
            bias = acc[pl.ds(c + s * per, per), pl.ds(9 * c, c)].astype(F32)
            one = cbias[pl.ds(s * cper, per), :].astype(F32)
            two = cbias[pl.ds(s * cper + per, per), :].astype(F32)
            return jnp.where(lane == 0, bias, jnp.where(lane == 1, one, two)).astype(BF16)
        k, tap = t // 9, t % 9
        return acc[pl.ds(k * c + s * per, per), pl.ds(tap * c, c)]

    spread(par[2], keep, send, n, 28, piece)


def merge_body(par, hidden, coarse, wm, out, tmp):
    bx, by, bz, c = hidden.shape
    cx, cy, cz = bx // 2, by // 2, bz // 2
    c2 = coarse.shape[3]
    cells = cx * cy * cz
    proj = jnp.dot(coarse[...].reshape(cells, c2), wm[...], preferred_element_type=F32)
    tmp[pl.ds(0, cells, stride=2), :] = proj
    tmp[pl.ds(1, cells, stride=2), :] = proj
    for x in range(bx):
        base = tmp[pl.ds((x // 2) * cy * bz, cy * bz), :].reshape(cy, 1, bz, c)
        total = hidden[x].astype(F32).reshape(cy, 2, bz, c) + base
        out[x] = total.astype(BF16).reshape(by, bz, c)


def swap_faces(first, second, axis):
    n = lax.axis_size(axis)
    one = [p for i in range(0, n - 1, 2) for p in ((i, i + 1), (i + 1, i))]
    two = [p for i in range(1, n - 1, 2) for p in ((i, i + 1), (i + 1, i))]
    got = lax.ppermute(second, axis, two)
    return lax.ppermute(first, axis, one), got


def split4_body(par, keep, got, own, over_sub, over_grp, over_both):
    g, s = par[0], par[1]

    def part(a, b):
        return (keep[a, :, b].astype(F32) + got[a, :, b].astype(F32)).astype(BF16)

    over_both[...] = part(1 - s, 1 - g)
    over_sub[...] = part(1 - s, g)
    over_grp[...] = part(s, 1 - g)
    own[...] = part(s, g)


def split_body(count, par, *refs):
    parts, keep, send = refs[:count], refs[count], refs[count + 1]

    def part(at):
        return sum(p[at].astype(F32) for p in parts).astype(BF16)

    send[...] = part(1 - par[0])
    keep[...] = part(par[0])


def sum_body(count, par, *refs):
    refs[count][...] = sum(p[...].astype(F32) for p in refs[:count]).astype(BF16)


def partners(value, grp_mask, sub_mask):
    n_grp, n_sub = lax.axis_size("grp"), lax.axis_size("sub")
    pairs = [
        (g * n_sub + s, (g ^ grp_mask) * n_sub + (s ^ sub_mask))
        for g in range(n_grp)
        for s in range(n_sub)
    ]
    return lax.ppermute(value, ("grp", "sub"), pairs)


def split_sum(parts, bit, name):
    rows, c = parts[0].shape
    half = ((rows // 2, c), BF16)
    shaped = [p.reshape(2, rows // 2, c) for p in parts]
    return call(
        functools.partial(split_body, len(parts)), name, (bit.reshape(1), *shaped), [half, half], (), 0.8
    )


def cores(send):
    return partners(send, 0, 1)


def spread_sum(keep, got, bits, name):
    half, rows, c = keep.shape
    rest = half // 2
    shape = (2, rest, 2, rows // 2, c)
    out = ((rest, rows // 2, c), BF16)
    own, over_sub, over_grp, over_both = call(
        split4_body, name, (bits, keep.reshape(shape), got.reshape(shape)), [out] * 4, (), 1
    )
    return own, over_sub, over_grp, over_both


def cross(own, over_sub, over_grp, over_both):
    return [own, partners(over_both, 1, 2), partners(over_sub, 0, 2), partners(over_grp, 1, 0)]


def finish_sum(parts, sub, grp, name):
    rest, rows, c = parts[0].shape
    parts = [p.reshape(rest * rows, c) for p in parts]
    for bit in range(2, lax.axis_size("sub").bit_length() - 1):
        keep, send = split_sum(parts, (sub >> bit) & 1, name + f"_sub{bit}")
        parts = [keep, partners(send, 0, 1 << bit)]
    bits = [0]
    last = lax.axis_size("grp").bit_length() - 2
    for bit in range(1, last + 1):
        mask = 1 << bit
        if bit == 1 and bit < last and parts[0].shape[0] % 32 == 0:
            keep, send = split_sum(parts, (grp >> bit) & 1, name + "_half")
            parts = [keep, partners(send, mask, 0)]
            bits.append(bit)
            continue
        out = [(parts[0].shape, BF16)]
        (total,) = call(
            functools.partial(sum_body, len(parts)), name + f"_sum{bit}", (sub.reshape(1), *parts), out, (), 0.5
        )
        parts = [total, partners(total, mask, 0)]
    (total,) = call(
        functools.partial(sum_body, len(parts)), name + "_total", (sub.reshape(1), *parts), [(parts[0].shape, BF16)], (), 0.5
    )
    pieces = [total]
    for which in range(1, 2 ** len(bits)):
        pieces.append(partners(total, sum(1 << bits[b] for b in range(len(bits)) if which >> b & 1), 0))
    return pieces, bits


def last_body(count, par, *refs):
    pieces, kernel, extra, rows = refs[:count], refs[count], refs[count + 1], refs[-1]
    size = pieces[0].shape[0]
    per = extra.shape[0] if len(refs) == count + 3 else kernel.shape[3]
    mine = par[0] if count == 2 else 2 * par[0] + par[1]
    for which in range(count):
        mask = which if count == 2 else 2 * (which & 1) + (which >> 1)
        rows[mine ^ mask] = pieces[which][...]

    def block(t):
        at, off = t * per // size, t * per % size
        if off + per <= size:
            return rows[at, pl.ds(off, per)].astype(F32)
        first = size - off
        return jnp.concatenate([rows[at, pl.ds(off, first)], rows[at + 1, pl.ds(0, per - first)]], axis=0).astype(F32)

    for t in range(27):
        kernel[(t // 3) % 3, t % 3, t // 9] = block(t)
    if len(refs) == count + 3:
        extra[...] = block(27)
    else:
        turned = block(27).T
        extra[...] = turned[0:1]
        refs[count + 2][:, pl.ds(0, per)] = turned[1:2]
        refs[count + 2][:, pl.ds(per, per)] = turned[2:3]


def last(pieces, bits, grp, per, outs, name):
    count = len(pieces)
    size, c = pieces[0].shape
    order = jnp.stack([(grp >> b) & 1 for b in (bits + bits)[:2]]).astype(jnp.int32)
    kernel, *rest = call(
        functools.partial(last_body, count),
        name,
        (order, *pieces),
        [((3, 3, 3, per, c), F32), *outs],
        [pltpu.VMEM((count, size, c), BF16)],
        1,
    )
    return jnp.swapaxes(kernel, 3, 4), *rest


def per_device(field, cotangent, fine_kernel, fine_bias, coarse_kernel, coarse_bias, merge_weight):
    grp, sub = lax.axis_index("grp"), lax.axis_index("sub")
    n = lax.axis_size("sub")
    bx, by, bz, c = field.shape
    cx, cy, cz = bx // 2, by // 2, bz // 2
    c2 = merge_weight.shape[0]
    par = jnp.stack([grp & 1, sub & 1, sub & 1]).astype(jnp.int32)
    cross_bits = jnp.stack([grp & 1, (sub >> 1) & 1]).astype(jnp.int32)
    ylo = (field, (bx, 1, bz, c), (0, 0, 0, 0))
    yhi = (field, (bx, 1, bz, c), (0, by - 1, 0, 0))
    face = ((by, bz, c), BF16)
    sa, sb = call(
        prep_body, "prep", (par, (field, None, None)), [face, face], [pltpu.SemaphoreType.DMA((2,))]
    )
    xa, xb = swap_faces(sa, sb, "grp")
    (pg,) = call(
        cubes_body, "cubes", (par, cotangent), [((cx, cy, cz, c), BF16)], [pltpu.VMEM((cx * cy * bz, c), F32)]
    )
    face = ((bx + 2, bz, c), BF16)
    ta, tb = call(turn_body, "turn", (par, ylo, yhi, xa, xb), [face, face])
    ya, yb = swap_faces(ta, tb, "sub")
    face = ((3, cy, cz, c), BF16)
    fpad, hidden, ds, pooled, pa, pb = call(
        fine_body,
        "fine",
        (par, field, xa, xb, ya, yb, fine_kernel, fine_bias.reshape(1, c), pg),
        [
            ((bx + 2, by + 2, bz, c), BF16),
            ((bx, by, bz, c), BF16),
            ((bx, by, bz, c), F32),
            ((cx, cy, cz, c), BF16),
            face,
            face,
        ],
        [pltpu.VMEM((9 * c, 3 * c), BF16), pltpu.VMEM((cy * bz, c), F32)],
        8,
    )
    pxa, pxb = swap_faces(pa, pb, "grp")
    face = ((2 * (cx + 4) + cx + 2, cz, c), BF16)
    qa, qb = call(turn2_body, "turn2", (par, pooled, pg, pxa, pxb), [face, face])
    pya, pyb = swap_faces(qa, qb, "sub")
    cells = cx * cy * cz
    part = (n // 2, 28 * (c2 // n), c)
    slope, coarse, ckeep, csend, cbias = call(
        functools.partial(coarse_body, n),
        "coarse",
        (par, pooled, pxa, pxb, pya, pyb, pg, coarse_kernel, coarse_bias.reshape(1, c2), merge_weight),
        [
            ((cx + 2, cy + 2, cz, c2), BF16),
            ((cx, cy, cz, c2), BF16),
            (part, BF16),
            (part, BF16),
            ((c2, c), BF16),
        ],
        [
            pltpu.VMEM((cx + 4, cy + 4, cz, c), BF16),
            pltpu.VMEM((cx + 2, cy + 2, cz, c), BF16),
            pltpu.VMEM((9 * c, 3 * c2), BF16),
            pltpu.VMEM((3 * c2, cells), BF16),
            pltpu.VMEM((cells, 10 * c), BF16),
            pltpu.VMEM((3 * c2, 10 * c), BF16),
            pltpu.VMEM((c2, c), BF16),
        ],
        6,
    )
    cgot = cores(csend)
    (output,) = call(
        merge_body,
        "merge",
        (par, hidden, coarse, merge_weight),
        [((bx, by, bz, c), BF16)],
        [pltpu.VMEM((cx * cy * bz, c), F32)],
        2,
    )
    output, cgot = lax.optimization_barrier((output, cgot))
    csent = spread_sum(ckeep, cgot, cross_bits, "coarse_split")
    slope, csent = lax.optimization_barrier((slope, csent))
    cparts = cross(*csent)
    voxels = bx * by * bz
    part = (n // 2, 28 * (c // n), c)
    fkeep, fsend = call(
        functools.partial(back_body, n),
        "back",
        (par, slope, coarse_kernel, cotangent, ds, fpad, cbias),
        [(part, BF16), (part, BF16)],
        [
            pltpu.VMEM((cx * cy * bz, c), F32),
            pltpu.VMEM((3 * c, voxels), BF16),
            pltpu.VMEM((voxels, 2 * c), BF16),
            pltpu.VMEM((3 * c, 10 * c), BF16),
        ],
        10,
    )
    fsend, cparts = lax.optimization_barrier((fsend, cparts))
    fgot = cores(fsend)
    fparts = cross(*spread_sum(fkeep, fgot, cross_bits, "fine_split"))
    coarse_sum = finish_sum(cparts, sub, grp, "coarse")
    fine_sum = finish_sum(fparts, sub, grp, "fine")
    per, cper = c // n, c2 // n
    grad_coarse, grad_merge = last(*coarse_sum, grp, cper, [((cper, c), F32)], "coarse_last")
    biases = [((1, per), F32), ((1, cper), F32)]
    grad_fine, bias, coarse_sums = last(*fine_sum, grp, per, biases, "fine_last")
    return (output, grad_fine, bias[0], grad_coarse, coarse_sums[0], grad_merge)


def solution(mesh):
    in_specs = (P("grp", "sub", None, None), P("grp", "sub", None, None), P(), P(), P(), P(), P())
    out_specs = (
        P("grp", "sub", None, None),
        P(None, None, None, None, "sub"),
        P("sub"),
        P(None, None, None, None, "sub"),
        P("sub"),
        P("sub", None),
    )
    return jax.shard_map(
        per_device, mesh=mesh, in_specs=in_specs, out_specs=out_specs, check_vma=False
    )
```

```python
import functools

import jax
import jax.numpy as jnp
from jax import lax
from jax.experimental import pallas as pl
from jax.experimental.pallas import tpu as pltpu
from jax.sharding import PartitionSpec as P

F32 = jnp.float32
BF16 = jnp.bfloat16
VMEM_LIMIT = 32 * 1024 * 1024


def call(body, name, args, outs, scratch=(), micros=1, limit=VMEM_LIMIT):
    specs = [pl.BlockSpec(memory_space=pltpu.SMEM)]
    arrays = [args[0]]
    for arg in args[1:]:
        if isinstance(arg, tuple) and arg[1] is None:
            arrays.append(arg[0])
            specs.append(pl.BlockSpec(memory_space=pltpu.HBM))
        elif isinstance(arg, tuple):
            arrays.append(arg[0])
            specs.append(pl.BlockSpec(arg[1], functools.partial(lambda at, _: at, arg[2])))
        else:
            arrays.append(arg)
            specs.append(pl.BlockSpec(memory_space=pltpu.VMEM))
    return pl.pallas_call(
        body,
        name=name,
        out_shape=[jax.ShapeDtypeStruct(s, t) for s, t in outs],
        grid=(1,) if any(isinstance(arg, tuple) and arg[1] for arg in args) else (),
        in_specs=specs,
        out_specs=[pl.BlockSpec(memory_space=pltpu.VMEM) for _ in outs],
        scratch_shapes=list(scratch),
        compiler_params=pltpu.CompilerParams(vmem_limit_bytes=limit),
        cost_estimate=pl.CostEstimate(
            flops=int(micros * 1e9), bytes_accessed=0, transcendentals=0
        ),
    )(*arrays)


def put_faces(odd, first, second, low, high):
    first[...] = jnp.where(odd, low, high)
    second[...] = jnp.where(odd, high, low)


def get_faces(odd, first, second):
    a, b = first[...], second[...]
    return jnp.where(odd, a, b), jnp.where(odd, b, a)


def sum_cube(rows, planes, ref):
    half = rows // 2
    ref[pl.ds(0, rows), :] = planes
    return ref[pl.ds(0, half, stride=2), :] + ref[pl.ds(1, half, stride=2), :]


def shift_rows(value, step, depth):
    rows = value.shape[0]
    moved = pltpu.roll(value, step % rows, 0)
    place = lax.broadcasted_iota(jnp.int32, value.shape, 0) % depth
    edge = 0 if step == 1 else depth - 1
    return jnp.where(place == edge, 0.0, moved)


def sigmoid(value):
    return 1.0 / (1.0 + jnp.exp(-value))


def prep_body(sub, par, field, out_a, out_b, sems):
    odd, end = par[sub], field.shape[1] - 1
    one = pltpu.make_async_copy(field.at[:, (1 - odd) * end], out_a, sems.at[0])
    two = pltpu.make_async_copy(field.at[:, odd * end], out_b, sems.at[1])
    one.start()
    two.start()
    one.wait()
    two.wait()


def turn_body(sub, par, field, ya, yb, own, out_a, out_b):
    bx, by = field.shape[0], field.shape[1]
    ylo, yhi = get_faces(par[sub] == 1, ya, yb)
    own[:, 1 : by + 1] = field[...]
    own[:, 0] = ylo
    own[:, by + 1] = yhi
    put_faces(par[0] == 1, out_a, out_b, own[0], own[bx - 1])


def fine_plane(three, wb, bias, by):
    _, bz, c = three[0].shape
    rows = by * bz
    taps = [plane[j : j + by].reshape(rows, c) for plane in three for j in range(3)]
    part = jnp.dot(jnp.concatenate(taps, axis=1), wb[...], preferred_element_type=F32)
    pre = (
        part[:, c : 2 * c]
        + shift_rows(part[:, :c], 1, bz)
        + shift_rows(part[:, 2 * c :], -1, bz)
        + bias[...]
    )
    sig = sigmoid(pre)
    hid = (pre * sig).astype(BF16).reshape(by, bz, c)
    return hid, (sig * (1.0 + pre * (1.0 - sig))).reshape(by, bz, c)


def pool(one, two, tmp):
    by, bz, c = one.shape
    cy = by // 2
    both = jnp.sum((one.astype(F32) + two.astype(F32)).reshape(cy, 2, bz, c), axis=1)
    total = sum_cube(cy * bz, both.reshape(cy * bz, c), tmp)
    return (total / 8.0).astype(BF16).reshape(cy, bz // 2, c)


def inner_body(par, own, w, bias, hidden, ds, pooled, wb, tmp):
    by, c = own.shape[1] - 2, own.shape[3]
    for i in range(3):
        for j in range(3):
            for k in range(3):
                wb[pl.ds((3 * i + j) * c, c), pl.ds(k * c, c)] = w[i, j, k]

    def plane(x, carry):
        hid, slope = fine_plane([own[x], own[x + 1], own[x + 2]], wb, bias, by)
        hidden[x], ds[x] = hid, slope
        return carry

    lax.fori_loop(0, hidden.shape[0], plane, 0)
    for q in range(pooled.shape[0]):
        pooled[q] = pool(hidden[2 * q + 1], hidden[2 * q + 2], tmp)


def outer_body(par, own, ra, rb, wb, bias, hid_in, pool_in, pg, hidden, ds, halo, pooled, out_a, out_b, tmp):
    bx, by = own.shape[0], own.shape[1] - 2
    cx = bx // 2
    xlo, xhi = get_faces(par[0] == 1, ra, rb)
    halo[0], halo[1] = xlo, xhi
    for at, three in ((0, [halo[0], own[0], own[1]]), (1, [own[bx - 2], own[bx - 1], halo[1]])):
        hidden[at], ds[at] = fine_plane(three, wb, bias, by)
    pooled[0] = pool(hidden[0], hid_in[0], tmp)
    pooled[1 : cx - 1] = pool_in[...]
    pooled[cx - 1] = pool(hid_in[bx - 3], hidden[1], tmp)
    low = jnp.concatenate([pooled[0:2], pg[0:1]], axis=0)
    high = jnp.concatenate([pooled[cx - 2 : cx], pg[cx - 1 : cx]], axis=0)
    put_faces(par[0] == 1, out_a, out_b, low, high)


def cubes_body(par, cot, pg, tmp):
    bx, by, bz, c = cot.shape
    cx, cy, cz = bx // 2, by // 2, bz // 2
    total = jnp.sum(cot[...].astype(F32).reshape(cx, 2, cy, 2, bz, c), axis=(1, 3))
    grad = sum_cube(cx * cy * bz, total.reshape(cx * cy * bz, c), tmp).astype(BF16)
    pg[...] = grad.reshape(cx, cy, cz, c)


def turn2_body(sub, par, pooled, pg, ra, rb, out_a, out_b):
    cy = pooled.shape[1]
    xlo, xhi = get_faces(par[0] == 1, ra, rb)

    def side(y, last):
        two = [jnp.concatenate([xlo[0:2, at], pooled[:, at], xhi[0:2, at]], axis=0) for at in (y, y + 1)]
        one = jnp.concatenate([xlo[2:3, last], pg[:, last], xhi[2:3, last]], axis=0)
        return jnp.concatenate([*two, one], axis=0)

    put_faces(par[sub] == 1, out_a, out_b, side(0, 0), side(cy - 2, cy - 1))


def reverse_bits(value, count):
    out = 0
    for _ in range(count):
        out, value = out * 2 + value % 2, value // 2
    return out


def spread(par, keep, send, n, blocks, piece):
    bits = n.bit_length() - 1
    half = n // 2
    for b in (0, 1):

        @pl.when(par == b)
        def _():
            for s in range(n):
                target = keep if s % 2 == b else send
                for t in range(blocks):
                    value = piece(s, t)
                    size = value.shape[0]
                    target[reverse_bits(s, bits) % half, pl.ds(t * size, size)] = value


def coarse_body(
    n, sub, par, pooled, ra, rb, ua, ub, pg, w, bias, wm,
    slope, coarse, keep, send, cbias, qpad, gpad, wb, st, rhs, acc, ct,
):
    cx, cy, cz, c = pooled.shape
    c2 = wm.shape[0]
    xlo, xhi = get_faces(par[0] == 1, ra, rb)
    ylo, yhi = get_faces(par[sub] == 1, ua, ub)
    qpad[2 : cx + 2, 2 : cy + 2] = pooled[...]
    qpad[0:2, 2 : cy + 2] = xlo[0:2]
    qpad[cx + 2 : cx + 4, 2 : cy + 2] = xhi[0:2]
    wide = cx + 4
    for t in (0, 1):
        qpad[:, t] = ylo[t * wide : (t + 1) * wide]
        qpad[:, cy + 2 + t] = yhi[t * wide : (t + 1) * wide]
    gpad[1 : cx + 1, 1 : cy + 1] = pg[...]
    gpad[0, 1 : cy + 1] = xlo[2]
    gpad[cx + 1, 1 : cy + 1] = xhi[2]
    gpad[:, 0] = ylo[2 * wide :]
    gpad[:, cy + 1] = yhi[2 * wide :]
    for i in range(3):
        for j in range(3):
            for k in range(3):
                wb[pl.ds((3 * i + j) * c, c), pl.ds(k * c2, c2)] = w[i, j, k]
    wide = cy + 2
    rows = wide * cz

    def plane(x, carry):
        taps = [qpad[x + i, j : j + wide].reshape(rows, c) for i in range(3) for j in range(3)]
        part = jnp.dot(jnp.concatenate(taps, axis=1), wb[...], preferred_element_type=F32)
        pre = (
            part[:, c2 : 2 * c2]
            + shift_rows(part[:, :c2], 1, cz)
            + shift_rows(part[:, 2 * c2 :], -1, cz)
            + bias[...]
        )
        sig = sigmoid(pre)
        back = lax.dot_general(
            gpad[x].reshape(rows, c), wm[...], (((1,), (1,)), ((), ())), preferred_element_type=F32
        )
        slope[x] = (back * (sig * (1.0 + pre * (1.0 - sig)))).astype(BF16).reshape(wide, cz, c2)

        @pl.when((x >= 1) & (x <= cx))
        def _():
            coarse[x - 1] = (pre * sig).astype(BF16).reshape(wide, cz, c2)[1 : cy + 1]

        return carry

    lax.fori_loop(0, cx + 2, plane, 0)
    cells = cx * cy * cz
    mid = slope[1 : cx + 1, 1 : cy + 1].reshape(cells, c2)
    wide_mid = mid.astype(F32)
    st[pl.ds(0, c2), :] = shift_rows(wide_mid, -1, cz).astype(BF16).T
    st[pl.ds(c2, c2), :] = mid.T
    st[pl.ds(2 * c2, c2), :] = shift_rows(wide_mid, 1, cz).astype(BF16).T
    for i in range(3):
        for j in range(3):
            rhs[:, pl.ds((3 * i + j) * c, c)] = qpad[
                1 + i : 1 + i + cx, 1 + j : 1 + j + cy
            ].reshape(cells, c)
    rhs[:, pl.ds(9 * c, c)] = jnp.ones((cells, c), BF16)
    acc[...] = jnp.dot(st[...], rhs[...], preferred_element_type=F32).astype(BF16)
    ct[...] = jnp.dot(
        coarse[...].reshape(cells, c2).T, pg[...].reshape(cells, c), preferred_element_type=F32
    ).astype(BF16)
    cbias[...] = acc[pl.ds(c2, c2), pl.ds(9 * c, c)]
    per = c2 // n

    def piece(s, t):
        if t == 27:
            return ct[pl.ds(s * per, per), :]
        k, tap = t // 9, t % 9
        return acc[pl.ds(k * c2 + s * per, per), pl.ds(tap * c, c)]

    spread(par[sub], keep, send, n, 28, piece)


def back_body(n, sub, par, slope, w, cot, ds, ds_edge, own, halo, cbias, keep, send, up, st, rhs, acc):
    bx, by, bz, c = cot.shape
    cx, cy, cz = bx // 2, by // 2, bz // 2
    c2 = slope.shape[3]
    cells = cx * cy * cz
    total = jnp.zeros((cells, 3 * c), F32)
    for i in range(3):
        for j in range(3):
            tap = slope[2 - i : 2 - i + cx, 2 - j : 2 - j + cy].reshape(cells, c2)
            total = total + lax.dot_general(
                tap,
                w[i, j].reshape(3 * c, c2),
                (((1,), (1,)), ((), ())),
                preferred_element_type=F32,
            )
    pooled = (
        total[:, c : 2 * c]
        + shift_rows(total[:, :c], -1, cz)
        + shift_rows(total[:, 2 * c :], 1, cz)
    ) * 0.125
    up[pl.ds(0, cells, stride=2), :] = pooled
    up[pl.ds(1, cells, stride=2), :] = pooled
    rows = by * bz
    for x in range(bx):
        base = up[pl.ds((x // 2) * cy * bz, cy * bz), :].reshape(cy, 1, bz, c)
        fine = cot[x].astype(F32).reshape(cy, 2, bz, c) + base
        gain = ds[x - 1] if 0 < x < bx - 1 else ds_edge[x // (bx - 1)]
        fs = (fine.reshape(rows, c) * gain.reshape(rows, c)).astype(BF16)
        wide = fs.astype(F32)
        st[pl.ds(0, c), pl.ds(x * rows, rows)] = shift_rows(wide, -1, bz).astype(BF16).T
        st[pl.ds(c, c), pl.ds(x * rows, rows)] = fs.T
        st[pl.ds(2 * c, c), pl.ds(x * rows, rows)] = shift_rows(wide, 1, bz).astype(BF16).T
    voxels = bx * rows
    for t in range(0, 10, 2):
        for h in (0, 1):
            i, j = (t + h) // 3, (t + h) % 3
            if t + h == 9:
                rhs[:, pl.ds(h * c, c)] = jnp.ones((voxels, c), BF16)
            else:
                first, past = max(i - 1, 0), min(i - 1 + bx, bx)
                at = (first - i + 1) * rows
                size = (past - first) * rows
                rhs[pl.ds(at, size), pl.ds(h * c, c)] = own[first:past, j : j + by].reshape(size, c)
                if i != 1:
                    edge = halo[i // 2, j : j + by].reshape(rows, c)
                    rhs[pl.ds(0 if i == 0 else size, rows), pl.ds(h * c, c)] = edge
        acc[:, pl.ds(t * c, 2 * c)] = jnp.dot(
            st[...], rhs[...], preferred_element_type=F32
        ).astype(BF16)
    per, cper = c // n, c2 // n
    lane = lax.broadcasted_iota(jnp.int32, (per, c), 1)

    def piece(s, t):
        if t == 27:
            bias = acc[pl.ds(c + s * per, per), pl.ds(9 * c, c)].astype(F32)
            one = cbias[pl.ds(s * cper, per), :].astype(F32)
            two = cbias[pl.ds(s * cper + per, per), :].astype(F32)
            return jnp.where(lane == 0, bias, jnp.where(lane == 1, one, two)).astype(BF16)
        k, tap = t // 9, t % 9
        return acc[pl.ds(k * c + s * per, per), pl.ds(tap * c, c)]

    spread(par[sub], keep, send, n, 28, piece)


def merge_body(par, hidden, hid_edge, coarse, wm, out, tmp):
    bx, by, bz, c = out.shape
    cx, cy, cz = bx // 2, by // 2, bz // 2
    c2 = coarse.shape[3]
    cells = cx * cy * cz
    proj = jnp.dot(coarse[...].reshape(cells, c2), wm[...], preferred_element_type=F32)
    tmp[pl.ds(0, cells, stride=2), :] = proj
    tmp[pl.ds(1, cells, stride=2), :] = proj
    for x in range(bx):
        base = tmp[pl.ds((x // 2) * cy * bz, cy * bz), :].reshape(cy, 1, bz, c)
        hid = hidden[x - 1] if 0 < x < bx - 1 else hid_edge[x // (bx - 1)]
        total = hid.astype(F32).reshape(cy, 2, bz, c) + base
        out[x] = total.astype(BF16).reshape(by, bz, c)


def swap_faces(first, second, axis):
    n = lax.axis_size(axis)
    one = [p for i in range(0, n - 1, 2) for p in ((i, i + 1), (i + 1, i))]
    two = [p for i in range(1, n - 1, 2) for p in ((i, i + 1), (i + 1, i))]
    got = lax.ppermute(second, axis, two)
    return lax.ppermute(first, axis, one), got


def split4_body(at_grp, at_sub, par, keep, got, own, over_sub, over_grp, over_both):
    g, s = par[at_grp], par[at_sub]

    def part(a, b):
        return (keep[a, :, b].astype(F32) + got[a, :, b].astype(F32)).astype(BF16)

    over_both[...] = part(1 - s, 1 - g)
    over_sub[...] = part(1 - s, g)
    over_grp[...] = part(s, 1 - g)
    own[...] = part(s, g)


def split_body(count, bit, par, *refs):
    parts, keep, send = refs[:count], refs[count], refs[count + 1]

    def part(at):
        return sum(p[at].astype(F32) for p in parts).astype(BF16)

    send[...] = part(1 - par[bit])
    keep[...] = part(par[bit])


def sum_body(count, par, *refs):
    refs[count][...] = sum(p[...].astype(F32) for p in refs[:count]).astype(BF16)


def partners(value, grp_mask, sub_mask):
    n_grp, n_sub = lax.axis_size("grp"), lax.axis_size("sub")
    pairs = [
        (g * n_sub + s, (g ^ grp_mask) * n_sub + (s ^ sub_mask))
        for g in range(n_grp)
        for s in range(n_sub)
    ]
    return lax.ppermute(value, ("grp", "sub"), pairs)


def split_sum(parts, bits, bit, name):
    rows, c = parts[0].shape
    half = ((rows // 2, c), BF16)
    shaped = [p.reshape(2, rows // 2, c) for p in parts]
    return call(
        functools.partial(split_body, len(parts), bit), name, (bits, *shaped), [half, half], (), 0.8
    )


def grp_bits():
    return lax.axis_size("grp").bit_length() - 1


def cores(send):
    return partners(send, 0, 1)


def spread_sum(keep, got, bits, name):
    half, rows, c = keep.shape
    rest = half // 2
    shape = (2, rest, 2, rows // 2, c)
    out = ((rest, rows // 2, c), BF16)
    own, over_sub, over_grp, over_both = call(
        functools.partial(split4_body, 0, grp_bits() + 1), name, (bits, keep.reshape(shape), got.reshape(shape)), [out] * 4, (), 1
    )
    return own, over_sub, over_grp, over_both


def cross(own, over_sub, over_grp, over_both):
    return [own, partners(over_both, 1, 2), partners(over_sub, 0, 2), partners(over_grp, 1, 0)]


def finish_sum(parts, places, name):
    rest, rows, c = parts[0].shape
    parts = [p.reshape(rest * rows, c) for p in parts]
    for bit in range(2, lax.axis_size("sub").bit_length() - 1):
        keep, send = split_sum(parts, places, grp_bits() + bit, name + f"_sub{bit}")
        parts = [keep, partners(send, 0, 1 << bit)]
    bits = [0]
    last = grp_bits() - 1
    for bit in range(1, last + 1):
        mask = 1 << bit
        if bit == 1 and bit < last and parts[0].shape[0] % 32 == 0:
            keep, send = split_sum(parts, places, bit, name + "_half")
            parts = [keep, partners(send, mask, 0)]
            bits.append(bit)
            continue
        out = [(parts[0].shape, BF16)]
        (total,) = call(
            functools.partial(sum_body, len(parts)), name + f"_sum{bit}", (places, *parts), out, (), 0.5
        )
        parts = [total, partners(total, mask, 0)]
    (total,) = call(
        functools.partial(sum_body, len(parts)), name + "_total", (places, *parts), [(parts[0].shape, BF16)], (), 0.5
    )
    pieces = [total]
    for which in range(1, 2 ** len(bits)):
        pieces.append(partners(total, sum(1 << bits[b] for b in range(len(bits)) if which >> b & 1), 0))
    return pieces, bits


def last_body(count, par, *refs):
    pieces, kernel, extra, rows = refs[:count], refs[count], refs[count + 1], refs[-1]
    size = pieces[0].shape[0]
    per = extra.shape[0] if len(refs) == count + 3 else kernel.shape[3]
    mine = par[0] if count == 2 else 2 * par[0] + par[1]
    for which in range(count):
        mask = which if count == 2 else 2 * (which & 1) + (which >> 1)
        rows[mine ^ mask] = pieces[which][...]

    def block(t):
        at, off = t * per // size, t * per % size
        if off + per <= size:
            return rows[at, pl.ds(off, per)].astype(F32)
        first = size - off
        return jnp.concatenate([rows[at, pl.ds(off, first)], rows[at + 1, pl.ds(0, per - first)]], axis=0).astype(F32)

    for t in range(27):
        kernel[(t // 3) % 3, t % 3, t // 9] = block(t)
    if len(refs) == count + 3:
        extra[...] = block(27)
    else:
        turned = block(27).T
        extra[...] = turned[0:1]
        refs[count + 2][:, pl.ds(0, per)] = turned[1:2]
        refs[count + 2][:, pl.ds(per, per)] = turned[2:3]


def last(pieces, bits, places, per, outs, name):
    count = len(pieces)
    size, c = pieces[0].shape
    kernel, *rest = call(
        functools.partial(last_body, count),
        name,
        (places, *pieces),
        [((3, 3, 3, per, c), F32), *outs],
        [pltpu.VMEM((count, size, c), BF16)],
        1,
    )
    return jnp.swapaxes(kernel, 3, 4), *rest


def per_device(field, cotangent, fine_kernel, fine_bias, coarse_kernel, coarse_bias, merge_weight):
    grp, sub = lax.axis_index("grp"), lax.axis_index("sub")
    n = lax.axis_size("sub")
    bx, by, bz, c = field.shape
    cx, cy, cz = bx // 2, by // 2, bz // 2
    c2 = merge_weight.shape[0]
    count = grp_bits()
    order = jnp.arange(count + n.bit_length() - 1, dtype=jnp.int32)
    par = jnp.where(order < count, grp >> order, sub >> (order - count)).astype(jnp.int32) & 1
    face = ((bx, bz, c), BF16)
    sa, sb = call(
        functools.partial(prep_body, count),
        "prep",
        (par, (field, None, None)),
        [face, face],
        [pltpu.SemaphoreType.DMA((2,))],
        limit=127 * 512 * 1024,
    )
    ya, yb = swap_faces(sa, sb, "sub")
    (pg,) = call(
        cubes_body, "cubes", (par, cotangent), [((cx, cy, cz, c), BF16)], [pltpu.VMEM((cx * cy * bz, c), F32)]
    )
    face = ((by + 2, bz, c), BF16)
    own, ta, tb = call(
        functools.partial(turn_body, count),
        "turn",
        (par, field, ya, yb),
        [((bx, by + 2, bz, c), BF16), face, face],
    )
    xa, xb = swap_faces(ta, tb, "grp")
    bias = fine_bias.reshape(1, c)
    hidden, ds, pooled, wb = call(
        inner_body,
        "inner",
        (par, own, fine_kernel, bias),
        [
            ((bx - 2, by, bz, c), BF16),
            ((bx - 2, by, bz, c), F32),
            ((cx - 2, cy, cz, c), BF16),
            ((9 * c, 3 * c), BF16),
        ],
        [pltpu.VMEM((cy * bz, c), F32)],
        6,
    )
    face = ((3, cy, cz, c), BF16)
    hid_edge, ds_edge, halo, pooled, pa, pb = call(
        outer_body,
        "outer",
        (par, own, xa, xb, wb, bias, hidden, pooled, pg),
        [
            ((2, by, bz, c), BF16),
            ((2, by, bz, c), F32),
            ((2, by + 2, bz, c), BF16),
            ((cx, cy, cz, c), BF16),
            face,
            face,
        ],
        [pltpu.VMEM((cy * bz, c), F32)],
        2,
    )
    pxa, pxb = swap_faces(pa, pb, "grp")
    face = ((2 * (cx + 4) + cx + 2, cz, c), BF16)
    qa, qb = call(functools.partial(turn2_body, count), "turn2", (par, pooled, pg, pxa, pxb), [face, face])
    pya, pyb = swap_faces(qa, qb, "sub")
    cells = cx * cy * cz
    part = (n // 2, 28 * (c2 // n), c)
    slope, coarse, ckeep, csend, cbias = call(
        functools.partial(coarse_body, n, count),
        "coarse",
        (par, pooled, pxa, pxb, pya, pyb, pg, coarse_kernel, coarse_bias.reshape(1, c2), merge_weight),
        [
            ((cx + 2, cy + 2, cz, c2), BF16),
            ((cx, cy, cz, c2), BF16),
            (part, BF16),
            (part, BF16),
            ((c2, c), BF16),
        ],
        [
            pltpu.VMEM((cx + 4, cy + 4, cz, c), BF16),
            pltpu.VMEM((cx + 2, cy + 2, cz, c), BF16),
            pltpu.VMEM((9 * c, 3 * c2), BF16),
            pltpu.VMEM((3 * c2, cells), BF16),
            pltpu.VMEM((cells, 10 * c), BF16),
            pltpu.VMEM((3 * c2, 10 * c), BF16),
            pltpu.VMEM((c2, c), BF16),
        ],
        6,
    )
    cgot = cores(csend)
    (output,) = call(
        merge_body,
        "merge",
        (par, hidden, hid_edge, coarse, merge_weight),
        [((bx, by, bz, c), BF16)],
        [pltpu.VMEM((cx * cy * bz, c), F32)],
        2,
    )
    output, cgot = lax.optimization_barrier((output, cgot))
    csent = spread_sum(ckeep, cgot, par, "coarse_split")
    slope, csent = lax.optimization_barrier((slope, csent))
    cparts = cross(*csent)
    voxels = bx * by * bz
    part = (n // 2, 28 * (c // n), c)
    fkeep, fsend = call(
        functools.partial(back_body, n, count),
        "back",
        (par, slope, coarse_kernel, cotangent, ds, ds_edge, own, halo, cbias),
        [(part, BF16), (part, BF16)],
        [
            pltpu.VMEM((cx * cy * bz, c), F32),
            pltpu.VMEM((3 * c, voxels), BF16),
            pltpu.VMEM((voxels, 2 * c), BF16),
            pltpu.VMEM((3 * c, 10 * c), BF16),
        ],
        10,
    )
    fsend, cparts = lax.optimization_barrier((fsend, cparts))
    fgot = cores(fsend)
    fparts = cross(*spread_sum(fkeep, fgot, par, "fine_split"))
    coarse_sum = finish_sum(cparts, par, "coarse")
    fine_sum = finish_sum(fparts, par, "fine")
    per, cper = c // n, c2 // n
    grad_coarse, grad_merge = last(*coarse_sum, par, cper, [((cper, c), F32)], "coarse_last")
    biases = [((1, per), F32), ((1, cper), F32)]
    grad_fine, bias, coarse_sums = last(*fine_sum, par, per, biases, "fine_last")
    return (output, grad_fine, bias[0], grad_coarse, coarse_sums[0], grad_merge)


def solution(mesh):
    in_specs = (P("grp", "sub", None, None), P("grp", "sub", None, None), P(), P(), P(), P(), P())
    out_specs = (
        P("grp", "sub", None, None),
        P(None, None, None, None, "sub"),
        P("sub"),
        P(None, None, None, None, "sub"),
        P("sub"),
        P("sub", None),
    )
    return jax.shard_map(
        per_device, mesh=mesh, in_specs=in_specs, out_specs=out_specs, check_vma=False
    )
```

```python
import functools

import jax
import jax.numpy as jnp
from jax import lax
from jax.experimental import pallas as pl
from jax.experimental.pallas import tpu as pltpu
from jax.sharding import PartitionSpec as P

F32 = jnp.float32
BF16 = jnp.bfloat16
VMEM_LIMIT = 32 * 1024 * 1024
PREP_LIMIT = 127 * 512 * 1024


def bit_of(axis, bit=0):
    return (lax.axis_index(axis) >> bit) & 1


def call(body, name, args, outs, scratch=(), micros=1, space=pltpu.VMEM):
    return pl.pallas_call(
        body,
        name=name,
        out_shape=[jax.ShapeDtypeStruct(s, t) for s, t in outs],
        in_specs=[pl.BlockSpec(memory_space=space) for _ in args],
        out_specs=[pl.BlockSpec(memory_space=space) for _ in outs],
        scratch_shapes=list(scratch),
        compiler_params=pltpu.CompilerParams(vmem_limit_bytes=VMEM_LIMIT if space == pltpu.VMEM else PREP_LIMIT),
        cost_estimate=pl.CostEstimate(
            flops=int(micros * 1e9), bytes_accessed=0, transcendentals=0
        ),
    )(*args)


def put_faces(odd, first, second, low, high):
    first[...] = jnp.where(odd, low, high)
    second[...] = jnp.where(odd, high, low)


def get_faces(odd, first, second):
    a, b = first[...], second[...]
    return jnp.where(odd, a, b), jnp.where(odd, b, a)


def sum_cube(rows, planes, ref):
    half = rows // 2
    ref[pl.ds(0, rows), :] = planes
    return ref[pl.ds(0, half, stride=2), :] + ref[pl.ds(1, half, stride=2), :]


def shift_rows(value, step, depth):
    rows = value.shape[0]
    moved = pltpu.roll(value, step % rows, 0)
    place = lax.broadcasted_iota(jnp.int32, value.shape, 0) % depth
    edge = 0 if step == 1 else depth - 1
    return jnp.where(place == edge, 0.0, moved)


def sigmoid(value):
    return 1.0 / (1.0 + jnp.exp(-value))


def prep_body(field, out_a, out_b, sems):
    odd, end = bit_of("sub"), field.shape[1] - 1
    one = pltpu.make_async_copy(field.at[:, (1 - odd) * end], out_a, sems.at[0])
    two = pltpu.make_async_copy(field.at[:, odd * end], out_b, sems.at[1])
    one.start()
    two.start()
    one.wait()
    two.wait()


def turn_body(field, ya, yb, own, out_a, out_b):
    bx, by = field.shape[0], field.shape[1]
    ylo, yhi = get_faces(bit_of("sub") == 1, ya, yb)
    own[:, 1 : by + 1] = field[...]
    own[:, 0] = ylo
    own[:, by + 1] = yhi
    put_faces(bit_of("grp") == 1, out_a, out_b, own[0], own[bx - 1])


def fine_plane(three, wb, bias, by):
    _, bz, c = three[0].shape
    rows = by * bz
    taps = [plane[j : j + by].reshape(rows, c) for plane in three for j in range(3)]
    part = jnp.dot(jnp.concatenate(taps, axis=1), wb[...], preferred_element_type=F32)
    pre = (
        part[:, c : 2 * c]
        + shift_rows(part[:, :c], 1, bz)
        + shift_rows(part[:, 2 * c :], -1, bz)
        + bias[...]
    )
    sig = sigmoid(pre)
    hid = (pre * sig).astype(BF16).reshape(by, bz, c)
    return hid, (sig * (1.0 + pre * (1.0 - sig))).reshape(by, bz, c)


def pool(one, two, tmp):
    by, bz, c = one.shape
    cy = by // 2
    both = jnp.sum((one.astype(F32) + two.astype(F32)).reshape(cy, 2, bz, c), axis=1)
    total = sum_cube(cy * bz, both.reshape(cy * bz, c), tmp)
    return (total / 8.0).astype(BF16).reshape(cy, bz // 2, c)


def inner_body(own, w, bias, hidden, ds, pooled, wb, tmp):
    by, c = own.shape[1] - 2, own.shape[3]
    for i in range(3):
        for j in range(3):
            for k in range(3):
                wb[pl.ds((3 * i + j) * c, c), pl.ds(k * c, c)] = w[i, j, k]

    def plane(x, carry):
        hid, slope = fine_plane([own[x], own[x + 1], own[x + 2]], wb, bias, by)
        hidden[x], ds[x] = hid, slope
        return carry

    lax.fori_loop(0, hidden.shape[0], plane, 0)
    for q in range(pooled.shape[0]):
        pooled[q] = pool(hidden[2 * q + 1], hidden[2 * q + 2], tmp)


def outer_body(own, ra, rb, wb, bias, hid_in, pool_in, pg, hidden, ds, halo, pooled, out_a, out_b, tmp):
    bx, by = own.shape[0], own.shape[1] - 2
    cx = bx // 2
    xlo, xhi = get_faces(bit_of("grp") == 1, ra, rb)
    halo[0], halo[1] = xlo, xhi
    for at, three in ((0, [halo[0], own[0], own[1]]), (1, [own[bx - 2], own[bx - 1], halo[1]])):
        hidden[at], ds[at] = fine_plane(three, wb, bias, by)
    pooled[0] = pool(hidden[0], hid_in[0], tmp)
    pooled[1 : cx - 1] = pool_in[...]
    pooled[cx - 1] = pool(hid_in[bx - 3], hidden[1], tmp)
    low = jnp.concatenate([pooled[0:2], pg[0:1]], axis=0)
    high = jnp.concatenate([pooled[cx - 2 : cx], pg[cx - 1 : cx]], axis=0)
    put_faces(bit_of("grp") == 1, out_a, out_b, low, high)


def cubes_body(cot, pg, bits, tmp):
    bx, by, bz, c = cot.shape
    cx, cy, cz = bx // 2, by // 2, bz // 2
    total = jnp.sum(cot[...].astype(F32).reshape(cx, 2, cy, 2, bz, c), axis=(1, 3))
    grad = sum_cube(cx * cy * bz, total.reshape(cx * cy * bz, c), tmp).astype(BF16)
    pg[...] = grad.reshape(cx, cy, cz, c)
    first = grp_bits()
    for k in range(bits.shape[0]):
        value = bit_of("grp", k) if k < first else bit_of("sub", k - first)
        bits[k] = jnp.full(bits.shape[1:], value, jnp.int32)


def turn2_body(pooled, pg, ra, rb, out_a, out_b):
    cy = pooled.shape[1]
    xlo, xhi = get_faces(bit_of("grp") == 1, ra, rb)

    def side(y, last):
        two = [jnp.concatenate([xlo[0:2, at], pooled[:, at], xhi[0:2, at]], axis=0) for at in (y, y + 1)]
        one = jnp.concatenate([xlo[2:3, last], pg[:, last], xhi[2:3, last]], axis=0)
        return jnp.concatenate([*two, one], axis=0)

    put_faces(bit_of("sub") == 1, out_a, out_b, side(0, 0), side(cy - 2, cy - 1))


def reverse_bits(value, count):
    out = 0
    for _ in range(count):
        out, value = out * 2 + value % 2, value // 2
    return out


def spread(keep, send, n, blocks, piece):
    bits = n.bit_length() - 1
    half = n // 2
    for b in (0, 1):

        @pl.when(bit_of("sub") == b)
        def _():
            for s in range(n):
                target = keep if s % 2 == b else send
                for t in range(blocks):
                    value = piece(s, t)
                    size = value.shape[0]
                    target[reverse_bits(s, bits) % half, pl.ds(t * size, size)] = value


def coarse_body(
    n, pooled, ra, rb, ua, ub, pg, w, bias, wm,
    slope, coarse, keep, send, cbias, qpad, gpad, wb, st, rhs, acc, ct,
):
    cx, cy, cz, c = pooled.shape
    c2 = wm.shape[0]
    xlo, xhi = get_faces(bit_of("grp") == 1, ra, rb)
    ylo, yhi = get_faces(bit_of("sub") == 1, ua, ub)
    qpad[2 : cx + 2, 2 : cy + 2] = pooled[...]
    qpad[0:2, 2 : cy + 2] = xlo[0:2]
    qpad[cx + 2 : cx + 4, 2 : cy + 2] = xhi[0:2]
    wide = cx + 4
    for t in (0, 1):
        qpad[:, t] = ylo[t * wide : (t + 1) * wide]
        qpad[:, cy + 2 + t] = yhi[t * wide : (t + 1) * wide]
    gpad[1 : cx + 1, 1 : cy + 1] = pg[...]
    gpad[0, 1 : cy + 1] = xlo[2]
    gpad[cx + 1, 1 : cy + 1] = xhi[2]
    gpad[:, 0] = ylo[2 * wide :]
    gpad[:, cy + 1] = yhi[2 * wide :]
    for i in range(3):
        for j in range(3):
            for k in range(3):
                wb[pl.ds((3 * i + j) * c, c), pl.ds(k * c2, c2)] = w[i, j, k]
    wide = cy + 2
    rows = wide * cz

    def plane(x, carry):
        taps = [qpad[x + i, j : j + wide].reshape(rows, c) for i in range(3) for j in range(3)]
        part = jnp.dot(jnp.concatenate(taps, axis=1), wb[...], preferred_element_type=F32)
        pre = (
            part[:, c2 : 2 * c2]
            + shift_rows(part[:, :c2], 1, cz)
            + shift_rows(part[:, 2 * c2 :], -1, cz)
            + bias[...]
        )
        sig = sigmoid(pre)
        back = lax.dot_general(
            gpad[x].reshape(rows, c), wm[...], (((1,), (1,)), ((), ())), preferred_element_type=F32
        )
        slope[x] = (back * (sig * (1.0 + pre * (1.0 - sig)))).astype(BF16).reshape(wide, cz, c2)

        @pl.when((x >= 1) & (x <= cx))
        def _():
            coarse[x - 1] = (pre * sig).astype(BF16).reshape(wide, cz, c2)[1 : cy + 1]

        return carry

    lax.fori_loop(0, cx + 2, plane, 0)
    cells = cx * cy * cz
    mid = slope[1 : cx + 1, 1 : cy + 1].reshape(cells, c2)
    wide_mid = mid.astype(F32)
    st[pl.ds(0, c2), :] = shift_rows(wide_mid, -1, cz).astype(BF16).T
    st[pl.ds(c2, c2), :] = mid.T
    st[pl.ds(2 * c2, c2), :] = shift_rows(wide_mid, 1, cz).astype(BF16).T
    for i in range(3):
        for j in range(3):
            rhs[:, pl.ds((3 * i + j) * c, c)] = qpad[
                1 + i : 1 + i + cx, 1 + j : 1 + j + cy
            ].reshape(cells, c)
    rhs[:, pl.ds(9 * c, c)] = jnp.ones((cells, c), BF16)
    acc[...] = jnp.dot(st[...], rhs[...], preferred_element_type=F32).astype(BF16)
    ct[...] = jnp.dot(
        coarse[...].reshape(cells, c2).T, pg[...].reshape(cells, c), preferred_element_type=F32
    ).astype(BF16)
    cbias[...] = acc[pl.ds(c2, c2), pl.ds(9 * c, c)]
    per = c2 // n

    def piece(s, t):
        if t == 27:
            return ct[pl.ds(s * per, per), :]
        k, tap = t // 9, t % 9
        return acc[pl.ds(k * c2 + s * per, per), pl.ds(tap * c, c)]

    spread(keep, send, n, 28, piece)


def back_body(n, slope, w, cot, ds, ds_edge, own, halo, cbias, keep, send, up, st, rhs, acc):
    bx, by, bz, c = cot.shape
    cx, cy, cz = bx // 2, by // 2, bz // 2
    c2 = slope.shape[3]
    cells = cx * cy * cz
    total = jnp.zeros((cells, 3 * c), F32)
    for i in range(3):
        for j in range(3):
            tap = slope[2 - i : 2 - i + cx, 2 - j : 2 - j + cy].reshape(cells, c2)
            total = total + lax.dot_general(
                tap,
                w[i, j].reshape(3 * c, c2),
                (((1,), (1,)), ((), ())),
                preferred_element_type=F32,
            )
    pooled = (
        total[:, c : 2 * c]
        + shift_rows(total[:, :c], -1, cz)
        + shift_rows(total[:, 2 * c :], 1, cz)
    ) * 0.125
    up[pl.ds(0, cells, stride=2), :] = pooled
    up[pl.ds(1, cells, stride=2), :] = pooled
    rows = by * bz
    for x in range(bx):
        base = up[pl.ds((x // 2) * cy * bz, cy * bz), :].reshape(cy, 1, bz, c)
        fine = cot[x].astype(F32).reshape(cy, 2, bz, c) + base
        gain = ds[x - 1] if 0 < x < bx - 1 else ds_edge[x // (bx - 1)]
        fs = (fine.reshape(rows, c) * gain.reshape(rows, c)).astype(BF16)
        wide = fs.astype(F32)
        st[pl.ds(0, c), pl.ds(x * rows, rows)] = shift_rows(wide, -1, bz).astype(BF16).T
        st[pl.ds(c, c), pl.ds(x * rows, rows)] = fs.T
        st[pl.ds(2 * c, c), pl.ds(x * rows, rows)] = shift_rows(wide, 1, bz).astype(BF16).T
    voxels = bx * rows
    for t in range(0, 10, 2):
        for h in (0, 1):
            i, j = (t + h) // 3, (t + h) % 3
            if t + h == 9:
                rhs[:, pl.ds(h * c, c)] = jnp.ones((voxels, c), BF16)
            else:
                first, past = max(i - 1, 0), min(i - 1 + bx, bx)
                at = (first - i + 1) * rows
                size = (past - first) * rows
                rhs[pl.ds(at, size), pl.ds(h * c, c)] = own[first:past, j : j + by].reshape(size, c)
                if i != 1:
                    edge = halo[i // 2, j : j + by].reshape(rows, c)
                    rhs[pl.ds(0 if i == 0 else size, rows), pl.ds(h * c, c)] = edge
        acc[:, pl.ds(t * c, 2 * c)] = jnp.dot(
            st[...], rhs[...], preferred_element_type=F32
        ).astype(BF16)
    per, cper = c // n, c2 // n
    lane = lax.broadcasted_iota(jnp.int32, (per, c), 1)

    def piece(s, t):
        if t == 27:
            bias = acc[pl.ds(c + s * per, per), pl.ds(9 * c, c)].astype(F32)
            one = cbias[pl.ds(s * cper, per), :].astype(F32)
            two = cbias[pl.ds(s * cper + per, per), :].astype(F32)
            return jnp.where(lane == 0, bias, jnp.where(lane == 1, one, two)).astype(BF16)
        k, tap = t // 9, t % 9
        return acc[pl.ds(k * c + s * per, per), pl.ds(tap * c, c)]

    spread(keep, send, n, 28, piece)


def merge_body(hidden, hid_edge, coarse, wm, out, tmp):
    bx, by, bz, c = out.shape
    cx, cy, cz = bx // 2, by // 2, bz // 2
    c2 = coarse.shape[3]
    cells = cx * cy * cz
    proj = jnp.dot(coarse[...].reshape(cells, c2), wm[...], preferred_element_type=F32)
    tmp[pl.ds(0, cells, stride=2), :] = proj
    tmp[pl.ds(1, cells, stride=2), :] = proj
    for x in range(bx):
        base = tmp[pl.ds((x // 2) * cy * bz, cy * bz), :].reshape(cy, 1, bz, c)
        hid = hidden[x - 1] if 0 < x < bx - 1 else hid_edge[x // (bx - 1)]
        total = hid.astype(F32).reshape(cy, 2, bz, c) + base
        out[x] = total.astype(BF16).reshape(by, bz, c)


def swap_faces(first, second, axis):
    n = lax.axis_size(axis)
    one = [p for i in range(0, n - 1, 2) for p in ((i, i + 1), (i + 1, i))]
    two = [p for i in range(1, n - 1, 2) for p in ((i, i + 1), (i + 1, i))]
    got = lax.ppermute(second, axis, two)
    return lax.ppermute(first, axis, one), got


def split4_body(keep, got, own, over_sub, over_grp, over_both):
    g, s = bit_of("grp"), bit_of("sub", 1)

    def part(a, b):
        return (keep[a, :, b].astype(F32) + got[a, :, b].astype(F32)).astype(BF16)

    over_both[...] = part(1 - s, 1 - g)
    over_sub[...] = part(1 - s, g)
    over_grp[...] = part(s, 1 - g)
    own[...] = part(s, g)


def total_of(parts):
    return sum(p.astype(F32) for p in parts).astype(BF16)


def halves(pair, bit):
    return jnp.where(bit == 1, pair[1], pair[0]), jnp.where(bit == 1, pair[0], pair[1])


def partners(value, grp_mask, sub_mask):
    n_grp, n_sub = lax.axis_size("grp"), lax.axis_size("sub")
    pairs = [
        (g * n_sub + s, (g ^ grp_mask) * n_sub + (s ^ sub_mask))
        for g in range(n_grp)
        for s in range(n_sub)
    ]
    return lax.ppermute(value, ("grp", "sub"), pairs)


def split_sum(parts, bit):
    rows, c = parts[0].shape
    return halves(total_of([p.reshape(2, rows // 2, c) for p in parts]), bit)


def grp_bits():
    return lax.axis_size("grp").bit_length() - 1


def cores(send):
    return partners(send, 0, 1)


def spread_sum(keep, got):
    half, rows, c = keep.shape
    rest = half // 2
    shape = (2, rest, 2, rows // 2, c)
    out = ((rest, rows // 2, c), BF16)
    return call(split4_body, "split", (keep.reshape(shape), got.reshape(shape)), [out] * 4, (), 1)


def spread_sum_plain(keep, got, places):
    half, rows, c = keep.shape
    rest = half // 2
    total = total_of([keep, got]).reshape(2, rest, 2, rows // 2, c)
    near, far = halves(total, places[grp_bits() + 1])
    own, over_grp = halves((near[:, 0], near[:, 1]), places[0])
    over_sub, over_both = halves((far[:, 0], far[:, 1]), places[0])
    return own, over_sub, over_grp, over_both


def cross(own, over_sub, over_grp, over_both):
    return [own, partners(over_both, 1, 2), partners(over_sub, 0, 2), partners(over_grp, 1, 0)]


def finish_sum(parts, places):
    rest, rows, c = parts[0].shape
    parts = [p.reshape(rest * rows, c) for p in parts]
    for bit in range(2, lax.axis_size("sub").bit_length() - 1):
        keep, send = split_sum(parts, places[grp_bits() + bit])
        parts = [keep, partners(send, 0, 1 << bit)]
    bits = [0]
    last = grp_bits() - 1
    for bit in range(1, last + 1):
        mask = 1 << bit
        if bit == 1 and bit < last and parts[0].shape[0] % 32 == 0:
            keep, send = split_sum(parts, places[bit])
            parts = [keep, partners(send, mask, 0)]
            bits.append(bit)
        else:
            total = total_of(parts)
            parts = [total, partners(total, mask, 0)]
    total = total_of(parts)
    pieces = [total]
    for which in range(1, 2 ** len(bits)):
        pieces.append(partners(total, sum(1 << bits[b] for b in range(len(bits)) if which >> b & 1), 0))
    return pieces


def last_body(count, *refs):
    pieces, kernel, extra, rows = refs[:count], refs[count], refs[count + 1], refs[-1]
    size = pieces[0].shape[0]
    per = extra.shape[0] if len(refs) == count + 3 else kernel.shape[3]
    mine = bit_of("grp") if count == 2 else 2 * bit_of("grp") + bit_of("grp", 1)
    for which in range(count):
        mask = which if count == 2 else 2 * (which & 1) + (which >> 1)
        rows[mine ^ mask] = pieces[which][...]

    def block(t):
        at, off = t * per // size, t * per % size
        if off + per <= size:
            return rows[at, pl.ds(off, per)].astype(F32)
        first = size - off
        return jnp.concatenate([rows[at, pl.ds(off, first)], rows[at + 1, pl.ds(0, per - first)]], axis=0).astype(F32)

    for t in range(27):
        kernel[(t // 3) % 3, t % 3, t // 9] = block(t)
    if len(refs) == count + 3:
        extra[...] = block(27)
    else:
        turned = block(27).T
        extra[...] = turned[0:1]
        refs[count + 2][:, pl.ds(0, per)] = turned[1:2]
        refs[count + 2][:, pl.ds(per, per)] = turned[2:3]


def last(pieces, per, outs, name):
    count = len(pieces)
    size, c = pieces[0].shape
    kernel, *rest = call(
        functools.partial(last_body, count),
        name,
        tuple(pieces),
        [((3, 3, 3, per, c), F32), *outs],
        [pltpu.VMEM((count, size, c), BF16)],
        1,
    )
    return jnp.swapaxes(kernel, 3, 4), *rest


def per_device(field, cotangent, fine_kernel, fine_bias, coarse_kernel, coarse_bias, merge_weight):
    n = lax.axis_size("sub")
    bx, by, bz, c = field.shape
    cx, cy, cz = bx // 2, by // 2, bz // 2
    c2 = merge_weight.shape[0]
    face = ((bx, bz, c), BF16)
    sa, sb = call(
        prep_body, "prep", (field,), [face, face], [pltpu.SemaphoreType.DMA((2,))], space=pltpu.HBM
    )
    ya, yb = swap_faces(sa, sb, "sub")
    count = grp_bits() + n.bit_length() - 1
    pg, places = call(
        cubes_body,
        "cubes",
        (cotangent,),
        [((cx, cy, cz, c), BF16), ((count, 1, c), jnp.int32)],
        [pltpu.VMEM((cx * cy * bz, c), F32)],
    )
    face = ((by + 2, bz, c), BF16)
    own, ta, tb = call(
        turn_body,
        "turn",
        (field, ya, yb),
        [((bx, by + 2, bz, c), BF16), face, face],
    )
    xa, xb = swap_faces(ta, tb, "grp")
    bias = fine_bias.reshape(1, c)
    hidden, ds, pooled, wb = call(
        inner_body,
        "inner",
        (own, fine_kernel, bias),
        [
            ((bx - 2, by, bz, c), BF16),
            ((bx - 2, by, bz, c), F32),
            ((cx - 2, cy, cz, c), BF16),
            ((9 * c, 3 * c), BF16),
        ],
        [pltpu.VMEM((cy * bz, c), F32)],
        6,
    )
    face = ((3, cy, cz, c), BF16)
    hid_edge, ds_edge, halo, pooled, pa, pb = call(
        outer_body,
        "outer",
        (own, xa, xb, wb, bias, hidden, pooled, pg),
        [
            ((2, by, bz, c), BF16),
            ((2, by, bz, c), F32),
            ((2, by + 2, bz, c), BF16),
            ((cx, cy, cz, c), BF16),
            face,
            face,
        ],
        [pltpu.VMEM((cy * bz, c), F32)],
        2,
    )
    pxa, pxb = swap_faces(pa, pb, "grp")
    face = ((2 * (cx + 4) + cx + 2, cz, c), BF16)
    qa, qb = call(turn2_body, "turn2", (pooled, pg, pxa, pxb), [face, face])
    pya, pyb = swap_faces(qa, qb, "sub")
    cells = cx * cy * cz
    part = (n // 2, 28 * (c2 // n), c)
    slope, coarse, ckeep, csend, cbias = call(
        functools.partial(coarse_body, n),
        "coarse",
        (pooled, pxa, pxb, pya, pyb, pg, coarse_kernel, coarse_bias.reshape(1, c2), merge_weight),
        [
            ((cx + 2, cy + 2, cz, c2), BF16),
            ((cx, cy, cz, c2), BF16),
            (part, BF16),
            (part, BF16),
            ((c2, c), BF16),
        ],
        [
            pltpu.VMEM((cx + 4, cy + 4, cz, c), BF16),
            pltpu.VMEM((cx + 2, cy + 2, cz, c), BF16),
            pltpu.VMEM((9 * c, 3 * c2), BF16),
            pltpu.VMEM((3 * c2, cells), BF16),
            pltpu.VMEM((cells, 10 * c), BF16),
            pltpu.VMEM((3 * c2, 10 * c), BF16),
            pltpu.VMEM((c2, c), BF16),
        ],
        6,
    )
    cgot = cores(csend)
    (output,) = call(
        merge_body,
        "merge",
        (hidden, hid_edge, coarse, merge_weight),
        [((bx, by, bz, c), BF16)],
        [pltpu.VMEM((cx * cy * bz, c), F32)],
        2,
    )
    output, cgot = lax.optimization_barrier((output, cgot))
    csent = spread_sum(ckeep, cgot)
    slope, csent = lax.optimization_barrier((slope, csent))
    cparts = cross(*csent)
    voxels = bx * by * bz
    part = (n // 2, 28 * (c // n), c)
    fkeep, fsend = call(
        functools.partial(back_body, n),
        "back",
        (slope, coarse_kernel, cotangent, ds, ds_edge, own, halo, cbias),
        [(part, BF16), (part, BF16)],
        [
            pltpu.VMEM((cx * cy * bz, c), F32),
            pltpu.VMEM((3 * c, voxels), BF16),
            pltpu.VMEM((voxels, 2 * c), BF16),
            pltpu.VMEM((3 * c, 10 * c), BF16),
        ],
        10,
    )
    fsend, cparts = lax.optimization_barrier((fsend, cparts))
    fgot = cores(fsend)
    fparts = cross(*spread_sum_plain(fkeep, fgot, places))
    coarse_sum = finish_sum(cparts, places)
    fine_sum = finish_sum(fparts, places)
    per, cper = c // n, c2 // n
    grad_coarse, grad_merge = last(coarse_sum, cper, [((cper, c), F32)], "coarse_last")
    biases = [((1, per), F32), ((1, cper), F32)]
    grad_fine, bias, coarse_sums = last(fine_sum, per, biases, "fine_last")
    return (output, grad_fine, bias[0], grad_coarse, coarse_sums[0], grad_merge)


def solution(mesh):
    in_specs = (P("grp", "sub", None, None), P("grp", "sub", None, None), P(), P(), P(), P(), P())
    out_specs = (
        P("grp", "sub", None, None),
        P(None, None, None, None, "sub"),
        P("sub"),
        P(None, None, None, None, "sub"),
        P("sub"),
        P("sub", None),
    )
    return jax.shard_map(
        per_device, mesh=mesh, in_specs=in_specs, out_specs=out_specs, check_vma=False
    )
```

```python
import functools

import jax
import jax.numpy as jnp
from jax import lax
from jax.experimental import pallas as pl
from jax.experimental.pallas import tpu as pltpu
from jax.sharding import PartitionSpec as P

F32 = jnp.float32
BF16 = jnp.bfloat16
VMEM_LIMIT = 32 * 1024 * 1024


def bit_of(axis, bit=0):
    return (lax.axis_index(axis) >> bit) & 1


def call(body, name, args, outs, scratch=(), micros=1):
    return pl.pallas_call(
        body,
        name=name,
        out_shape=[jax.ShapeDtypeStruct(s, t) for s, t in outs],
        in_specs=[pl.BlockSpec(memory_space=pltpu.VMEM) for _ in args],
        out_specs=[pl.BlockSpec(memory_space=pltpu.VMEM) for _ in outs],
        scratch_shapes=list(scratch),
        compiler_params=pltpu.CompilerParams(vmem_limit_bytes=VMEM_LIMIT),
        cost_estimate=pl.CostEstimate(
            flops=int(micros * 1e9), bytes_accessed=0, transcendentals=0
        ),
    )(*args)


def put_faces(odd, first, second, low, high):
    first[...] = jnp.where(odd, low, high)
    second[...] = jnp.where(odd, high, low)


def get_faces(odd, first, second):
    a, b = first[...], second[...]
    return jnp.where(odd, a, b), jnp.where(odd, b, a)


def sum_cube(rows, planes, ref):
    half = rows // 2
    ref[pl.ds(0, rows), :] = planes
    return ref[pl.ds(0, half, stride=2), :] + ref[pl.ds(1, half, stride=2), :]


def shift_rows(value, step, depth):
    rows = value.shape[0]
    moved = pltpu.roll(value, step % rows, 0)
    place = lax.broadcasted_iota(jnp.int32, value.shape, 0) % depth
    edge = 0 if step == 1 else depth - 1
    return jnp.where(place == edge, 0.0, moved)


def sigmoid(value):
    return 1.0 / (1.0 + jnp.exp(-value))


def turn_body(field, ya, yb, own, out_a, out_b):
    bx, by = field.shape[0], field.shape[1]
    ylo, yhi = get_faces(bit_of("sub") == 1, ya, yb)
    own[:, 1 : by + 1] = field[...]
    own[:, 0] = ylo
    own[:, by + 1] = yhi
    put_faces(bit_of("grp") == 1, out_a, out_b, own[0], own[bx - 1])


def fine_plane(three, wb, bias, by):
    _, bz, c = three[0].shape
    rows = by * bz
    taps = [plane[j : j + by].reshape(rows, c) for plane in three for j in range(3)]
    part = jnp.dot(jnp.concatenate(taps, axis=1), wb[...], preferred_element_type=F32)
    pre = (
        part[:, c : 2 * c]
        + shift_rows(part[:, :c], 1, bz)
        + shift_rows(part[:, 2 * c :], -1, bz)
        + bias[...]
    )
    sig = sigmoid(pre)
    hid = (pre * sig).astype(BF16).reshape(by, bz, c)
    return hid, (sig * (1.0 + pre * (1.0 - sig))).reshape(by, bz, c)


def pool(one, two, tmp):
    by, bz, c = one.shape
    cy = by // 2
    both = jnp.sum((one.astype(F32) + two.astype(F32)).reshape(cy, 2, bz, c), axis=1)
    total = sum_cube(cy * bz, both.reshape(cy * bz, c), tmp)
    return (total / 8.0).astype(BF16).reshape(cy, bz // 2, c)


def inner_body(own, w, bias, hidden, ds, pooled, wb, tmp):
    by, c = own.shape[1] - 2, own.shape[3]
    for i in range(3):
        for j in range(3):
            for k in range(3):
                wb[pl.ds((3 * i + j) * c, c), pl.ds(k * c, c)] = w[i, j, k]

    def plane(x, carry):
        hid, slope = fine_plane([own[x], own[x + 1], own[x + 2]], wb, bias, by)
        hidden[x], ds[x] = hid, slope
        return carry

    lax.fori_loop(0, hidden.shape[0], plane, 0)
    for q in range(pooled.shape[0]):
        pooled[q] = pool(hidden[2 * q + 1], hidden[2 * q + 2], tmp)


def outer_body(own, ra, rb, wb, bias, hid_in, pool_in, pg, hidden, ds, halo, pooled, out_a, out_b, tmp):
    bx, by = own.shape[0], own.shape[1] - 2
    cx = bx // 2
    xlo, xhi = get_faces(bit_of("grp") == 1, ra, rb)
    halo[0], halo[1] = xlo, xhi
    for at, three in ((0, [halo[0], own[0], own[1]]), (1, [own[bx - 2], own[bx - 1], halo[1]])):
        hidden[at], ds[at] = fine_plane(three, wb, bias, by)
    pooled[0] = pool(hidden[0], hid_in[0], tmp)
    pooled[1 : cx - 1] = pool_in[...]
    pooled[cx - 1] = pool(hid_in[bx - 3], hidden[1], tmp)
    low = jnp.concatenate([pooled[0:2], pg[0:1]], axis=0)
    high = jnp.concatenate([pooled[cx - 2 : cx], pg[cx - 1 : cx]], axis=0)
    put_faces(bit_of("grp") == 1, out_a, out_b, low, high)


def cubes_body(cot, pg, bits, tmp):
    bx, by, bz, c = cot.shape
    cx, cy, cz = bx // 2, by // 2, bz // 2
    total = jnp.sum(cot[...].astype(F32).reshape(cx, 2, cy, 2, bz, c), axis=(1, 3))
    grad = sum_cube(cx * cy * bz, total.reshape(cx * cy * bz, c), tmp).astype(BF16)
    pg[...] = grad.reshape(cx, cy, cz, c)
    first = grp_bits()
    for k in range(bits.shape[0]):
        value = bit_of("grp", k) if k < first else bit_of("sub", k - first)
        bits[k] = jnp.full(bits.shape[1:], value, jnp.int32)


def turn2_body(pooled, pg, ra, rb, out_a, out_b):
    cy = pooled.shape[1]
    xlo, xhi = get_faces(bit_of("grp") == 1, ra, rb)

    def side(y, last):
        two = [jnp.concatenate([xlo[0:2, at], pooled[:, at], xhi[0:2, at]], axis=0) for at in (y, y + 1)]
        one = jnp.concatenate([xlo[2:3, last], pg[:, last], xhi[2:3, last]], axis=0)
        return jnp.concatenate([*two, one], axis=0)

    put_faces(bit_of("sub") == 1, out_a, out_b, side(0, 0), side(cy - 2, cy - 1))


def reverse_bits(value, count):
    out = 0
    for _ in range(count):
        out, value = out * 2 + value % 2, value // 2
    return out


def spread(keep, send, n, blocks, piece):
    bits = n.bit_length() - 1
    half = n // 2
    for b in (0, 1):

        @pl.when(bit_of("sub") == b)
        def _():
            for s in range(n):
                target = keep if s % 2 == b else send
                for t in range(blocks):
                    value = piece(s, t)
                    size = value.shape[0]
                    target[reverse_bits(s, bits) % half, pl.ds(t * size, size)] = value


def coarse_body(
    n, pooled, ra, rb, ua, ub, pg, w, bias, wm,
    slope, coarse, keep, send, cbias, qpad, gpad, wb, st, rhs, acc, ct,
):
    cx, cy, cz, c = pooled.shape
    c2 = wm.shape[0]
    xlo, xhi = get_faces(bit_of("grp") == 1, ra, rb)
    ylo, yhi = get_faces(bit_of("sub") == 1, ua, ub)
    qpad[2 : cx + 2, 2 : cy + 2] = pooled[...]
    qpad[0:2, 2 : cy + 2] = xlo[0:2]
    qpad[cx + 2 : cx + 4, 2 : cy + 2] = xhi[0:2]
    wide = cx + 4
    for t in (0, 1):
        qpad[:, t] = ylo[t * wide : (t + 1) * wide]
        qpad[:, cy + 2 + t] = yhi[t * wide : (t + 1) * wide]
    gpad[1 : cx + 1, 1 : cy + 1] = pg[...]
    gpad[0, 1 : cy + 1] = xlo[2]
    gpad[cx + 1, 1 : cy + 1] = xhi[2]
    gpad[:, 0] = ylo[2 * wide :]
    gpad[:, cy + 1] = yhi[2 * wide :]
    for i in range(3):
        for j in range(3):
            for k in range(3):
                wb[pl.ds((3 * i + j) * c, c), pl.ds(k * c2, c2)] = w[i, j, k]
    wide = cy + 2
    rows = wide * cz

    def plane(x, carry):
        taps = [qpad[x + i, j : j + wide].reshape(rows, c) for i in range(3) for j in range(3)]
        part = jnp.dot(jnp.concatenate(taps, axis=1), wb[...], preferred_element_type=F32)
        pre = (
            part[:, c2 : 2 * c2]
            + shift_rows(part[:, :c2], 1, cz)
            + shift_rows(part[:, 2 * c2 :], -1, cz)
            + bias[...]
        )
        sig = sigmoid(pre)
        back = lax.dot_general(
            gpad[x].reshape(rows, c), wm[...], (((1,), (1,)), ((), ())), preferred_element_type=F32
        )
        slope[x] = (back * (sig * (1.0 + pre * (1.0 - sig)))).astype(BF16).reshape(wide, cz, c2)

        @pl.when((x >= 1) & (x <= cx))
        def _():
            coarse[x - 1] = (pre * sig).astype(BF16).reshape(wide, cz, c2)[1 : cy + 1]

        return carry

    lax.fori_loop(0, cx + 2, plane, 0)
    cells = cx * cy * cz
    mid = slope[1 : cx + 1, 1 : cy + 1].reshape(cells, c2)
    wide_mid = mid.astype(F32)
    st[pl.ds(0, c2), :] = shift_rows(wide_mid, -1, cz).astype(BF16).T
    st[pl.ds(c2, c2), :] = mid.T
    st[pl.ds(2 * c2, c2), :] = shift_rows(wide_mid, 1, cz).astype(BF16).T
    for i in range(3):
        for j in range(3):
            rhs[:, pl.ds((3 * i + j) * c, c)] = qpad[
                1 + i : 1 + i + cx, 1 + j : 1 + j + cy
            ].reshape(cells, c)
    rhs[:, pl.ds(9 * c, c)] = jnp.ones((cells, c), BF16)
    acc[...] = jnp.dot(st[...], rhs[...], preferred_element_type=F32).astype(BF16)
    ct[...] = jnp.dot(
        coarse[...].reshape(cells, c2).T, pg[...].reshape(cells, c), preferred_element_type=F32
    ).astype(BF16)
    cbias[...] = acc[pl.ds(c2, c2), pl.ds(9 * c, c)]
    per = c2 // n

    def piece(s, t):
        if t == 27:
            return ct[pl.ds(s * per, per), :]
        k, tap = t // 9, t % 9
        return acc[pl.ds(k * c2 + s * per, per), pl.ds(tap * c, c)]

    spread(keep, send, n, 28, piece)


def back_body(n, slope, w, cot, ds, ds_edge, own, halo, cbias, keep, send, up, st, rhs, acc):
    bx, by, bz, c = cot.shape
    cx, cy, cz = bx // 2, by // 2, bz // 2
    c2 = slope.shape[3]
    cells = cx * cy * cz
    total = jnp.zeros((cells, 3 * c), F32)
    for i in range(3):
        for j in range(3):
            tap = slope[2 - i : 2 - i + cx, 2 - j : 2 - j + cy].reshape(cells, c2)
            total = total + lax.dot_general(
                tap,
                w[i, j].reshape(3 * c, c2),
                (((1,), (1,)), ((), ())),
                preferred_element_type=F32,
            )
    pooled = (
        total[:, c : 2 * c]
        + shift_rows(total[:, :c], -1, cz)
        + shift_rows(total[:, 2 * c :], 1, cz)
    ) * 0.125
    up[pl.ds(0, cells, stride=2), :] = pooled
    up[pl.ds(1, cells, stride=2), :] = pooled
    rows = by * bz
    for x in range(bx):
        base = up[pl.ds((x // 2) * cy * bz, cy * bz), :].reshape(cy, 1, bz, c)
        fine = cot[x].astype(F32).reshape(cy, 2, bz, c) + base
        gain = ds[x - 1] if 0 < x < bx - 1 else ds_edge[x // (bx - 1)]
        fs = (fine.reshape(rows, c) * gain.reshape(rows, c)).astype(BF16)
        wide = fs.astype(F32)
        st[pl.ds(0, c), pl.ds(x * rows, rows)] = shift_rows(wide, -1, bz).astype(BF16).T
        st[pl.ds(c, c), pl.ds(x * rows, rows)] = fs.T
        st[pl.ds(2 * c, c), pl.ds(x * rows, rows)] = shift_rows(wide, 1, bz).astype(BF16).T
    voxels = bx * rows
    for t in range(0, 10, 2):
        for h in (0, 1):
            i, j = (t + h) // 3, (t + h) % 3
            if t + h == 9:
                rhs[:, pl.ds(h * c, c)] = jnp.ones((voxels, c), BF16)
            else:
                first, past = max(i - 1, 0), min(i - 1 + bx, bx)
                at = (first - i + 1) * rows
                size = (past - first) * rows
                rhs[pl.ds(at, size), pl.ds(h * c, c)] = own[first:past, j : j + by].reshape(size, c)
                if i != 1:
                    edge = halo[i // 2, j : j + by].reshape(rows, c)
                    rhs[pl.ds(0 if i == 0 else size, rows), pl.ds(h * c, c)] = edge
        acc[:, pl.ds(t * c, 2 * c)] = jnp.dot(
            st[...], rhs[...], preferred_element_type=F32
        ).astype(BF16)
    per, cper = c // n, c2 // n
    lane = lax.broadcasted_iota(jnp.int32, (per, c), 1)

    def piece(s, t):
        if t == 27:
            bias = acc[pl.ds(c + s * per, per), pl.ds(9 * c, c)].astype(F32)
            one = cbias[pl.ds(s * cper, per), :].astype(F32)
            two = cbias[pl.ds(s * cper + per, per), :].astype(F32)
            return jnp.where(lane == 0, bias, jnp.where(lane == 1, one, two)).astype(BF16)
        k, tap = t // 9, t % 9
        return acc[pl.ds(k * c + s * per, per), pl.ds(tap * c, c)]

    spread(keep, send, n, 28, piece)


def merge_body(hidden, hid_edge, coarse, wm, out, tmp):
    bx, by, bz, c = out.shape
    cx, cy, cz = bx // 2, by // 2, bz // 2
    c2 = coarse.shape[3]
    cells = cx * cy * cz
    proj = jnp.dot(coarse[...].reshape(cells, c2), wm[...], preferred_element_type=F32)
    tmp[pl.ds(0, cells, stride=2), :] = proj
    tmp[pl.ds(1, cells, stride=2), :] = proj
    for x in range(bx):
        base = tmp[pl.ds((x // 2) * cy * bz, cy * bz), :].reshape(cy, 1, bz, c)
        hid = hidden[x - 1] if 0 < x < bx - 1 else hid_edge[x // (bx - 1)]
        total = hid.astype(F32).reshape(cy, 2, bz, c) + base
        out[x] = total.astype(BF16).reshape(by, bz, c)


def swap_faces(first, second, axis):
    n = lax.axis_size(axis)
    one = [p for i in range(0, n - 1, 2) for p in ((i, i + 1), (i + 1, i))]
    two = [p for i in range(1, n - 1, 2) for p in ((i, i + 1), (i + 1, i))]
    got = lax.ppermute(second, axis, two)
    return lax.ppermute(first, axis, one), got


def split4_body(keep, got, own, over_sub, over_grp, over_both):
    g, s = bit_of("grp"), bit_of("sub", 1)

    def part(a, b):
        return (keep[a, :, b].astype(F32) + got[a, :, b].astype(F32)).astype(BF16)

    over_both[...] = part(1 - s, 1 - g)
    over_sub[...] = part(1 - s, g)
    over_grp[...] = part(s, 1 - g)
    own[...] = part(s, g)


def total_of(parts):
    return sum(p.astype(F32) for p in parts).astype(BF16)


def halves(pair, bit):
    return jnp.where(bit == 1, pair[1], pair[0]), jnp.where(bit == 1, pair[0], pair[1])


def partners(value, grp_mask, sub_mask):
    n_grp, n_sub = lax.axis_size("grp"), lax.axis_size("sub")
    pairs = [
        (g * n_sub + s, (g ^ grp_mask) * n_sub + (s ^ sub_mask))
        for g in range(n_grp)
        for s in range(n_sub)
    ]
    return lax.ppermute(value, ("grp", "sub"), pairs)


def split_sum(parts, bit):
    rows, c = parts[0].shape
    return halves(total_of([p.reshape(2, rows // 2, c) for p in parts]), bit)


def grp_bits():
    return lax.axis_size("grp").bit_length() - 1


def cores(send):
    return partners(send, 0, 1)


def spread_sum(keep, got):
    half, rows, c = keep.shape
    rest = half // 2
    shape = (2, rest, 2, rows // 2, c)
    out = ((rest, rows // 2, c), BF16)
    return call(split4_body, "split", (keep.reshape(shape), got.reshape(shape)), [out] * 4, (), 1)


def cross(own, over_sub, over_grp, over_both):
    return [own, partners(over_both, 1, 2), partners(over_sub, 0, 2), partners(over_grp, 1, 0)]


def split_body(count, axis, bit, *refs):
    mine = bit_of(axis, bit)

    def part(at):
        return sum(p[at].astype(F32) for p in refs[:count]).astype(BF16)

    refs[count + 1][...] = part(1 - mine)
    refs[count][...] = part(mine)


def sum_body(count, *refs):
    refs[count][...] = sum(p[...].astype(F32) for p in refs[:count]).astype(BF16)


def split_sum_kernel(parts, axis, bit, name):
    rows, c = parts[0].shape
    half = ((rows // 2, c), BF16)
    shaped = [p.reshape(2, rows // 2, c) for p in parts]
    return call(functools.partial(split_body, len(parts), axis, bit), name, shaped, [half, half], (), 0.8)


def sum_kernel(parts, name):
    out = [(parts[0].shape, BF16)]
    return call(functools.partial(sum_body, len(parts)), name, parts, out, (), 0.5)[0]


def finish_sum(parts, places, name, kernels):
    rest, rows, c = parts[0].shape
    parts = [p.reshape(rest * rows, c) for p in parts]
    for bit in range(2, lax.axis_size("sub").bit_length() - 1):
        keep, send = split_sum(parts, places[grp_bits() + bit])
        parts = [keep, partners(send, 0, 1 << bit)]
    bits = [0]
    last = grp_bits() - 1
    for bit in range(1, last + 1):
        mask = 1 << bit
        if bit == 1 and bit < last and parts[0].shape[0] % 32 == 0:
            if "half" in kernels:
                keep, send = split_sum_kernel(parts, "grp", bit, name + "_half")
            else:
                keep, send = split_sum(parts, places[bit])
            parts = [keep, partners(send, mask, 0)]
            bits.append(bit)
        else:
            total = sum_kernel(parts, name + "_sum") if "sum" in kernels else total_of(parts)
            parts = [total, partners(total, mask, 0)]
    total = sum_kernel(parts, name + "_total") if "total" in kernels else total_of(parts)
    pieces = [total]
    for which in range(1, 2 ** len(bits)):
        pieces.append(partners(total, sum(1 << bits[b] for b in range(len(bits)) if which >> b & 1), 0))
    return pieces


def last_body(count, *refs):
    pieces, kernel, extra, rows = refs[:count], refs[count], refs[count + 1], refs[-1]
    size = pieces[0].shape[0]
    per = extra.shape[0] if len(refs) == count + 3 else kernel.shape[3]
    mine = bit_of("grp") if count == 2 else 2 * bit_of("grp") + bit_of("grp", 1)
    for which in range(count):
        mask = which if count == 2 else 2 * (which & 1) + (which >> 1)
        rows[mine ^ mask] = pieces[which][...]

    def block(t):
        at, off = t * per // size, t * per % size
        if off + per <= size:
            return rows[at, pl.ds(off, per)].astype(F32)
        first = size - off
        return jnp.concatenate([rows[at, pl.ds(off, first)], rows[at + 1, pl.ds(0, per - first)]], axis=0).astype(F32)

    for t in range(27):
        kernel[(t // 3) % 3, t % 3, t // 9] = block(t)
    if len(refs) == count + 3:
        extra[...] = block(27)
    else:
        turned = block(27).T
        extra[...] = turned[0:1]
        refs[count + 2][:, pl.ds(0, per)] = turned[1:2]
        refs[count + 2][:, pl.ds(per, per)] = turned[2:3]


def last(pieces, per, outs, name):
    count = len(pieces)
    size, c = pieces[0].shape
    kernel, *rest = call(
        functools.partial(last_body, count),
        name,
        tuple(pieces),
        [((3, 3, 3, per, c), F32), *outs],
        [pltpu.VMEM((count, size, c), BF16)],
        1,
    )
    return jnp.swapaxes(kernel, 3, 4), *rest


def per_device(field, cotangent, fine_kernel, fine_bias, coarse_kernel, coarse_bias, merge_weight):
    n = lax.axis_size("sub")
    bx, by, bz, c = field.shape
    cx, cy, cz = bx // 2, by // 2, bz // 2
    c2 = merge_weight.shape[0]
    odd = bit_of("sub") == 1
    sa = jnp.where(odd, field[:, 0], field[:, by - 1])
    sb = jnp.where(odd, field[:, by - 1], field[:, 0])
    ya, yb = swap_faces(sa, sb, "sub")
    count = grp_bits() + n.bit_length() - 1
    pg, places = call(
        cubes_body,
        "cubes",
        (cotangent,),
        [((cx, cy, cz, c), BF16), ((count, 1, c), jnp.int32)],
        [pltpu.VMEM((cx * cy * bz, c), F32)],
    )
    face = ((by + 2, bz, c), BF16)
    own, ta, tb = call(
        turn_body,
        "turn",
        (field, ya, yb),
        [((bx, by + 2, bz, c), BF16), face, face],
    )
    xa, xb = swap_faces(ta, tb, "grp")
    bias = fine_bias.reshape(1, c)
    hidden, ds, pooled, wb = call(
        inner_body,
        "inner",
        (own, fine_kernel, bias),
        [
            ((bx - 2, by, bz, c), BF16),
            ((bx - 2, by, bz, c), F32),
            ((cx - 2, cy, cz, c), BF16),
            ((9 * c, 3 * c), BF16),
        ],
        [pltpu.VMEM((cy * bz, c), F32)],
        6,
    )
    face = ((3, cy, cz, c), BF16)
    hid_edge, ds_edge, halo, pooled, pa, pb = call(
        outer_body,
        "outer",
        (own, xa, xb, wb, bias, hidden, pooled, pg),
        [
            ((2, by, bz, c), BF16),
            ((2, by, bz, c), F32),
            ((2, by + 2, bz, c), BF16),
            ((cx, cy, cz, c), BF16),
            face,
            face,
        ],
        [pltpu.VMEM((cy * bz, c), F32)],
        2,
    )
    pxa, pxb = swap_faces(pa, pb, "grp")
    face = ((2 * (cx + 4) + cx + 2, cz, c), BF16)
    qa, qb = call(turn2_body, "turn2", (pooled, pg, pxa, pxb), [face, face])
    pya, pyb = swap_faces(qa, qb, "sub")
    cells = cx * cy * cz
    part = (n // 2, 28 * (c2 // n), c)
    slope, coarse, ckeep, csend, cbias = call(
        functools.partial(coarse_body, n),
        "coarse",
        (pooled, pxa, pxb, pya, pyb, pg, coarse_kernel, coarse_bias.reshape(1, c2), merge_weight),
        [
            ((cx + 2, cy + 2, cz, c2), BF16),
            ((cx, cy, cz, c2), BF16),
            (part, BF16),
            (part, BF16),
            ((c2, c), BF16),
        ],
        [
            pltpu.VMEM((cx + 4, cy + 4, cz, c), BF16),
            pltpu.VMEM((cx + 2, cy + 2, cz, c), BF16),
            pltpu.VMEM((9 * c, 3 * c2), BF16),
            pltpu.VMEM((3 * c2, cells), BF16),
            pltpu.VMEM((cells, 10 * c), BF16),
            pltpu.VMEM((3 * c2, 10 * c), BF16),
            pltpu.VMEM((c2, c), BF16),
        ],
        6,
    )
    cgot = cores(csend)
    (output,) = call(
        merge_body,
        "merge",
        (hidden, hid_edge, coarse, merge_weight),
        [((bx, by, bz, c), BF16)],
        [pltpu.VMEM((cx * cy * bz, c), F32)],
        2,
    )
    output, cgot = lax.optimization_barrier((output, cgot))
    csent = spread_sum(ckeep, cgot)
    slope, csent = lax.optimization_barrier((slope, csent))
    cparts = cross(*csent)
    voxels = bx * by * bz
    part = (n // 2, 28 * (c // n), c)
    fkeep, fsend = call(
        functools.partial(back_body, n),
        "back",
        (slope, coarse_kernel, cotangent, ds, ds_edge, own, halo, cbias),
        [(part, BF16), (part, BF16)],
        [
            pltpu.VMEM((cx * cy * bz, c), F32),
            pltpu.VMEM((3 * c, voxels), BF16),
            pltpu.VMEM((voxels, 2 * c), BF16),
            pltpu.VMEM((3 * c, 10 * c), BF16),
        ],
        10,
    )
    fsend, cparts = lax.optimization_barrier((fsend, cparts))
    fgot = cores(fsend)
    fparts = cross(*spread_sum(fkeep, fgot))
    coarse_sum = finish_sum(cparts, places, "coarse", ('half', 'sum'))
    fine_sum = finish_sum(fparts, places, "fine", ('half', 'sum'))
    per, cper = c // n, c2 // n
    grad_coarse, grad_merge = last(coarse_sum, cper, [((cper, c), F32)], "coarse_last")
    biases = [((1, per), F32), ((1, cper), F32)]
    grad_fine, bias, coarse_sums = last(fine_sum, per, biases, "fine_last")
    return (output, grad_fine, bias[0], grad_coarse, coarse_sums[0], grad_merge)


def solution(mesh):
    in_specs = (P("grp", "sub", None, None), P("grp", "sub", None, None), P(), P(), P(), P(), P())
    out_specs = (
        P("grp", "sub", None, None),
        P(None, None, None, None, "sub"),
        P("sub"),
        P(None, None, None, None, "sub"),
        P("sub"),
        P("sub", None),
    )
    return jax.shard_map(
        per_device, mesh=mesh, in_specs=in_specs, out_specs=out_specs, check_vma=False
    )
```

```python
import functools

import jax
import jax.numpy as jnp
from jax import lax
from jax.experimental import pallas as pl
from jax.experimental.pallas import tpu as pltpu
from jax.sharding import PartitionSpec as P

F32 = jnp.float32
BF16 = jnp.bfloat16
VMEM_LIMIT = 32 * 1024 * 1024


def bit_of(axis, bit=0):
    return (lax.axis_index(axis) >> bit) & 1


def call(body, name, args, outs, scratch=(), micros=1):
    return pl.pallas_call(
        body,
        name=name,
        out_shape=[jax.ShapeDtypeStruct(s, t) for s, t in outs],
        in_specs=[pl.BlockSpec(memory_space=pltpu.VMEM) for _ in args],
        out_specs=[pl.BlockSpec(memory_space=pltpu.VMEM) for _ in outs],
        scratch_shapes=list(scratch),
        compiler_params=pltpu.CompilerParams(vmem_limit_bytes=VMEM_LIMIT),
        cost_estimate=pl.CostEstimate(
            flops=int(micros * 1e9), bytes_accessed=0, transcendentals=0
        ),
    )(*args)


def put_faces(odd, first, second, low, high):
    first[...] = jnp.where(odd, low, high)
    second[...] = jnp.where(odd, high, low)


def get_faces(odd, first, second):
    a, b = first[...], second[...]
    return jnp.where(odd, a, b), jnp.where(odd, b, a)


def sum_cube(rows, planes, ref):
    half = rows // 2
    ref[pl.ds(0, rows), :] = planes
    return ref[pl.ds(0, half, stride=2), :] + ref[pl.ds(1, half, stride=2), :]


def shift_rows(value, step, depth):
    rows = value.shape[0]
    moved = pltpu.roll(value, step % rows, 0)
    place = lax.broadcasted_iota(jnp.int32, value.shape, 0) % depth
    edge = 0 if step == 1 else depth - 1
    return jnp.where(place == edge, 0.0, moved)


def sigmoid(value):
    return 1.0 / (1.0 + jnp.exp(-value))


def turn_body(field, ya, yb, pg, own, out_a, out_b):
    bx, by, bz, c = field.shape
    cx, cy, cz, _ = pg.shape
    ylo, yhi = get_faces(bit_of("sub") == 1, ya, yb)
    own[:, 1 : by + 1] = field[...]
    own[:, 0] = ylo
    own[:, by + 1] = yhi

    def side(x, at):
        return jnp.concatenate([own[x].reshape((by + 2) * bz, c), pg[at].reshape(cy * cz, c)], axis=0)

    put_faces(bit_of("grp") == 1, out_a, out_b, side(0, 0), side(bx - 1, cx - 1))


def x_faces(xa, xb, fine, coarse):
    by, bz, c = fine
    cy, cz, _ = coarse
    lo, hi = get_faces(bit_of("grp") == 1, xa, xb)
    rows = by * bz
    return (
        (lo[:rows].reshape(by, bz, c), hi[:rows].reshape(by, bz, c)),
        (lo[rows:].reshape(cy, cz, c), hi[rows:].reshape(cy, cz, c)),
    )


def fine_plane(three, wb, bias, by):
    _, bz, c = three[0].shape
    rows = by * bz * (len(three) - 2)
    taps = [
        jnp.concatenate([plane[j : j + by].reshape(by * bz, c) for plane in three[i : len(three) - 2 + i]], axis=0)
        for i in range(3)
        for j in range(3)
    ]
    part = jnp.dot(jnp.concatenate(taps, axis=1), wb[...], preferred_element_type=F32)
    pre = (
        part[:, c : 2 * c]
        + shift_rows(part[:, :c], 1, bz)
        + shift_rows(part[:, 2 * c :], -1, bz)
        + bias[...]
    )
    sig = sigmoid(pre)
    hid = (pre * sig).astype(BF16).reshape(-1, by, bz, c)
    return hid, (sig * (1.0 + pre * (1.0 - sig))).reshape(-1, by, bz, c)


def pool(one, two, tmp):
    by, bz, c = one.shape
    cy = by // 2
    both = jnp.sum((one.astype(F32) + two.astype(F32)).reshape(cy, 2, bz, c), axis=1)
    total = sum_cube(cy * bz, both.reshape(cy * bz, c), tmp)
    return (total / 8.0).astype(BF16).reshape(cy, bz // 2, c)


def inner_body(own, w, bias, hidden, ds, pooled, wb, tmp):
    by, c = own.shape[1] - 2, own.shape[3]
    for i in range(3):
        for j in range(3):
            for k in range(3):
                wb[pl.ds((3 * i + j) * c, c), pl.ds(k * c, c)] = w[i, j, k]

    def plane(x, carry):
        hid, slope = fine_plane([own[3 * x + k] for k in range(5)], wb, bias, by)
        hidden[pl.ds(3 * x, 3)], ds[pl.ds(3 * x, 3)] = hid, slope
        return carry

    lax.fori_loop(0, hidden.shape[0] // 3, plane, 0)
    for q in range(pooled.shape[0]):
        pooled[q] = pool(hidden[2 * q + 1], hidden[2 * q + 2], tmp)


def edge_body(second, own, face, wb, bias, hid_in, pool_in, hidden, ds, pooled, out, tmp):
    bx, by, bz, c = own.shape
    cx = bx // 2
    low = bit_of("grp") == (0 if second else 1)
    halo = face[pl.ds(0, by * bz), :].reshape(by, bz, c)
    near, inside = own[jnp.where(low, 0, bx - 1)], own[jnp.where(low, 1, bx - 2)]
    three = [jnp.where(low, halo, inside), near, jnp.where(low, inside, halo)]
    hid, slope = fine_plane(three, wb, bias, by - 2)
    hidden[...], ds[...] = hid[0], slope[0]
    pooled[...] = pool(hidden[...], hid_in[jnp.where(low, 0, bx - 3)], tmp)
    out[0] = jnp.where(low, pooled[...], pool_in[cx - 3])
    out[1] = jnp.where(low, pool_in[0], pooled[...])


def taps_body(w, wb):
    c, c2 = w.shape[3], w.shape[4]
    for i in range(3):
        for j in range(3):
            for k in range(3):
                wb[pl.ds((3 * i + j) * c, c), pl.ds(k * c2, c2)] = w[i, j, k]


def cubes_body(cot, pg, bits, tmp):
    bx, by, bz, c = cot.shape
    cx, cy, cz = bx // 2, by // 2, bz // 2
    total = jnp.sum(cot[...].astype(F32).reshape(cx, 2, cy, 2, bz, c), axis=(1, 3))
    grad = sum_cube(cx * cy * bz, total.reshape(cx * cy * bz, c), tmp).astype(BF16)
    pg[...] = grad.reshape(cx, cy, cz, c)
    first = grp_bits()
    for k in range(bits.shape[0]):
        value = bit_of("grp", k) if k < first else bit_of("sub", k - first)
        bits[k] = jnp.full(bits.shape[1:], value, jnp.int32)


def pooled_of(pool_in, pool_a, pool_b):
    lo, hi = get_faces(bit_of("grp") == 1, pool_a, pool_b)
    return jnp.concatenate([lo[None], pool_in[...], hi[None]], axis=0)


def turn2_body(pool_in, pool_a, pool_b, pg, ra, rb, xa, xb, out_a, out_b):
    cy, cz, c = pool_a.shape
    pooled = pooled_of(pool_in, pool_a, pool_b)
    xlo, xhi = get_faces(bit_of("grp") == 1, ra, rb)
    _, (glo, ghi) = x_faces(xa, xb, (2 * cy + 2, 2 * cz, c), (cy, cz, c))

    def side(y, last):
        two = [jnp.concatenate([xlo[:, at], pooled[:, at], xhi[:, at]], axis=0) for at in (y, y + 1)]
        one = jnp.concatenate([glo[None, last], pg[:, last], ghi[None, last]], axis=0)
        return jnp.concatenate([*two, one], axis=0)

    put_faces(bit_of("sub") == 1, out_a, out_b, side(0, 0), side(cy - 2, cy - 1))


def reverse_bits(value, count):
    out = 0
    for _ in range(count):
        out, value = out * 2 + value % 2, value // 2
    return out


def spread(keep, send, n, blocks, piece):
    bits = n.bit_length() - 1
    half = n // 2
    for b in (0, 1):

        @pl.when(bit_of("sub") == b)
        def _():
            for s in range(n):
                target = keep if s % 2 == b else send
                for t in range(blocks):
                    value = piece(s, t)
                    size = value.shape[0]
                    target[reverse_bits(s, bits) % half, pl.ds(t * size, size)] = value


def coarse_part(taps, grads, wb, bias, wm, cz):
    c2 = wm.shape[0]
    part = jnp.dot(jnp.concatenate(taps, axis=1), wb[...], preferred_element_type=F32)
    pre = (
        part[:, c2 : 2 * c2]
        + shift_rows(part[:, :c2], 1, cz)
        + shift_rows(part[:, 2 * c2 :], -1, cz)
        + bias[...]
    )
    sig = sigmoid(pre)
    back = lax.dot_general(grads, wm[...], (((1,), (1,)), ((), ())), preferred_element_type=F32)
    return (back * (sig * (1.0 + pre * (1.0 - sig)))).astype(BF16), (pre * sig).astype(BF16)


def mid_body(pool_in, pool_a, pool_b, ra, rb, xa, xb, pg, wb, bias, wm, slope, coarse, qx, gx):
    cx, cy, cz, c = pg.shape
    c2 = wm.shape[0]
    qx[0:2], qx[cx + 2 : cx + 4] = get_faces(bit_of("grp") == 1, ra, rb)
    qx[2 : cx + 2] = pooled_of(pool_in, pool_a, pool_b)
    _, (gx[0], gx[cx + 1]) = x_faces(xa, xb, (2 * cy + 2, 2 * cz, c), (cy, cz, c))
    gx[1 : cx + 1] = pg[...]
    for first in range(0, cx + 2, 3):
        planes = range(first, first + 3)
        taps = [
            jnp.concatenate([qx[x + i, j : j + cy - 2].reshape(-1, c) for x in planes], axis=0)
            for i in range(3)
            for j in range(3)
        ]
        grads = jnp.concatenate([gx[x, 1 : cy - 1].reshape(-1, c) for x in planes], axis=0)
        out, act = coarse_part(taps, grads, wb, bias, wm, cz)
        slope[first : first + 3] = out.reshape(3, cy - 2, cz, c2)
        act = act.reshape(3, cy - 2, cz, c2)
        for h, x in enumerate(planes):
            if 1 <= x <= cx:
                coarse[x - 1] = act[h]


def coarse_body(
    n, pool_in, pool_a, pool_b, ra, rb, ua, ub, xa, xb, pg, wb, bias, wm, slope_mid, coarse_mid,
    slope, coarse, keep, send, cbias, qpad, gpad, st, rhs, acc, ct,
):
    cx, cy, cz, c = pg.shape
    c2 = wm.shape[0]
    xlo, xhi = get_faces(bit_of("grp") == 1, ra, rb)
    ylo, yhi = get_faces(bit_of("sub") == 1, ua, ub)
    qpad[2 : cx + 2, 2 : cy + 2] = pooled_of(pool_in, pool_a, pool_b)
    qpad[0:2, 2 : cy + 2] = xlo
    qpad[cx + 2 : cx + 4, 2 : cy + 2] = xhi
    wide = cx + 4
    for t in (0, 1):
        qpad[:, t] = ylo[t * wide : (t + 1) * wide]
        qpad[:, cy + 2 + t] = yhi[t * wide : (t + 1) * wide]
    gpad[1 : cx + 1, 1 : cy + 1] = pg[...]
    _, (glo, ghi) = x_faces(xa, xb, (2 * cy + 2, 2 * cz, c), (cy, cz, c))
    gpad[0, 1 : cy + 1] = glo
    gpad[cx + 1, 1 : cy + 1] = ghi
    gpad[:, 0] = ylo[2 * wide :]
    gpad[:, cy + 1] = yhi[2 * wide :]
    def both(ref, x, j):
        return jnp.concatenate([ref[x, j : j + 2], ref[x, cy + j : cy + 2 + j]], axis=0).reshape(4 * cz, -1)

    planes = range(cx + 2)
    taps = [
        jnp.concatenate([both(qpad, x + i, j) for x in planes], axis=0) for i in range(3) for j in range(3)
    ]
    grads = jnp.concatenate([both(gpad, x, 0) for x in planes], axis=0)
    out, act = coarse_part(taps, grads, wb, bias, wm, cz)
    out, act = (v.reshape(cx + 2, 4, cz, c2) for v in (out, act))
    slope[:, 0:2] = out[:, 0:2]
    slope[:, cy : cy + 2] = out[:, 2:4]
    slope[:, 2:cy] = slope_mid[...]
    coarse[:, 0] = act[1 : cx + 1, 1]
    coarse[:, cy - 1] = act[1 : cx + 1, 2]
    coarse[:, 1 : cy - 1] = coarse_mid[...]
    cells = cx * cy * cz
    mid = slope[1 : cx + 1, 1 : cy + 1].reshape(cells, c2)
    wide_mid = mid.astype(F32)
    st[pl.ds(0, c2), :] = shift_rows(wide_mid, -1, cz).astype(BF16).T
    st[pl.ds(c2, c2), :] = mid.T
    st[pl.ds(2 * c2, c2), :] = shift_rows(wide_mid, 1, cz).astype(BF16).T
    for i in range(3):
        for j in range(3):
            rhs[:, pl.ds((3 * i + j) * c, c)] = qpad[
                1 + i : 1 + i + cx, 1 + j : 1 + j + cy
            ].reshape(cells, c)
    rhs[:, pl.ds(9 * c, c)] = jnp.ones((cells, c), BF16)
    acc[...] = jnp.dot(st[...], rhs[...], preferred_element_type=F32).astype(BF16)
    ct[...] = jnp.dot(
        coarse[...].reshape(cells, c2).T, pg[...].reshape(cells, c), preferred_element_type=F32
    ).astype(BF16)
    cbias[...] = acc[pl.ds(c2, c2), pl.ds(9 * c, c)]
    per = c2 // n

    def piece(s, t):
        if t == 27:
            return ct[pl.ds(s * per, per), :]
        k, tap = t // 9, t % 9
        return acc[pl.ds(k * c2 + s * per, per), pl.ds(tap * c, c)]

    spread(keep, send, n, 28, piece)


def back_body(n, slope, w, cot, ds, ds_a, ds_b, own, xa, xb, cbias, keep, send, up, st, rhs, acc):
    bx, by, bz, c = cot.shape
    cx, cy, cz = bx // 2, by // 2, bz // 2
    c2 = slope.shape[3]
    cells = cx * cy * cz
    total = jnp.zeros((cells, 3 * c), F32)
    for i in range(3):
        for j in range(3):
            tap = slope[2 - i : 2 - i + cx, 2 - j : 2 - j + cy].reshape(cells, c2)
            total = total + lax.dot_general(
                tap,
                w[i, j].reshape(3 * c, c2),
                (((1,), (1,)), ((), ())),
                preferred_element_type=F32,
            )
    pooled = (
        total[:, c : 2 * c]
        + shift_rows(total[:, :c], -1, cz)
        + shift_rows(total[:, 2 * c :], 1, cz)
    ) * 0.125
    up[pl.ds(0, cells, stride=2), :] = pooled
    up[pl.ds(1, cells, stride=2), :] = pooled
    rows = by * bz
    edges = get_faces(bit_of("grp") == 1, ds_a, ds_b)
    halo, _ = x_faces(xa, xb, (by + 2, bz, c), (cy, cz, c))
    for x in range(bx):
        base = up[pl.ds((x // 2) * cy * bz, cy * bz), :].reshape(cy, 1, bz, c)
        fine = cot[x].astype(F32).reshape(cy, 2, bz, c) + base
        gain = ds[x - 1] if 0 < x < bx - 1 else edges[x // (bx - 1)]
        fs = (fine.reshape(rows, c) * gain.reshape(rows, c)).astype(BF16)
        wide = fs.astype(F32)
        st[pl.ds(0, c), pl.ds(x * rows, rows)] = shift_rows(wide, -1, bz).astype(BF16).T
        st[pl.ds(c, c), pl.ds(x * rows, rows)] = fs.T
        st[pl.ds(2 * c, c), pl.ds(x * rows, rows)] = shift_rows(wide, 1, bz).astype(BF16).T
    voxels = bx * rows
    for t in range(0, 10, 2):
        for h in (0, 1):
            i, j = (t + h) // 3, (t + h) % 3
            if t + h == 9:
                rhs[:, pl.ds(h * c, c)] = jnp.ones((voxels, c), BF16)
            else:
                first, past = max(i - 1, 0), min(i - 1 + bx, bx)
                at = (first - i + 1) * rows
                size = (past - first) * rows
                rhs[pl.ds(at, size), pl.ds(h * c, c)] = own[first:past, j : j + by].reshape(size, c)
                if i != 1:
                    edge = halo[i // 2][j : j + by].reshape(rows, c)
                    rhs[pl.ds(0 if i == 0 else size, rows), pl.ds(h * c, c)] = edge
        acc[:, pl.ds(t * c, 2 * c)] = jnp.dot(
            st[...], rhs[...], preferred_element_type=F32
        ).astype(BF16)
    per, cper = c // n, c2 // n
    lane = lax.broadcasted_iota(jnp.int32, (per, c), 1)

    def piece(s, t):
        if t == 27:
            bias = acc[pl.ds(c + s * per, per), pl.ds(9 * c, c)].astype(F32)
            one = cbias[pl.ds(s * cper, per), :].astype(F32)
            two = cbias[pl.ds(s * cper + per, per), :].astype(F32)
            return jnp.where(lane == 0, bias, jnp.where(lane == 1, one, two)).astype(BF16)
        k, tap = t // 9, t % 9
        return acc[pl.ds(k * c + s * per, per), pl.ds(tap * c, c)]

    spread(keep, send, n, 28, piece)


def merge_body(hidden, hid_a, hid_b, coarse, wm, out, tmp):
    bx, by, bz, c = out.shape
    cx, cy, cz = bx // 2, by // 2, bz // 2
    c2 = coarse.shape[3]
    cells = cx * cy * cz
    proj = jnp.dot(coarse[...].reshape(cells, c2), wm[...], preferred_element_type=F32)
    tmp[pl.ds(0, cells, stride=2), :] = proj
    tmp[pl.ds(1, cells, stride=2), :] = proj
    edges = get_faces(bit_of("grp") == 1, hid_a, hid_b)
    for x in range(bx):
        base = tmp[pl.ds((x // 2) * cy * bz, cy * bz), :].reshape(cy, 1, bz, c)
        hid = hidden[x - 1] if 0 < x < bx - 1 else edges[x // (bx - 1)]
        total = hid.astype(F32).reshape(cy, 2, bz, c) + base
        out[x] = total.astype(BF16).reshape(by, bz, c)


def swap_faces(first, second, axis):
    n = lax.axis_size(axis)
    one = [p for i in range(0, n - 1, 2) for p in ((i, i + 1), (i + 1, i))]
    two = [p for i in range(1, n - 1, 2) for p in ((i, i + 1), (i + 1, i))]
    got = lax.ppermute(second, axis, two)
    return lax.ppermute(first, axis, one), got


def split4_body(keep, got, own, over_sub, over_grp, over_both):
    g, s = bit_of("grp"), bit_of("sub", 1)

    def part(a, b):
        return (keep[a, :, b].astype(F32) + got[a, :, b].astype(F32)).astype(BF16)

    over_both[...] = part(1 - s, 1 - g)
    over_sub[...] = part(1 - s, g)
    over_grp[...] = part(s, 1 - g)
    own[...] = part(s, g)


def total_of(parts):
    return sum(p.astype(F32) for p in parts).astype(BF16)


def halves(pair, bit):
    return jnp.where(bit == 1, pair[1], pair[0]), jnp.where(bit == 1, pair[0], pair[1])


def partners(value, grp_mask, sub_mask):
    n_grp, n_sub = lax.axis_size("grp"), lax.axis_size("sub")
    pairs = [
        (g * n_sub + s, (g ^ grp_mask) * n_sub + (s ^ sub_mask))
        for g in range(n_grp)
        for s in range(n_sub)
    ]
    return lax.ppermute(value, ("grp", "sub"), pairs)


def split_sum(parts, bit):
    rows, c = parts[0].shape
    return halves(total_of([p.reshape(2, rows // 2, c) for p in parts]), bit)


def grp_bits():
    return lax.axis_size("grp").bit_length() - 1


def cores(send):
    return partners(send, 0, 1)


def spread_sum(keep, got):
    half, rows, c = keep.shape
    rest = half // 2
    shape = (2, rest, 2, rows // 2, c)
    out = ((rest, rows // 2, c), BF16)
    return call(split4_body, "split", (keep.reshape(shape), got.reshape(shape)), [out] * 4, (), 1)


def cross(own, over_sub, over_grp, over_both):
    return [own, partners(over_both, 1, 2), partners(over_sub, 0, 2), partners(over_grp, 1, 0)]


def split_body(count, axis, bit, *refs):
    mine = bit_of(axis, bit)

    def part(at):
        return sum(p[at].astype(F32) for p in refs[:count]).astype(BF16)

    refs[count + 1][...] = part(1 - mine)
    refs[count][...] = part(mine)


def sum_body(count, *refs):
    refs[count][...] = sum(p[...].astype(F32) for p in refs[:count]).astype(BF16)


def split_sum_kernel(parts, axis, bit, name):
    rows, c = parts[0].shape
    half = ((rows // 2, c), BF16)
    shaped = [p.reshape(2, rows // 2, c) for p in parts]
    return call(functools.partial(split_body, len(parts), axis, bit), name, shaped, [half, half], (), 0.8)


def sum_kernel(parts, name):
    out = [(parts[0].shape, BF16)]
    return call(functools.partial(sum_body, len(parts)), name, parts, out, (), 0.5)[0]


def finish_sum(parts, places, name, kernels):
    rest, rows, c = parts[0].shape
    parts = [p.reshape(rest * rows, c) for p in parts]
    for bit in range(2, lax.axis_size("sub").bit_length() - 1):
        keep, send = split_sum(parts, places[grp_bits() + bit])
        parts = [keep, partners(send, 0, 1 << bit)]
    parts = yield parts
    bits = [0]
    last = grp_bits() - 1
    for bit in range(1, last + 1):
        mask = 1 << bit
        if bit == 1 and bit < last and parts[0].shape[0] % 32 == 0:
            if "half" in kernels:
                keep, send = split_sum_kernel(parts, "grp", bit, name + "_half")
            else:
                keep, send = split_sum(parts, places[bit])
            keep, send = yield keep, send
            parts = yield keep, partners(send, mask, 0)
            bits.append(bit)
        else:
            total = sum_kernel(parts, name + "_sum") if "sum" in kernels else total_of(parts)
            total = yield total
            parts = yield total, partners(total, mask, 0)
    total = sum_kernel(parts, name + "_total") if "total" in kernels else total_of(parts)
    pieces = [total]
    for which in range(1, 2 ** len(bits)):
        pieces.append(partners(total, sum(1 << bits[b] for b in range(len(bits)) if which >> b & 1), 0))
    return pieces


def step(run, value):
    try:
        return run.send(value), None
    except StopIteration as done:
        return None, done.value


def side_by_side(ahead, behind, arrived):
    first, first_done = step(ahead, step(ahead, None)[0])
    first, arrived = lax.optimization_barrier((first, arrived))
    first, first_done = step(ahead, first)
    behind = behind(arrived)
    second, second_done = step(behind, None)
    while second_done is None:
        if first_done is None:
            first, first_done = step(ahead, first)
        if first_done is None:
            first, first_done = step(ahead, first)
        second, second_done = step(behind, second)
        if second_done is None:
            second, second_done = step(behind, second)
            if first_done is None and second_done is None:
                first, second = lax.optimization_barrier((first, second))
    return first_done, second_done


def last_body(count, *refs):
    pieces, kernel, extra, rows = refs[:count], refs[count], refs[count + 1], refs[-1]
    size = pieces[0].shape[0]
    per = extra.shape[0] if len(refs) == count + 3 else kernel.shape[3]
    mine = bit_of("grp") if count == 2 else 2 * bit_of("grp") + bit_of("grp", 1)
    for which in range(count):
        mask = which if count == 2 else 2 * (which & 1) + (which >> 1)
        rows[mine ^ mask] = pieces[which][...]

    def block(t):
        at, off = t * per // size, t * per % size
        if off + per <= size:
            return rows[at, pl.ds(off, per)].astype(F32)
        first = size - off
        return jnp.concatenate([rows[at, pl.ds(off, first)], rows[at + 1, pl.ds(0, per - first)]], axis=0).astype(F32)

    for t in range(27):
        kernel[(t // 3) % 3, t % 3, t // 9] = block(t)
    if len(refs) == count + 3:
        extra[...] = block(27)
    else:
        turned = block(27).T
        extra[...] = turned[0:1]
        refs[count + 2][:, pl.ds(0, per)] = turned[1:2]
        refs[count + 2][:, pl.ds(per, per)] = turned[2:3]


def last(pieces, per, outs, name):
    count = len(pieces)
    size, c = pieces[0].shape
    kernel, *rest = call(
        functools.partial(last_body, count),
        name,
        tuple(pieces),
        [((3, 3, 3, per, c), F32), *outs],
        [pltpu.VMEM((count, size, c), BF16)],
        1,
    )
    return jnp.swapaxes(kernel, 3, 4), *rest


def per_device(field, cotangent, fine_kernel, fine_bias, coarse_kernel, coarse_bias, merge_weight):
    n = lax.axis_size("sub")
    bx, by, bz, c = field.shape
    cx, cy, cz = bx // 2, by // 2, bz // 2
    c2 = merge_weight.shape[0]
    odd = bit_of("sub") == 1
    sa = jnp.where(odd, field[:, 0], field[:, by - 1])
    sb = jnp.where(odd, field[:, by - 1], field[:, 0])
    ya, yb = swap_faces(sa, sb, "sub")
    count = grp_bits() + n.bit_length() - 1
    pg, places = call(
        cubes_body,
        "cubes",
        (cotangent,),
        [((cx, cy, cz, c), BF16), ((count, 1, c), jnp.int32)],
        [pltpu.VMEM((cx * cy * bz, c), F32)],
    )
    face = (((by + 2) * bz + cy * cz, c), BF16)
    own, ta, tb = call(
        turn_body, "turn", (field, ya, yb, pg), [((bx, by + 2, bz, c), BF16), face, face]
    )
    xa, xb = swap_faces(ta, tb, "grp")
    bias = fine_bias.reshape(1, c)
    hidden, ds, pool_in, wb = call(
        inner_body,
        "inner",
        (own, fine_kernel, bias),
        [
            ((bx - 2, by, bz, c), BF16),
            ((bx - 2, by, bz, c), F32),
            ((cx - 2, cy, cz, c), BF16),
            ((9 * c, 3 * c), BF16),
        ],
        [pltpu.VMEM((cy * bz, c), F32)],
        6,
    )

    def edge(second, face):
        return call(
            functools.partial(edge_body, second),
            "edge",
            (own, face, wb, bias, hidden, pool_in),
            [
                ((by, bz, c), BF16),
                ((by, bz, c), F32),
                ((cy, cz, c), BF16),
                ((2, cy, cz, c), BF16),
            ],
            [pltpu.VMEM((cy * bz, c), F32)],
            1,
        )

    hid_a, ds_a, pool_a, pa = edge(False, xa)
    hid_b, ds_b, pool_b, pb = edge(True, xb)
    pxa, pxb = swap_faces(pa, pb, "grp")
    (taps,) = call(taps_body, "taps", (coarse_kernel,), [((9 * c, 3 * c2), BF16)], (), 0.5)
    pxa, taps = lax.optimization_barrier((pxa, taps))
    face = ((2 * (cx + 4) + cx + 2, cz, c), BF16)
    pooled = (pool_in, pool_a, pool_b)
    qa, qb = call(turn2_body, "turn2", (*pooled, pg, pxa, pxb, xa, xb), [face, face])
    pya, pyb = swap_faces(qa, qb, "sub")
    bias2 = coarse_bias.reshape(1, c2)
    slope_mid, coarse_mid = call(
        mid_body,
        "mid",
        (*pooled, pxa, pxb, xa, xb, pg, taps, bias2, merge_weight),
        [((cx + 2, cy - 2, cz, c2), BF16), ((cx, cy - 2, cz, c2), BF16)],
        [pltpu.VMEM((cx + 4, cy, cz, c), BF16), pltpu.VMEM((cx + 2, cy, cz, c), BF16)],
        2,
    )
    cells = cx * cy * cz
    part = (n // 2, 28 * (c2 // n), c)
    slope, coarse, ckeep, csend, cbias = call(
        functools.partial(coarse_body, n),
        "coarse",
        (*pooled, pxa, pxb, pya, pyb, xa, xb, pg, taps, bias2, merge_weight, slope_mid, coarse_mid),
        [
            ((cx + 2, cy + 2, cz, c2), BF16),
            ((cx, cy, cz, c2), BF16),
            (part, BF16),
            (part, BF16),
            ((c2, c), BF16),
        ],
        [
            pltpu.VMEM((cx + 4, cy + 4, cz, c), BF16),
            pltpu.VMEM((cx + 2, cy + 2, cz, c), BF16),
            pltpu.VMEM((3 * c2, cells), BF16),
            pltpu.VMEM((cells, 10 * c), BF16),
            pltpu.VMEM((3 * c2, 10 * c), BF16),
            pltpu.VMEM((c2, c), BF16),
        ],
        6,
    )
    cgot = cores(csend)
    (output,) = call(
        merge_body,
        "merge",
        (hidden, hid_a, hid_b, coarse, merge_weight),
        [((bx, by, bz, c), BF16)],
        [pltpu.VMEM((cx * cy * bz, c), F32)],
        2,
    )
    output, cgot = lax.optimization_barrier((output, cgot))
    csent = spread_sum(ckeep, cgot)
    slope, csent = lax.optimization_barrier((slope, csent))
    cparts = cross(*csent)
    voxels = bx * by * bz
    part = (n // 2, 28 * (c // n), c)
    fkeep, fsend = call(
        functools.partial(back_body, n),
        "back",
        (slope, coarse_kernel, cotangent, ds, ds_a, ds_b, own, xa, xb, cbias),
        [(part, BF16), (part, BF16)],
        [
            pltpu.VMEM((cx * cy * bz, c), F32),
            pltpu.VMEM((3 * c, voxels), BF16),
            pltpu.VMEM((voxels, 2 * c), BF16),
            pltpu.VMEM((3 * c, 10 * c), BF16),
        ],
        10,
    )

    coarse_sum, fine_sum = side_by_side(
        finish_sum(cparts, places, "coarse", ("half", "sum")),
        lambda got: finish_sum(cross(*spread_sum(fkeep, jnp.stack(got))), places, "fine", ("half", "sum")),
        [cores(part) for part in fsend],
    )
    per, cper = c // n, c2 // n
    grad_coarse, grad_merge = last(coarse_sum, cper, [((cper, c), F32)], "coarse_last")
    fine_sum, grad_merge = lax.optimization_barrier((fine_sum, grad_merge))
    biases = [((1, per), F32), ((1, cper), F32)]
    grad_fine, bias, coarse_sums = last(fine_sum, per, biases, "fine_last")
    return (output, grad_fine, bias[0], grad_coarse, coarse_sums[0], grad_merge)


def solution(mesh):
    in_specs = (P("grp", "sub", None, None), P("grp", "sub", None, None), P(), P(), P(), P(), P())
    out_specs = (
        P("grp", "sub", None, None),
        P(None, None, None, None, "sub"),
        P("sub"),
        P(None, None, None, None, "sub"),
        P("sub"),
        P("sub", None),
    )
    return jax.shard_map(
        per_device, mesh=mesh, in_specs=in_specs, out_specs=out_specs, check_vma=False
    )
```

```python
import functools

import jax
import jax.numpy as jnp
from jax import lax
from jax.experimental import pallas as pl
from jax.experimental.pallas import tpu as pltpu
from jax.sharding import PartitionSpec as P

F32 = jnp.float32
BF16 = jnp.bfloat16
VMEM_LIMIT = 32 * 1024 * 1024


def bit_of(axis, bit=0):
    return (lax.axis_index(axis) >> bit) & 1


def call(body, name, args, outs, scratch=(), micros=1):
    return pl.pallas_call(
        body,
        name=name,
        out_shape=[jax.ShapeDtypeStruct(s, t) for s, t in outs],
        in_specs=[pl.BlockSpec(memory_space=pltpu.VMEM) for _ in args],
        out_specs=[pl.BlockSpec(memory_space=pltpu.VMEM) for _ in outs],
        scratch_shapes=list(scratch),
        compiler_params=pltpu.CompilerParams(vmem_limit_bytes=VMEM_LIMIT),
        cost_estimate=pl.CostEstimate(
            flops=int(micros * 1e9), bytes_accessed=0, transcendentals=0
        ),
    )(*args)


def put_faces(odd, first, second, low, high):
    first[...] = jnp.where(odd, low, high)
    second[...] = jnp.where(odd, high, low)


def get_faces(odd, first, second):
    a, b = first[...], second[...]
    return jnp.where(odd, a, b), jnp.where(odd, b, a)


def sum_cube(rows, planes, ref):
    half = rows // 2
    ref[pl.ds(0, rows), :] = planes
    return ref[pl.ds(0, half, stride=2), :] + ref[pl.ds(1, half, stride=2), :]


def shift_rows(value, step, depth):
    rows = value.shape[0]
    moved = pltpu.roll(value, step % rows, 0)
    place = lax.broadcasted_iota(jnp.int32, value.shape, 0) % depth
    edge = 0 if step == 1 else depth - 1
    return jnp.where(place == edge, 0.0, moved)


def sigmoid(value):
    return 1.0 / (1.0 + jnp.exp(-value))


def turn_body(field, ya, yb, pg, own, out_a, out_b):
    bx, by, bz, c = field.shape
    cx, cy, cz, _ = pg.shape
    ylo, yhi = get_faces(bit_of("sub") == 1, ya, yb)
    own[:, 1 : by + 1] = field[...]
    own[:, 0] = ylo
    own[:, by + 1] = yhi

    def side(x, at):
        return jnp.concatenate([own[x].reshape((by + 2) * bz, c), pg[at].reshape(cy * cz, c)], axis=0)

    put_faces(bit_of("grp") == 1, out_a, out_b, side(0, 0), side(bx - 1, cx - 1))


def x_faces(xa, xb, fine, coarse):
    by, bz, c = fine
    cy, cz, _ = coarse
    lo, hi = get_faces(bit_of("grp") == 1, xa, xb)
    rows = by * bz
    return (
        (lo[:rows].reshape(by, bz, c), hi[:rows].reshape(by, bz, c)),
        (lo[rows:].reshape(cy, cz, c), hi[rows:].reshape(cy, cz, c)),
    )


def fine_plane(three, wb, bias, by):
    _, bz, c = three[0].shape
    rows = by * bz * (len(three) - 2)
    taps = [
        jnp.concatenate([plane[j : j + by].reshape(by * bz, c) for plane in three[i : len(three) - 2 + i]], axis=0)
        for i in range(3)
        for j in range(3)
    ]
    part = jnp.dot(jnp.concatenate(taps, axis=1), wb[...], preferred_element_type=F32)
    pre = (
        part[:, c : 2 * c]
        + shift_rows(part[:, :c], 1, bz)
        + shift_rows(part[:, 2 * c :], -1, bz)
        + bias[...]
    )
    sig = sigmoid(pre)
    hid = (pre * sig).astype(BF16).reshape(-1, by, bz, c)
    return hid, (sig * (1.0 + pre * (1.0 - sig))).reshape(-1, by, bz, c)


def pool(one, two, tmp):
    by, bz, c = one.shape
    cy = by // 2
    both = jnp.sum((one.astype(F32) + two.astype(F32)).reshape(cy, 2, bz, c), axis=1)
    total = sum_cube(cy * bz, both.reshape(cy * bz, c), tmp)
    return (total / 8.0).astype(BF16).reshape(cy, bz // 2, c)


def inner_body(own, w, bias, hidden, ds, pooled, wb, tmp):
    by, c = own.shape[1] - 2, own.shape[3]
    for i in range(3):
        for j in range(3):
            for k in range(3):
                wb[pl.ds((3 * i + j) * c, c), pl.ds(k * c, c)] = w[i, j, k]

    def plane(x, carry):
        hid, slope = fine_plane([own[3 * x + k] for k in range(5)], wb, bias, by)
        hidden[pl.ds(3 * x, 3)], ds[pl.ds(3 * x, 3)] = hid, slope
        return carry

    lax.fori_loop(0, hidden.shape[0] // 3, plane, 0)
    for q in range(pooled.shape[0]):
        pooled[q] = pool(hidden[2 * q + 1], hidden[2 * q + 2], tmp)


def edge_body(second, own, face, wb, bias, hid_in, pool_in, hidden, ds, pooled, out, tmp):
    bx, by, bz, c = own.shape
    cx = bx // 2
    low = bit_of("grp") == (0 if second else 1)
    halo = face[pl.ds(0, by * bz), :].reshape(by, bz, c)
    near, inside = own[jnp.where(low, 0, bx - 1)], own[jnp.where(low, 1, bx - 2)]
    three = [jnp.where(low, halo, inside), near, jnp.where(low, inside, halo)]
    hid, slope = fine_plane(three, wb, bias, by - 2)
    hidden[...], ds[...] = hid[0], slope[0]
    pooled[...] = pool(hidden[...], hid_in[jnp.where(low, 0, bx - 3)], tmp)
    out[0] = jnp.where(low, pooled[...], pool_in[cx - 3])
    out[1] = jnp.where(low, pool_in[0], pooled[...])


def taps_body(w, wb):
    c, c2 = w.shape[3], w.shape[4]
    for i in range(3):
        for j in range(3):
            for k in range(3):
                wb[pl.ds((3 * i + j) * c, c), pl.ds(k * c2, c2)] = w[i, j, k]


def cubes_body(cot, pg, bits, tmp):
    bx, by, bz, c = cot.shape
    cx, cy, cz = bx // 2, by // 2, bz // 2
    total = jnp.sum(cot[...].astype(F32).reshape(cx, 2, cy, 2, bz, c), axis=(1, 3))
    grad = sum_cube(cx * cy * bz, total.reshape(cx * cy * bz, c), tmp).astype(BF16)
    pg[...] = grad.reshape(cx, cy, cz, c)
    first = grp_bits()
    for k in range(bits.shape[0]):
        value = bit_of("grp", k) if k < first else bit_of("sub", k - first)
        bits[k] = jnp.full(bits.shape[1:], value, jnp.int32)


def pooled_of(pool_in, pool_a, pool_b):
    lo, hi = get_faces(bit_of("grp") == 1, pool_a, pool_b)
    return jnp.concatenate([lo[None], pool_in[...], hi[None]], axis=0)


def turn2_body(pool_in, pool_a, pool_b, pg, ra, rb, xa, xb, out_a, out_b):
    cy, cz, c = pool_a.shape
    pooled = pooled_of(pool_in, pool_a, pool_b)
    xlo, xhi = get_faces(bit_of("grp") == 1, ra, rb)
    _, (glo, ghi) = x_faces(xa, xb, (2 * cy + 2, 2 * cz, c), (cy, cz, c))

    def side(y, last):
        two = [jnp.concatenate([xlo[:, at], pooled[:, at], xhi[:, at]], axis=0) for at in (y, y + 1)]
        one = jnp.concatenate([glo[None, last], pg[:, last], ghi[None, last]], axis=0)
        return jnp.concatenate([*two, one], axis=0)

    put_faces(bit_of("sub") == 1, out_a, out_b, side(0, 0), side(cy - 2, cy - 1))


def reverse_bits(value, count):
    out = 0
    for _ in range(count):
        out, value = out * 2 + value % 2, value // 2
    return out


def spread(keep, send, n, blocks, piece):
    bits = n.bit_length() - 1
    half = n // 2
    for b in (0, 1):

        @pl.when(bit_of("sub") == b)
        def _():
            for s in range(n):
                target = keep if s % 2 == b else send
                for t in range(blocks):
                    value = piece(s, t)
                    size = value.shape[0]
                    target[reverse_bits(s, bits) % half, pl.ds(t * size, size)] = value


def coarse_part(taps, grads, wb, bias, wm, cz):
    c2 = wm.shape[0]
    part = jnp.dot(jnp.concatenate(taps, axis=1), wb[...], preferred_element_type=F32)
    pre = (
        part[:, c2 : 2 * c2]
        + shift_rows(part[:, :c2], 1, cz)
        + shift_rows(part[:, 2 * c2 :], -1, cz)
        + bias[...]
    )
    sig = sigmoid(pre)
    back = lax.dot_general(grads, wm[...], (((1,), (1,)), ((), ())), preferred_element_type=F32)
    return (back * (sig * (1.0 + pre * (1.0 - sig)))).astype(BF16), (pre * sig).astype(BF16)


def mid_body(pool_in, pool_a, pool_b, ra, rb, xa, xb, pg, wb, bias, wm, slope, coarse, qx, gx):
    cx, cy, cz, c = pg.shape
    c2 = wm.shape[0]
    qx[0:2], qx[cx + 2 : cx + 4] = get_faces(bit_of("grp") == 1, ra, rb)
    qx[2 : cx + 2] = pooled_of(pool_in, pool_a, pool_b)
    _, (gx[0], gx[cx + 1]) = x_faces(xa, xb, (2 * cy + 2, 2 * cz, c), (cy, cz, c))
    gx[1 : cx + 1] = pg[...]
    for first in range(0, cx + 2, 3):
        planes = range(first, first + 3)
        taps = [
            jnp.concatenate([qx[x + i, j : j + cy - 2].reshape(-1, c) for x in planes], axis=0)
            for i in range(3)
            for j in range(3)
        ]
        grads = jnp.concatenate([gx[x, 1 : cy - 1].reshape(-1, c) for x in planes], axis=0)
        out, act = coarse_part(taps, grads, wb, bias, wm, cz)
        slope[first : first + 3] = out.reshape(3, cy - 2, cz, c2)
        act = act.reshape(3, cy - 2, cz, c2)
        for h, x in enumerate(planes):
            if 1 <= x <= cx:
                coarse[x - 1] = act[h]


def coarse_body(
    n, pool_in, pool_a, pool_b, ra, rb, ua, ub, xa, xb, pg, wb, bias, wm, slope_mid, coarse_mid,
    slope, coarse, keep, send, cbias, qpad, gpad, st, acc, ct,
):
    cx, cy, cz, c = pg.shape
    c2 = wm.shape[0]
    xlo, xhi = get_faces(bit_of("grp") == 1, ra, rb)
    ylo, yhi = get_faces(bit_of("sub") == 1, ua, ub)
    qpad[2 : cx + 2, 2 : cy + 2] = pooled_of(pool_in, pool_a, pool_b)
    qpad[0:2, 2 : cy + 2] = xlo
    qpad[cx + 2 : cx + 4, 2 : cy + 2] = xhi
    wide = cx + 4
    for t in (0, 1):
        qpad[:, t] = ylo[t * wide : (t + 1) * wide]
        qpad[:, cy + 2 + t] = yhi[t * wide : (t + 1) * wide]
    gpad[1 : cx + 1, 1 : cy + 1] = pg[...]
    _, (glo, ghi) = x_faces(xa, xb, (2 * cy + 2, 2 * cz, c), (cy, cz, c))
    gpad[0, 1 : cy + 1] = glo
    gpad[cx + 1, 1 : cy + 1] = ghi
    gpad[:, 0] = ylo[2 * wide :]
    gpad[:, cy + 1] = yhi[2 * wide :]
    def both(ref, x, j):
        return jnp.concatenate([ref[x, j : j + 2], ref[x, cy + j : cy + 2 + j]], axis=0).reshape(4 * cz, -1)

    planes = range(cx + 2)
    taps = [
        jnp.concatenate([both(qpad, x + i, j) for x in planes], axis=0) for i in range(3) for j in range(3)
    ]
    grads = jnp.concatenate([both(gpad, x, 0) for x in planes], axis=0)
    out, act = coarse_part(taps, grads, wb, bias, wm, cz)
    out, act = (v.reshape(cx + 2, 4, cz, c2) for v in (out, act))
    slope[:, 0:2] = out[:, 0:2]
    slope[:, cy : cy + 2] = out[:, 2:4]
    slope[:, 2:cy] = slope_mid[...]
    coarse[:, 0] = act[1 : cx + 1, 1]
    coarse[:, cy - 1] = act[1 : cx + 1, 2]
    coarse[:, 1 : cy - 1] = coarse_mid[...]
    cells = cx * cy * cz
    mid = slope[1 : cx + 1, 1 : cy + 1].reshape(cells, c2)
    wide_mid = mid.astype(F32)
    st[pl.ds(0, c2), :] = shift_rows(wide_mid, -1, cz).astype(BF16).T
    st[pl.ds(c2, c2), :] = mid.T
    st[pl.ds(2 * c2, c2), :] = shift_rows(wide_mid, 1, cz).astype(BF16).T

    def window(t):
        if t == 9:
            return jnp.ones((cells, c), BF16)
        i, j = 1 + t // 3, 1 + t % 3
        return qpad[i : i + cx, j : j + cy].reshape(cells, c)

    for t in range(0, 10, 2):
        acc[:, pl.ds(t * c, 2 * c)] = jnp.dot(
            st[...], jnp.concatenate([window(t), window(t + 1)], axis=1), preferred_element_type=F32
        ).astype(BF16)
    ct[...] = jnp.dot(
        coarse[...].reshape(cells, c2).T, pg[...].reshape(cells, c), preferred_element_type=F32
    ).astype(BF16)
    cbias[...] = acc[pl.ds(c2, c2), pl.ds(9 * c, c)]
    per = c2 // n

    def piece(s, t):
        if t == 27:
            return ct[pl.ds(s * per, per), :]
        k, tap = t // 9, t % 9
        return acc[pl.ds(k * c2 + s * per, per), pl.ds(tap * c, c)]

    spread(keep, send, n, 28, piece)


def back_body(n, slope, w, cot, ds, ds_a, ds_b, own, xa, xb, cbias, keep, send, up, st, acc):
    bx, by, bz, c = cot.shape
    cx, cy, cz = bx // 2, by // 2, bz // 2
    c2 = slope.shape[3]
    cells = cx * cy * cz
    total = jnp.zeros((cells, 3 * c), F32)
    for i in range(3):
        for j in range(3):
            tap = slope[2 - i : 2 - i + cx, 2 - j : 2 - j + cy].reshape(cells, c2)
            total = total + lax.dot_general(
                tap,
                w[i, j].reshape(3 * c, c2),
                (((1,), (1,)), ((), ())),
                preferred_element_type=F32,
            )
    pooled = (
        total[:, c : 2 * c]
        + shift_rows(total[:, :c], -1, cz)
        + shift_rows(total[:, 2 * c :], 1, cz)
    ) * 0.125
    up[pl.ds(0, cells, stride=2), :] = pooled
    up[pl.ds(1, cells, stride=2), :] = pooled
    rows = by * bz
    edges = get_faces(bit_of("grp") == 1, ds_a, ds_b)
    halo, _ = x_faces(xa, xb, (by + 2, bz, c), (cy, cz, c))
    for x in range(bx):
        base = up[pl.ds((x // 2) * cy * bz, cy * bz), :].reshape(cy, 1, bz, c)
        fine = cot[x].astype(F32).reshape(cy, 2, bz, c) + base
        gain = ds[x - 1] if 0 < x < bx - 1 else edges[x // (bx - 1)]
        fs = (fine.reshape(rows, c) * gain.reshape(rows, c)).astype(BF16)
        wide = fs.astype(F32)
        st[pl.ds(0, c), pl.ds(x * rows, rows)] = shift_rows(wide, -1, bz).astype(BF16).T
        st[pl.ds(c, c), pl.ds(x * rows, rows)] = fs.T
        st[pl.ds(2 * c, c), pl.ds(x * rows, rows)] = shift_rows(wide, 1, bz).astype(BF16).T

    def window(t, x):
        if t == 9:
            return jnp.ones((rows, c), BF16)
        x, j = x + t // 3 - 1, t % 3
        plane = own[x, j : j + by] if 0 <= x < bx else halo[int(x == bx)][j : j + by]
        return plane.reshape(rows, c)

    for t in range(0, 10, 2):
        total = jnp.zeros((3 * c, 2 * c), F32)
        for first in range(0, bx, 1):
            pairs = [jnp.concatenate([window(t, x), window(t + 1, x)], axis=1) for x in range(first, first + 1)]
            total = total + jnp.dot(
                st[:, pl.ds(first * rows, 1 * rows)],
                jnp.concatenate(pairs, axis=0),
                preferred_element_type=F32,
            )
        acc[:, pl.ds(t * c, 2 * c)] = total.astype(BF16)
    per, cper = c // n, c2 // n
    lane = lax.broadcasted_iota(jnp.int32, (per, c), 1)

    def piece(s, t):
        if t == 27:
            bias = acc[pl.ds(c + s * per, per), pl.ds(9 * c, c)].astype(F32)
            one = cbias[pl.ds(s * cper, per), :].astype(F32)
            two = cbias[pl.ds(s * cper + per, per), :].astype(F32)
            return jnp.where(lane == 0, bias, jnp.where(lane == 1, one, two)).astype(BF16)
        k, tap = t // 9, t % 9
        return acc[pl.ds(k * c + s * per, per), pl.ds(tap * c, c)]

    spread(keep, send, n, 28, piece)


def merge_body(hidden, hid_a, hid_b, coarse, wm, out, tmp):
    bx, by, bz, c = out.shape
    cx, cy, cz = bx // 2, by // 2, bz // 2
    c2 = coarse.shape[3]
    cells = cx * cy * cz
    proj = jnp.dot(coarse[...].reshape(cells, c2), wm[...], preferred_element_type=F32)
    tmp[pl.ds(0, cells, stride=2), :] = proj
    tmp[pl.ds(1, cells, stride=2), :] = proj
    edges = get_faces(bit_of("grp") == 1, hid_a, hid_b)
    for x in range(bx):
        base = tmp[pl.ds((x // 2) * cy * bz, cy * bz), :].reshape(cy, 1, bz, c)
        hid = hidden[x - 1] if 0 < x < bx - 1 else edges[x // (bx - 1)]
        total = hid.astype(F32).reshape(cy, 2, bz, c) + base
        out[x] = total.astype(BF16).reshape(by, bz, c)


def swap_faces(first, second, axis):
    n = lax.axis_size(axis)
    one = [p for i in range(0, n - 1, 2) for p in ((i, i + 1), (i + 1, i))]
    two = [p for i in range(1, n - 1, 2) for p in ((i, i + 1), (i + 1, i))]
    got = lax.ppermute(second, axis, two)
    return lax.ppermute(first, axis, one), got


def split4_body(keep, got, own, over_sub, over_grp, over_both):
    g, s = bit_of("grp"), bit_of("sub", 1)

    def part(a, b):
        return (keep[a, :, b].astype(F32) + got[a, :, b].astype(F32)).astype(BF16)

    over_both[...] = part(1 - s, 1 - g)
    over_sub[...] = part(1 - s, g)
    over_grp[...] = part(s, 1 - g)
    own[...] = part(s, g)


def total_of(parts):
    return sum(p.astype(F32) for p in parts).astype(BF16)


def halves(pair, bit):
    return jnp.where(bit == 1, pair[1], pair[0]), jnp.where(bit == 1, pair[0], pair[1])


def partners(value, grp_mask, sub_mask):
    n_grp, n_sub = lax.axis_size("grp"), lax.axis_size("sub")
    pairs = [
        (g * n_sub + s, (g ^ grp_mask) * n_sub + (s ^ sub_mask))
        for g in range(n_grp)
        for s in range(n_sub)
    ]
    return lax.ppermute(value, ("grp", "sub"), pairs)


def split_sum(parts, bit):
    rows, c = parts[0].shape
    return halves(total_of([p.reshape(2, rows // 2, c) for p in parts]), bit)


def grp_bits():
    return lax.axis_size("grp").bit_length() - 1


def cores(send):
    return partners(send, 0, 1)


def spread_sum(keep, got):
    half, rows, c = keep.shape
    rest = half // 2
    shape = (2, rest, 2, rows // 2, c)
    out = ((rest, rows // 2, c), BF16)
    return call(split4_body, "split", (keep.reshape(shape), got.reshape(shape)), [out] * 4, (), 1)


def cross(own, over_sub, over_grp, over_both):
    return [own, partners(over_both, 1, 2), partners(over_sub, 0, 2), partners(over_grp, 1, 0)]


def split_body(count, axis, bit, *refs):
    mine = bit_of(axis, bit)

    def part(at):
        return sum(p[at].astype(F32) for p in refs[:count]).astype(BF16)

    refs[count + 1][...] = part(1 - mine)
    refs[count][...] = part(mine)


def sum_body(count, *refs):
    refs[count][...] = sum(p[...].astype(F32) for p in refs[:count]).astype(BF16)


def split_sum_kernel(parts, axis, bit, name):
    rows, c = parts[0].shape
    half = ((rows // 2, c), BF16)
    shaped = [p.reshape(2, rows // 2, c) for p in parts]
    return call(functools.partial(split_body, len(parts), axis, bit), name, shaped, [half, half], (), 0.8)


def sum_kernel(parts, name):
    out = [(parts[0].shape, BF16)]
    return call(functools.partial(sum_body, len(parts)), name, parts, out, (), 0.5)[0]


def finish_sum(parts, places, name, kernels):
    rest, rows, c = parts[0].shape
    parts = [p.reshape(rest * rows, c) for p in parts]
    for bit in range(2, lax.axis_size("sub").bit_length() - 1):
        keep, send = split_sum(parts, places[grp_bits() + bit])
        parts = [keep, partners(send, 0, 1 << bit)]
    parts = yield parts
    bits = [0]
    last = grp_bits() - 1
    for bit in range(1, last + 1):
        mask = 1 << bit
        if bit == 1 and bit < last and parts[0].shape[0] % 32 == 0:
            if "half" in kernels:
                keep, send = split_sum_kernel(parts, "grp", bit, name + "_half")
            else:
                keep, send = split_sum(parts, places[bit])
            keep, send = yield keep, send
            parts = yield keep, partners(send, mask, 0)
            bits.append(bit)
        else:
            total = sum_kernel(parts, name + "_sum") if "sum" in kernels else total_of(parts)
            total = yield total
            parts = yield total, partners(total, mask, 0)
    total = sum_kernel(parts, name + "_total") if "total" in kernels else total_of(parts)
    pieces = [total]
    for which in range(1, 2 ** len(bits)):
        pieces.append(partners(total, sum(1 << bits[b] for b in range(len(bits)) if which >> b & 1), 0))
    return pieces


def step(run, value):
    try:
        return run.send(value), None
    except StopIteration as done:
        return None, done.value


def side_by_side(ahead, behind, arrived):
    first, first_done = step(ahead, step(ahead, None)[0])
    first, arrived = lax.optimization_barrier((first, arrived))
    first, first_done = step(ahead, first)
    behind = behind(arrived)
    second, second_done = step(behind, None)
    while second_done is None:
        if first_done is None:
            first, first_done = step(ahead, first)
        if first_done is None:
            first, first_done = step(ahead, first)
        second, second_done = step(behind, second)
        if second_done is None:
            second, second_done = step(behind, second)
            if first_done is None and second_done is None:
                first, second = lax.optimization_barrier((first, second))
    return first_done, second_done


def last_body(count, *refs):
    pieces, kernel, extra, rows = refs[:count], refs[count], refs[count + 1], refs[-1]
    size = pieces[0].shape[0]
    per = extra.shape[0] if len(refs) == count + 3 else kernel.shape[3]
    mine = bit_of("grp") if count == 2 else 2 * bit_of("grp") + bit_of("grp", 1)
    for which in range(count):
        mask = which if count == 2 else 2 * (which & 1) + (which >> 1)
        rows[mine ^ mask] = pieces[which][...]

    def block(t):
        at, off = t * per // size, t * per % size
        if off + per <= size:
            return rows[at, pl.ds(off, per)].astype(F32)
        first = size - off
        return jnp.concatenate([rows[at, pl.ds(off, first)], rows[at + 1, pl.ds(0, per - first)]], axis=0).astype(F32)

    for t in range(27):
        kernel[(t // 3) % 3, t % 3, t // 9] = block(t)
    if len(refs) == count + 3:
        extra[...] = block(27)
    else:
        turned = block(27).T
        extra[...] = turned[0:1]
        refs[count + 2][:, pl.ds(0, per)] = turned[1:2]
        refs[count + 2][:, pl.ds(per, per)] = turned[2:3]


def last(pieces, per, outs, name):
    count = len(pieces)
    size, c = pieces[0].shape
    kernel, *rest = call(
        functools.partial(last_body, count),
        name,
        tuple(pieces),
        [((3, 3, 3, per, c), F32), *outs],
        [pltpu.VMEM((count, size, c), BF16)],
        1,
    )
    return jnp.swapaxes(kernel, 3, 4), *rest


def per_device(field, cotangent, fine_kernel, fine_bias, coarse_kernel, coarse_bias, merge_weight):
    n = lax.axis_size("sub")
    bx, by, bz, c = field.shape
    cx, cy, cz = bx // 2, by // 2, bz // 2
    c2 = merge_weight.shape[0]
    odd = bit_of("sub") == 1
    sa = jnp.where(odd, field[:, 0], field[:, by - 1])
    sb = jnp.where(odd, field[:, by - 1], field[:, 0])
    ya, yb = swap_faces(sa, sb, "sub")
    count = grp_bits() + n.bit_length() - 1
    pg, places = call(
        cubes_body,
        "cubes",
        (cotangent,),
        [((cx, cy, cz, c), BF16), ((count, 1, c), jnp.int32)],
        [pltpu.VMEM((cx * cy * bz, c), F32)],
    )
    face = (((by + 2) * bz + cy * cz, c), BF16)
    own, ta, tb = call(
        turn_body, "turn", (field, ya, yb, pg), [((bx, by + 2, bz, c), BF16), face, face]
    )
    xa, xb = swap_faces(ta, tb, "grp")
    bias = fine_bias.reshape(1, c)
    hidden, ds, pool_in, wb = call(
        inner_body,
        "inner",
        (own, fine_kernel, bias),
        [
            ((bx - 2, by, bz, c), BF16),
            ((bx - 2, by, bz, c), F32),
            ((cx - 2, cy, cz, c), BF16),
            ((9 * c, 3 * c), BF16),
        ],
        [pltpu.VMEM((cy * bz, c), F32)],
        6,
    )

    def edge(second, face):
        return call(
            functools.partial(edge_body, second),
            "edge",
            (own, face, wb, bias, hidden, pool_in),
            [
                ((by, bz, c), BF16),
                ((by, bz, c), F32),
                ((cy, cz, c), BF16),
                ((2, cy, cz, c), BF16),
            ],
            [pltpu.VMEM((cy * bz, c), F32)],
            1,
        )

    hid_a, ds_a, pool_a, pa = edge(False, xa)
    hid_b, ds_b, pool_b, pb = edge(True, xb)
    pxa, pxb = swap_faces(pa, pb, "grp")
    (taps,) = call(taps_body, "taps", (coarse_kernel,), [((9 * c, 3 * c2), BF16)], (), 0.5)
    pxa, taps = lax.optimization_barrier((pxa, taps))
    face = ((2 * (cx + 4) + cx + 2, cz, c), BF16)
    pooled = (pool_in, pool_a, pool_b)
    qa, qb = call(turn2_body, "turn2", (*pooled, pg, pxa, pxb, xa, xb), [face, face])
    pya, pyb = swap_faces(qa, qb, "sub")
    bias2 = coarse_bias.reshape(1, c2)
    pyb, pya = lax.optimization_barrier((pyb, pya))
    slope_mid, coarse_mid = call(
        mid_body,
        "mid",
        (*pooled, pxa, pxb, xa, xb, pg, taps, bias2, merge_weight),
        [((cx + 2, cy - 2, cz, c2), BF16), ((cx, cy - 2, cz, c2), BF16)],
        [pltpu.VMEM((cx + 4, cy, cz, c), BF16), pltpu.VMEM((cx + 2, cy, cz, c), BF16)],
        2,
    )
    cells = cx * cy * cz
    part = (n // 2, 28 * (c2 // n), c)
    slope, coarse, ckeep, csend, cbias = call(
        functools.partial(coarse_body, n),
        "coarse",
        (*pooled, pxa, pxb, pya, pyb, xa, xb, pg, taps, bias2, merge_weight, slope_mid, coarse_mid),
        [
            ((cx + 2, cy + 2, cz, c2), BF16),
            ((cx, cy, cz, c2), BF16),
            (part, BF16),
            (part, BF16),
            ((c2, c), BF16),
        ],
        [
            pltpu.VMEM((cx + 4, cy + 4, cz, c), BF16),
            pltpu.VMEM((cx + 2, cy + 2, cz, c), BF16),
            pltpu.VMEM((3 * c2, cells), BF16),
            pltpu.VMEM((3 * c2, 10 * c), BF16),
            pltpu.VMEM((c2, c), BF16),
        ],
        6,
    )
    cgot = cores(csend)
    (output,) = call(
        merge_body,
        "merge",
        (hidden, hid_a, hid_b, coarse, merge_weight),
        [((bx, by, bz, c), BF16)],
        [pltpu.VMEM((cx * cy * bz, c), F32)],
        2,
    )
    output, cgot = lax.optimization_barrier((output, cgot))
    csent = spread_sum(ckeep, cgot)
    slope, csent = lax.optimization_barrier((slope, csent))
    cparts = cross(*csent)
    voxels = bx * by * bz
    part = (n // 2, 28 * (c // n), c)
    fkeep, fsend = call(
        functools.partial(back_body, n),
        "back",
        (slope, coarse_kernel, cotangent, ds, ds_a, ds_b, own, xa, xb, cbias),
        [(part, BF16), (part, BF16)],
        [
            pltpu.VMEM((cx * cy * bz, c), F32),
            pltpu.VMEM((3 * c, voxels), BF16),
            pltpu.VMEM((3 * c, 10 * c), BF16),
        ],
        10,
    )

    coarse_sum, fine_sum = side_by_side(
        finish_sum(cparts, places, "coarse", ("half", "sum")),
        lambda got: finish_sum(cross(*spread_sum(fkeep, jnp.stack(got))), places, "fine", ("half", "sum")),
        [cores(part) for part in fsend],
    )
    per, cper = c // n, c2 // n
    grad_coarse, grad_merge = last(coarse_sum, cper, [((cper, c), F32)], "coarse_last")
    fine_sum, grad_merge = lax.optimization_barrier((fine_sum, grad_merge))
    biases = [((1, per), F32), ((1, cper), F32)]
    grad_fine, bias, coarse_sums = last(fine_sum, per, biases, "fine_last")
    return (output, grad_fine, bias[0], grad_coarse, coarse_sums[0], grad_merge)


def solution(mesh):
    in_specs = (P("grp", "sub", None, None), P("grp", "sub", None, None), P(), P(), P(), P(), P())
    out_specs = (
        P("grp", "sub", None, None),
        P(None, None, None, None, "sub"),
        P("sub"),
        P(None, None, None, None, "sub"),
        P("sub"),
        P("sub", None),
    )
    return jax.shard_map(
        per_device, mesh=mesh, in_specs=in_specs, out_specs=out_specs, check_vma=False
    )
```

```python
import functools

import jax
import jax.numpy as jnp
from jax import lax
from jax.experimental import pallas as pl
from jax.experimental.pallas import tpu as pltpu
from jax.sharding import PartitionSpec as P

F32 = jnp.float32
BF16 = jnp.bfloat16
VMEM_LIMIT = 32 * 1024 * 1024


def bit_of(axis, bit=0):
    return (lax.axis_index(axis) >> bit) & 1


def call(body, name, args, outs, scratch=(), micros=1):
    return pl.pallas_call(
        body,
        name=name,
        out_shape=[jax.ShapeDtypeStruct(s, t) for s, t in outs],
        in_specs=[pl.BlockSpec(memory_space=pltpu.VMEM) for _ in args],
        out_specs=[pl.BlockSpec(memory_space=pltpu.VMEM) for _ in outs],
        scratch_shapes=list(scratch),
        compiler_params=pltpu.CompilerParams(vmem_limit_bytes=VMEM_LIMIT),
        cost_estimate=pl.CostEstimate(
            flops=int(micros * 1e9), bytes_accessed=0, transcendentals=0
        ),
    )(*args)


def put_faces(odd, first, second, low, high):
    first[...] = jnp.where(odd, low, high)
    second[...] = jnp.where(odd, high, low)


def get_faces(odd, first, second):
    a, b = first[...], second[...]
    return jnp.where(odd, a, b), jnp.where(odd, b, a)


def sum_cube(rows, planes, ref):
    half = rows // 2
    ref[pl.ds(0, rows), :] = planes
    return ref[pl.ds(0, half, stride=2), :] + ref[pl.ds(1, half, stride=2), :]


def shift_rows(value, step, depth):
    rows = value.shape[0]
    moved = pltpu.roll(value, step % rows, 0)
    place = lax.broadcasted_iota(jnp.int32, value.shape, 0) % depth
    edge = 0 if step == 1 else depth - 1
    return jnp.where(place == edge, 0.0, moved)


def sigmoid(value):
    return 1.0 / (1.0 + jnp.exp(-value))


def turn_body(field, ya, yb, pg, own, out_a, out_b):
    bx, by, bz, c = field.shape
    cx, cy, cz, _ = pg.shape
    ylo, yhi = get_faces(bit_of("sub") == 1, ya, yb)
    own[:, 1 : by + 1] = field[...]
    own[:, 0] = ylo
    own[:, by + 1] = yhi

    def side(x, at):
        return jnp.concatenate([own[x].reshape((by + 2) * bz, c), pg[at].reshape(cy * cz, c)], axis=0)

    put_faces(bit_of("grp") == 1, out_a, out_b, side(0, 0), side(bx - 1, cx - 1))


def x_faces(xa, xb, fine, coarse):
    by, bz, c = fine
    cy, cz, _ = coarse
    lo, hi = get_faces(bit_of("grp") == 1, xa, xb)
    rows = by * bz
    return (
        (lo[:rows].reshape(by, bz, c), hi[:rows].reshape(by, bz, c)),
        (lo[rows:].reshape(cy, cz, c), hi[rows:].reshape(cy, cz, c)),
    )


def fine_plane(three, wb, bias, by):
    _, bz, c = three[0].shape
    rows = by * bz * (len(three) - 2)
    taps = [
        jnp.concatenate([plane[j : j + by].reshape(by * bz, c) for plane in three[i : len(three) - 2 + i]], axis=0)
        for i in range(3)
        for j in range(3)
    ]
    part = jnp.dot(jnp.concatenate(taps, axis=1), wb[...], preferred_element_type=F32)
    pre = (
        part[:, c : 2 * c]
        + shift_rows(part[:, :c], 1, bz)
        + shift_rows(part[:, 2 * c :], -1, bz)
        + bias[...]
    )
    sig = sigmoid(pre)
    hid = (pre * sig).astype(BF16).reshape(-1, by, bz, c)
    return hid, (sig * (1.0 + pre * (1.0 - sig))).reshape(-1, by, bz, c)


def pool(one, two, tmp):
    by, bz, c = one.shape
    cy = by // 2
    both = jnp.sum((one.astype(F32) + two.astype(F32)).reshape(cy, 2, bz, c), axis=1)
    total = sum_cube(cy * bz, both.reshape(cy * bz, c), tmp)
    return (total / 8.0).astype(BF16).reshape(cy, bz // 2, c)


def inner_body(own, w, bias, hidden, ds, pooled, wb, tmp):
    by, c = own.shape[1] - 2, own.shape[3]
    for i in range(3):
        for j in range(3):
            for k in range(3):
                wb[pl.ds((3 * i + j) * c, c), pl.ds(k * c, c)] = w[i, j, k]

    def plane(x, carry):
        hid, slope = fine_plane([own[3 * x + k] for k in range(5)], wb, bias, by)
        hidden[pl.ds(3 * x, 3)], ds[pl.ds(3 * x, 3)] = hid, slope
        return carry

    lax.fori_loop(0, hidden.shape[0] // 3, plane, 0)
    for q in range(pooled.shape[0]):
        pooled[q] = pool(hidden[2 * q + 1], hidden[2 * q + 2], tmp)


def edge_body(second, own, face, wb, bias, hid_in, pool_in, hidden, ds, pooled, out, tmp):
    bx, by, bz, c = own.shape
    cx = bx // 2
    low = bit_of("grp") == (0 if second else 1)
    halo = face[pl.ds(0, by * bz), :].reshape(by, bz, c)
    near, inside = own[jnp.where(low, 0, bx - 1)], own[jnp.where(low, 1, bx - 2)]
    three = [jnp.where(low, halo, inside), near, jnp.where(low, inside, halo)]
    hid, slope = fine_plane(three, wb, bias, by - 2)
    hidden[...], ds[...] = hid[0], slope[0]
    pooled[...] = pool(hidden[...], hid_in[jnp.where(low, 0, bx - 3)], tmp)
    out[0] = jnp.where(low, pooled[...], pool_in[cx - 3])
    out[1] = jnp.where(low, pool_in[0], pooled[...])


def taps_body(w, wb):
    c, c2 = w.shape[3], w.shape[4]
    for i in range(3):
        for j in range(3):
            for k in range(3):
                wb[pl.ds((3 * i + j) * c, c), pl.ds(k * c2, c2)] = w[i, j, k]


def cubes_body(cot, pg, bits, tmp):
    bx, by, bz, c = cot.shape
    cx, cy, cz = bx // 2, by // 2, bz // 2
    total = jnp.sum(cot[...].astype(F32).reshape(cx, 2, cy, 2, bz, c), axis=(1, 3))
    grad = sum_cube(cx * cy * bz, total.reshape(cx * cy * bz, c), tmp).astype(BF16)
    pg[...] = grad.reshape(cx, cy, cz, c)
    first = grp_bits()
    for k in range(bits.shape[0]):
        value = bit_of("grp", k) if k < first else bit_of("sub", k - first)
        bits[k] = jnp.full(bits.shape[1:], value, jnp.int32)


def pooled_of(pool_in, pool_a, pool_b):
    lo, hi = get_faces(bit_of("grp") == 1, pool_a, pool_b)
    return jnp.concatenate([lo[None], pool_in[...], hi[None]], axis=0)


def turn2_body(pool_in, pool_a, pool_b, pg, ra, rb, xa, xb, out_a, out_b):
    cy, cz, c = pool_a.shape
    pooled = pooled_of(pool_in, pool_a, pool_b)
    xlo, xhi = get_faces(bit_of("grp") == 1, ra, rb)
    _, (glo, ghi) = x_faces(xa, xb, (2 * cy + 2, 2 * cz, c), (cy, cz, c))

    def side(y, last):
        two = [jnp.concatenate([xlo[:, at], pooled[:, at], xhi[:, at]], axis=0) for at in (y, y + 1)]
        one = jnp.concatenate([glo[None, last], pg[:, last], ghi[None, last]], axis=0)
        return jnp.concatenate([*two, one], axis=0)

    put_faces(bit_of("sub") == 1, out_a, out_b, side(0, 0), side(cy - 2, cy - 1))


def reverse_bits(value, count):
    out = 0
    for _ in range(count):
        out, value = out * 2 + value % 2, value // 2
    return out


def spread(keep, send, n, blocks, piece):
    bits = n.bit_length() - 1
    half = n // 2
    for b in (0, 1):

        @pl.when(bit_of("sub") == b)
        def _():
            for s in range(n):
                target = keep if s % 2 == b else send
                for t in range(blocks):
                    value = piece(s, t)
                    size = value.shape[0]
                    target[reverse_bits(s, bits) % half, pl.ds(t * size, size)] = value


def coarse_part(taps, grads, wb, bias, wm, cz):
    c2 = wm.shape[0]
    part = jnp.dot(jnp.concatenate(taps, axis=1), wb[...], preferred_element_type=F32)
    pre = (
        part[:, c2 : 2 * c2]
        + shift_rows(part[:, :c2], 1, cz)
        + shift_rows(part[:, 2 * c2 :], -1, cz)
        + bias[...]
    )
    sig = sigmoid(pre)
    back = lax.dot_general(grads, wm[...], (((1,), (1,)), ((), ())), preferred_element_type=F32)
    return (back * (sig * (1.0 + pre * (1.0 - sig)))).astype(BF16), (pre * sig).astype(BF16)


def mid_body(pool_in, pool_a, pool_b, ra, rb, xa, xb, pg, wb, bias, wm, slope, coarse, qx, gx):
    cx, cy, cz, c = pg.shape
    c2 = wm.shape[0]
    qx[0:2], qx[cx + 2 : cx + 4] = get_faces(bit_of("grp") == 1, ra, rb)
    qx[2 : cx + 2] = pooled_of(pool_in, pool_a, pool_b)
    _, (gx[0], gx[cx + 1]) = x_faces(xa, xb, (2 * cy + 2, 2 * cz, c), (cy, cz, c))
    gx[1 : cx + 1] = pg[...]
    for first in range(0, cx + 2, 3):
        planes = range(first, first + 3)
        taps = [
            jnp.concatenate([qx[x + i, j : j + cy - 2].reshape(-1, c) for x in planes], axis=0)
            for i in range(3)
            for j in range(3)
        ]
        grads = jnp.concatenate([gx[x, 1 : cy - 1].reshape(-1, c) for x in planes], axis=0)
        out, act = coarse_part(taps, grads, wb, bias, wm, cz)
        slope[first : first + 3] = out.reshape(3, cy - 2, cz, c2)
        act = act.reshape(3, cy - 2, cz, c2)
        for h, x in enumerate(planes):
            if 1 <= x <= cx:
                coarse[x - 1] = act[h]


def coarse_body(
    n, pool_in, pool_a, pool_b, ra, rb, ua, ub, xa, xb, pg, wb, bias, wm, slope_mid, coarse_mid,
    slope, coarse, keep, send, cbias, qpad, gpad, st, acc, ct,
):
    cx, cy, cz, c = pg.shape
    c2 = wm.shape[0]
    xlo, xhi = get_faces(bit_of("grp") == 1, ra, rb)
    ylo, yhi = get_faces(bit_of("sub") == 1, ua, ub)
    qpad[2 : cx + 2, 2 : cy + 2] = pooled_of(pool_in, pool_a, pool_b)
    qpad[0:2, 2 : cy + 2] = xlo
    qpad[cx + 2 : cx + 4, 2 : cy + 2] = xhi
    wide = cx + 4
    for t in (0, 1):
        qpad[:, t] = ylo[t * wide : (t + 1) * wide]
        qpad[:, cy + 2 + t] = yhi[t * wide : (t + 1) * wide]
    gpad[1 : cx + 1, 1 : cy + 1] = pg[...]
    _, (glo, ghi) = x_faces(xa, xb, (2 * cy + 2, 2 * cz, c), (cy, cz, c))
    gpad[0, 1 : cy + 1] = glo
    gpad[cx + 1, 1 : cy + 1] = ghi
    gpad[:, 0] = ylo[2 * wide :]
    gpad[:, cy + 1] = yhi[2 * wide :]
    def both(ref, x, j):
        return jnp.concatenate([ref[x, j : j + 2], ref[x, cy + j : cy + 2 + j]], axis=0).reshape(4 * cz, -1)

    planes = range(cx + 2)
    taps = [
        jnp.concatenate([both(qpad, x + i, j) for x in planes], axis=0) for i in range(3) for j in range(3)
    ]
    grads = jnp.concatenate([both(gpad, x, 0) for x in planes], axis=0)
    out, act = coarse_part(taps, grads, wb, bias, wm, cz)
    out, act = (v.reshape(cx + 2, 4, cz, c2) for v in (out, act))
    slope[:, 0:2] = out[:, 0:2]
    slope[:, cy : cy + 2] = out[:, 2:4]
    slope[:, 2:cy] = slope_mid[...]
    coarse[:, 0] = act[1 : cx + 1, 1]
    coarse[:, cy - 1] = act[1 : cx + 1, 2]
    coarse[:, 1 : cy - 1] = coarse_mid[...]
    cells = cx * cy * cz
    mid = slope[1 : cx + 1, 1 : cy + 1].reshape(cells, c2)
    wide_mid = mid.astype(F32)
    st[pl.ds(0, c2), :] = shift_rows(wide_mid, -1, cz).astype(BF16).T
    st[pl.ds(c2, c2), :] = mid.T
    st[pl.ds(2 * c2, c2), :] = shift_rows(wide_mid, 1, cz).astype(BF16).T

    def window(t):
        if t == 9:
            return jnp.ones((cells, c), BF16)
        i, j = 1 + t // 3, 1 + t % 3
        return qpad[i : i + cx, j : j + cy].reshape(cells, c)

    for t in range(0, 10, 2):
        acc[:, pl.ds(t * c, 2 * c)] = jnp.dot(
            st[...], jnp.concatenate([window(t), window(t + 1)], axis=1), preferred_element_type=F32
        ).astype(BF16)
    ct[...] = jnp.dot(
        coarse[...].reshape(cells, c2).T, pg[...].reshape(cells, c), preferred_element_type=F32
    ).astype(BF16)
    cbias[...] = acc[pl.ds(c2, c2), pl.ds(9 * c, c)]
    per = c2 // n

    def piece(s, t):
        if t == 27:
            return ct[pl.ds(s * per, per), :]
        k, tap = t // 9, t % 9
        return acc[pl.ds(k * c2 + s * per, per), pl.ds(tap * c, c)]

    spread(keep, send, n, 28, piece)


def back_body(n, slope, w, cot, ds, ds_a, ds_b, own, xa, xb, cbias, keep, send, up, st, acc):
    bx, by, bz, c = cot.shape
    cx, cy, cz = bx // 2, by // 2, bz // 2
    c2 = slope.shape[3]
    cells = cx * cy * cz
    total = jnp.zeros((cells, 3 * c), F32)
    for i in range(3):
        for j in range(3):
            tap = slope[2 - i : 2 - i + cx, 2 - j : 2 - j + cy].reshape(cells, c2)
            total = total + lax.dot_general(
                tap,
                w[i, j].reshape(3 * c, c2),
                (((1,), (1,)), ((), ())),
                preferred_element_type=F32,
            )
    pooled = (
        total[:, c : 2 * c]
        + shift_rows(total[:, :c], -1, cz)
        + shift_rows(total[:, 2 * c :], 1, cz)
    ) * 0.125
    up[pl.ds(0, cells, stride=2), :] = pooled
    up[pl.ds(1, cells, stride=2), :] = pooled
    rows = by * bz
    edges = get_faces(bit_of("grp") == 1, ds_a, ds_b)
    halo, _ = x_faces(xa, xb, (by + 2, bz, c), (cy, cz, c))
    for x in range(bx):
        base = up[pl.ds((x // 2) * cy * bz, cy * bz), :].reshape(cy, 1, bz, c)
        fine = cot[x].astype(F32).reshape(cy, 2, bz, c) + base
        gain = ds[x - 1] if 0 < x < bx - 1 else edges[x // (bx - 1)]
        fs = (fine.reshape(rows, c) * gain.reshape(rows, c)).astype(BF16)
        wide = fs.astype(F32)
        st[pl.ds(0, c), pl.ds(x * rows, rows)] = shift_rows(wide, -1, bz).astype(BF16).T
        st[pl.ds(c, c), pl.ds(x * rows, rows)] = fs.T
        st[pl.ds(2 * c, c), pl.ds(x * rows, rows)] = shift_rows(wide, 1, bz).astype(BF16).T

    def window(t, x):
        if t == 9:
            return jnp.ones((rows, c), BF16)
        x, j = x + t // 3 - 1, t % 3
        plane = own[x, j : j + by] if 0 <= x < bx else halo[int(x == bx)][j : j + by]
        return plane.reshape(rows, c)

    for t in range(0, 10, 2):
        total = jnp.zeros((3 * c, 2 * c), F32)
        for first in range(0, bx, 1):
            pairs = [jnp.concatenate([window(t, x), window(t + 1, x)], axis=1) for x in range(first, first + 1)]
            total = total + jnp.dot(
                st[:, pl.ds(first * rows, 1 * rows)],
                jnp.concatenate(pairs, axis=0),
                preferred_element_type=F32,
            )
        acc[:, pl.ds(t * c, 2 * c)] = total.astype(BF16)
    per, cper = c // n, c2 // n
    lane = lax.broadcasted_iota(jnp.int32, (per, c), 1)

    def piece(s, t):
        if t == 27:
            bias = acc[pl.ds(c + s * per, per), pl.ds(9 * c, c)].astype(F32)
            one = cbias[pl.ds(s * cper, per), :].astype(F32)
            two = cbias[pl.ds(s * cper + per, per), :].astype(F32)
            return jnp.where(lane == 0, bias, jnp.where(lane == 1, one, two)).astype(BF16)
        k, tap = t // 9, t % 9
        return acc[pl.ds(k * c + s * per, per), pl.ds(tap * c, c)]

    spread(keep, send, n, 28, piece)


def merge_body(hidden, hid_a, hid_b, coarse, wm, out, tmp):
    bx, by, bz, c = out.shape
    cx, cy, cz = bx // 2, by // 2, bz // 2
    c2 = coarse.shape[3]
    cells = cx * cy * cz
    proj = jnp.dot(coarse[...].reshape(cells, c2), wm[...], preferred_element_type=F32)
    tmp[pl.ds(0, cells, stride=2), :] = proj
    tmp[pl.ds(1, cells, stride=2), :] = proj
    edges = get_faces(bit_of("grp") == 1, hid_a, hid_b)
    for x in range(bx):
        base = tmp[pl.ds((x // 2) * cy * bz, cy * bz), :].reshape(cy, 1, bz, c)
        hid = hidden[x - 1] if 0 < x < bx - 1 else edges[x // (bx - 1)]
        total = hid.astype(F32).reshape(cy, 2, bz, c) + base
        out[x] = total.astype(BF16).reshape(by, bz, c)


def swap_faces(first, second, axis):
    n = lax.axis_size(axis)
    one = [p for i in range(0, n - 1, 2) for p in ((i, i + 1), (i + 1, i))]
    two = [p for i in range(1, n - 1, 2) for p in ((i, i + 1), (i + 1, i))]
    got = lax.ppermute(second, axis, two)
    return lax.ppermute(first, axis, one), got


def split4_body(keep, got, own, over_sub, over_grp, over_both):
    g, s = bit_of("grp"), bit_of("sub", 1)

    def part(a, b):
        return (keep[a, :, b].astype(F32) + got[a, :, b].astype(F32)).astype(BF16)

    over_both[...] = part(1 - s, 1 - g)
    over_sub[...] = part(1 - s, g)
    over_grp[...] = part(s, 1 - g)
    own[...] = part(s, g)


def total_of(parts):
    return sum(p.astype(F32) for p in parts).astype(BF16)


def halves(pair, bit):
    return jnp.where(bit == 1, pair[1], pair[0]), jnp.where(bit == 1, pair[0], pair[1])


def partners(value, grp_mask, sub_mask):
    n_grp, n_sub = lax.axis_size("grp"), lax.axis_size("sub")
    pairs = [
        (g * n_sub + s, (g ^ grp_mask) * n_sub + (s ^ sub_mask))
        for g in range(n_grp)
        for s in range(n_sub)
    ]
    return lax.ppermute(value, ("grp", "sub"), pairs)


def split_sum(parts, bit):
    rows, c = parts[0].shape
    return halves(total_of([p.reshape(2, rows // 2, c) for p in parts]), bit)


def grp_bits():
    return lax.axis_size("grp").bit_length() - 1


def cores(send):
    return partners(send, 0, 1)


def spread_sum(keep, got):
    half, rows, c = keep.shape
    rest = half // 2
    shape = (2, rest, 2, rows // 2, c)
    out = ((rest, rows // 2, c), BF16)
    return call(split4_body, "split", (keep.reshape(shape), got.reshape(shape)), [out] * 4, (), 1)


def cross(own, over_sub, over_grp, over_both):
    return [own, partners(over_sub, 0, 2), partners(over_both, 1, 2), partners(over_grp, 1, 0)]


def split_body(count, axis, bit, *refs):
    mine = bit_of(axis, bit)

    def part(at):
        return sum(p[at].astype(F32) for p in refs[:count]).astype(BF16)

    refs[count + 1][...] = part(1 - mine)
    refs[count][...] = part(mine)


def sum_body(count, *refs):
    refs[count][...] = sum(p[...].astype(F32) for p in refs[:count]).astype(BF16)


def split_sum_kernel(parts, axis, bit, name):
    rows, c = parts[0].shape
    half = ((rows // 2, c), BF16)
    shaped = [p.reshape(2, rows // 2, c) for p in parts]
    return call(functools.partial(split_body, len(parts), axis, bit), name, shaped, [half, half], (), 0.8)


def sum_kernel(parts, name):
    out = [(parts[0].shape, BF16)]
    return call(functools.partial(sum_body, len(parts)), name, parts, out, (), 0.5)[0]


def finish_sum(parts, places, name, kernels):
    rest, rows, c = parts[0].shape
    parts = [p.reshape(rest * rows, c) for p in parts]
    for bit in range(2, lax.axis_size("sub").bit_length() - 1):
        keep, send = split_sum(parts, places[grp_bits() + bit])
        parts = [keep, partners(send, 0, 1 << bit)]
    parts = yield parts
    bits = [0]
    last = grp_bits() - 1
    for bit in range(1, last + 1):
        mask = 1 << bit
        if bit == 1 and bit < last and parts[0].shape[0] % 32 == 0:
            if "half" in kernels:
                keep, send = split_sum_kernel(parts, "grp", bit, name + "_half")
            else:
                keep, send = split_sum(parts, places[bit])
            keep, send = yield keep, send
            parts = yield keep, partners(send, mask, 0)
            bits.append(bit)
        else:
            total = sum_kernel(parts, name + "_sum") if "sum" in kernels else total_of(parts)
            total = yield total
            parts = yield total, partners(total, mask, 0)
    total = sum_kernel(parts, name + "_total") if "total" in kernels else total_of(parts)
    pieces = [total]
    for which in range(1, 2 ** len(bits)):
        pieces.append(partners(total, sum(1 << bits[b] for b in range(len(bits)) if which >> b & 1), 0))
    return pieces


def step(run, value):
    try:
        return run.send(value), None
    except StopIteration as done:
        return None, done.value


def side_by_side(ahead, behind, arrived):
    first, first_done = step(ahead, step(ahead, None)[0])
    first, arrived = lax.optimization_barrier((first, arrived))
    first, first_done = step(ahead, first)
    behind = behind(arrived)
    second, second_done = step(behind, None)
    while second_done is None:
        if first_done is None:
            first, first_done = step(ahead, first)
        if first_done is None:
            first, first_done = step(ahead, first)
        second, second_done = step(behind, second)
        if second_done is None:
            second, second_done = step(behind, second)
            if first_done is None and second_done is None:
                first, second = lax.optimization_barrier((first, second))
    return first_done, second_done


def last_body(count, *refs):
    pieces, kernel, extra, rows = refs[:count], refs[count], refs[count + 1], refs[-1]
    size = pieces[0].shape[0]
    per = extra.shape[0] if len(refs) == count + 3 else kernel.shape[3]
    mine = bit_of("grp") if count == 2 else 2 * bit_of("grp") + bit_of("grp", 1)
    for which in range(count):
        mask = which if count == 2 else 2 * (which & 1) + (which >> 1)
        rows[mine ^ mask] = pieces[which][...]

    def block(t):
        at, off = t * per // size, t * per % size
        if off + per <= size:
            return rows[at, pl.ds(off, per)].astype(F32)
        first = size - off
        return jnp.concatenate([rows[at, pl.ds(off, first)], rows[at + 1, pl.ds(0, per - first)]], axis=0).astype(F32)

    for t in range(27):
        kernel[(t // 3) % 3, t % 3, t // 9] = block(t)
    if len(refs) == count + 3:
        extra[...] = block(27)
    else:
        turned = block(27).T
        extra[...] = turned[0:1]
        refs[count + 2][:, pl.ds(0, per)] = turned[1:2]
        refs[count + 2][:, pl.ds(per, per)] = turned[2:3]


def last(pieces, per, outs, name):
    count = len(pieces)
    size, c = pieces[0].shape
    kernel, *rest = call(
        functools.partial(last_body, count),
        name,
        tuple(pieces),
        [((3, 3, 3, per, c), F32), *outs],
        [pltpu.VMEM((count, size, c), BF16)],
        1,
    )
    return jnp.swapaxes(kernel, 3, 4), *rest


def per_device(field, cotangent, fine_kernel, fine_bias, coarse_kernel, coarse_bias, merge_weight):
    n = lax.axis_size("sub")
    bx, by, bz, c = field.shape
    cx, cy, cz = bx // 2, by // 2, bz // 2
    c2 = merge_weight.shape[0]
    odd = bit_of("sub") == 1
    sa = jnp.where(odd, field[:, 0], field[:, by - 1])
    sb = jnp.where(odd, field[:, by - 1], field[:, 0])
    ya, yb = swap_faces(sa, sb, "sub")
    count = grp_bits() + n.bit_length() - 1
    pg, places = call(
        cubes_body,
        "cubes",
        (cotangent,),
        [((cx, cy, cz, c), BF16), ((count, 1, c), jnp.int32)],
        [pltpu.VMEM((cx * cy * bz, c), F32)],
    )
    face = (((by + 2) * bz + cy * cz, c), BF16)
    own, ta, tb = call(
        turn_body, "turn", (field, ya, yb, pg), [((bx, by + 2, bz, c), BF16), face, face]
    )
    xa, xb = swap_faces(ta, tb, "grp")
    bias = fine_bias.reshape(1, c)
    hidden, ds, pool_in, wb = call(
        inner_body,
        "inner",
        (own, fine_kernel, bias),
        [
            ((bx - 2, by, bz, c), BF16),
            ((bx - 2, by, bz, c), F32),
            ((cx - 2, cy, cz, c), BF16),
            ((9 * c, 3 * c), BF16),
        ],
        [pltpu.VMEM((cy * bz, c), F32)],
        6,
    )

    def edge(second, face):
        return call(
            functools.partial(edge_body, second),
            "edge",
            (own, face, wb, bias, hidden, pool_in),
            [
                ((by, bz, c), BF16),
                ((by, bz, c), F32),
                ((cy, cz, c), BF16),
                ((2, cy, cz, c), BF16),
            ],
            [pltpu.VMEM((cy * bz, c), F32)],
            1,
        )

    hid_a, ds_a, pool_a, pa = edge(False, xa)
    hid_b, ds_b, pool_b, pb = edge(True, xb)
    pxa, pxb = swap_faces(pa, pb, "grp")
    (taps,) = call(taps_body, "taps", (coarse_kernel,), [((9 * c, 3 * c2), BF16)], (), 0.5)
    pxa, taps = lax.optimization_barrier((pxa, taps))
    face = ((2 * (cx + 4) + cx + 2, cz, c), BF16)
    pooled = (pool_in, pool_a, pool_b)
    qa, qb = call(turn2_body, "turn2", (*pooled, pg, pxa, pxb, xa, xb), [face, face])
    pya, pyb = swap_faces(qa, qb, "sub")
    bias2 = coarse_bias.reshape(1, c2)
    pyb, pya = lax.optimization_barrier((pyb, pya))
    slope_mid, coarse_mid = call(
        mid_body,
        "mid",
        (*pooled, pxa, pxb, xa, xb, pg, taps, bias2, merge_weight),
        [((cx + 2, cy - 2, cz, c2), BF16), ((cx, cy - 2, cz, c2), BF16)],
        [pltpu.VMEM((cx + 4, cy, cz, c), BF16), pltpu.VMEM((cx + 2, cy, cz, c), BF16)],
        2,
    )
    cells = cx * cy * cz
    part = (n // 2, 28 * (c2 // n), c)
    slope, coarse, ckeep, csend, cbias = call(
        functools.partial(coarse_body, n),
        "coarse",
        (*pooled, pxa, pxb, pya, pyb, xa, xb, pg, taps, bias2, merge_weight, slope_mid, coarse_mid),
        [
            ((cx + 2, cy + 2, cz, c2), BF16),
            ((cx, cy, cz, c2), BF16),
            (part, BF16),
            (part, BF16),
            ((c2, c), BF16),
        ],
        [
            pltpu.VMEM((cx + 4, cy + 4, cz, c), BF16),
            pltpu.VMEM((cx + 2, cy + 2, cz, c), BF16),
            pltpu.VMEM((3 * c2, cells), BF16),
            pltpu.VMEM((3 * c2, 10 * c), BF16),
            pltpu.VMEM((c2, c), BF16),
        ],
        6,
    )
    cgot = cores(csend)
    (output,) = call(
        merge_body,
        "merge",
        (hidden, hid_a, hid_b, coarse, merge_weight),
        [((bx, by, bz, c), BF16)],
        [pltpu.VMEM((cx * cy * bz, c), F32)],
        2,
    )
    output, cgot = lax.optimization_barrier((output, cgot))
    csent = spread_sum(ckeep, cgot)
    slope, csent = lax.optimization_barrier((slope, csent))
    cparts = cross(*csent)
    voxels = bx * by * bz
    part = (n // 2, 28 * (c // n), c)
    fkeep, fsend = call(
        functools.partial(back_body, n),
        "back",
        (slope, coarse_kernel, cotangent, ds, ds_a, ds_b, own, xa, xb, cbias),
        [(part, BF16), (part, BF16)],
        [
            pltpu.VMEM((cx * cy * bz, c), F32),
            pltpu.VMEM((3 * c, voxels), BF16),
            pltpu.VMEM((3 * c, 10 * c), BF16),
        ],
        10,
    )

    coarse_sum, fine_sum = side_by_side(
        finish_sum(cparts, places, "coarse", ("half", "sum")),
        lambda got: finish_sum(cross(*spread_sum(fkeep, jnp.stack(got))), places, "fine", ("half", "sum")),
        [cores(part) for part in fsend],
    )
    per, cper = c // n, c2 // n
    grad_coarse, grad_merge = last(coarse_sum, cper, [((cper, c), F32)], "coarse_last")
    fine_sum, grad_merge = lax.optimization_barrier((fine_sum, grad_merge))
    biases = [((1, per), F32), ((1, cper), F32)]
    grad_fine, bias, coarse_sums = last(fine_sum, per, biases, "fine_last")
    return (output, grad_fine, bias[0], grad_coarse, coarse_sums[0], grad_merge)


def solution(mesh):
    in_specs = (P("grp", "sub", None, None), P("grp", "sub", None, None), P(), P(), P(), P(), P())
    out_specs = (
        P("grp", "sub", None, None),
        P(None, None, None, None, "sub"),
        P("sub"),
        P(None, None, None, None, "sub"),
        P("sub"),
        P("sub", None),
    )
    return jax.shard_map(
        per_device, mesh=mesh, in_specs=in_specs, out_specs=out_specs, check_vma=False
    )
```

```python
import functools

import jax
import jax.numpy as jnp
from jax import lax
from jax.experimental import pallas as pl
from jax.experimental.pallas import tpu as pltpu
from jax.sharding import PartitionSpec as P

F32 = jnp.float32
BF16 = jnp.bfloat16
VMEM_LIMIT = 32 * 1024 * 1024


def bit_of(axis, bit=0):
    return (lax.axis_index(axis) >> bit) & 1


def call(body, name, args, outs, scratch=(), micros=1):
    return pl.pallas_call(
        body,
        name=name,
        out_shape=[jax.ShapeDtypeStruct(s, t) for s, t in outs],
        in_specs=[pl.BlockSpec(memory_space=pltpu.VMEM) for _ in args],
        out_specs=[pl.BlockSpec(memory_space=pltpu.VMEM) for _ in outs],
        scratch_shapes=list(scratch),
        compiler_params=pltpu.CompilerParams(vmem_limit_bytes=VMEM_LIMIT),
        cost_estimate=pl.CostEstimate(
            flops=int(micros * 1e9), bytes_accessed=0, transcendentals=0
        ),
    )(*args)


def put_faces(odd, first, second, low, high):
    first[...] = jnp.where(odd, low, high)
    second[...] = jnp.where(odd, high, low)


def get_faces(odd, first, second):
    a, b = first[...], second[...]
    return jnp.where(odd, a, b), jnp.where(odd, b, a)


def sum_cube(rows, planes, ref):
    half = rows // 2
    ref[pl.ds(0, rows), :] = planes
    return ref[pl.ds(0, half, stride=2), :] + ref[pl.ds(1, half, stride=2), :]


def shift_rows(value, step, depth):
    rows = value.shape[0]
    moved = pltpu.roll(value, step % rows, 0)
    place = lax.broadcasted_iota(jnp.int32, value.shape, 0) % depth
    edge = 0 if step == 1 else depth - 1
    return jnp.where(place == edge, 0.0, moved)


def sigmoid(value):
    return 0.5 + 0.5 * jnp.tanh(0.5 * value)


def turn_body(field, ya, yb, pg, own, out_a, out_b):
    bx, by, bz, c = field.shape
    cx, cy, cz, _ = pg.shape
    ylo, yhi = get_faces(bit_of("sub") == 1, ya, yb)
    own[:, 1 : by + 1] = field[...]
    own[:, 0] = ylo
    own[:, by + 1] = yhi

    def side(x, at):
        return jnp.concatenate([own[x].reshape((by + 2) * bz, c), pg[at].reshape(cy * cz, c)], axis=0)

    put_faces(bit_of("grp") == 1, out_a, out_b, side(0, 0), side(bx - 1, cx - 1))


def x_faces(xa, xb, fine, coarse):
    by, bz, c = fine
    cy, cz, _ = coarse
    lo, hi = get_faces(bit_of("grp") == 1, xa, xb)
    rows = by * bz
    return (
        (lo[:rows].reshape(by, bz, c), hi[:rows].reshape(by, bz, c)),
        (lo[rows:].reshape(cy, cz, c), hi[rows:].reshape(cy, cz, c)),
    )


def fine_plane(three, wb, bias, by):
    _, bz, c = three[0].shape
    rows = by * bz * (len(three) - 2)
    taps = [
        jnp.concatenate([plane[j : j + by].reshape(by * bz, c) for plane in three[i : len(three) - 2 + i]], axis=0)
        for i in range(3)
        for j in range(3)
    ]
    part = jnp.dot(jnp.concatenate(taps, axis=1), wb[...], preferred_element_type=F32)
    pre = (
        part[:, c : 2 * c]
        + shift_rows(part[:, :c], 1, bz)
        + shift_rows(part[:, 2 * c :], -1, bz)
        + bias[...]
    )
    sig = sigmoid(pre)
    hid = (pre * sig).astype(BF16).reshape(-1, by, bz, c)
    return hid, (sig * (1.0 + pre * (1.0 - sig))).reshape(-1, by, bz, c)


def pool(one, two, tmp):
    by, bz, c = one.shape
    cy = by // 2
    both = jnp.sum((one.astype(F32) + two.astype(F32)).reshape(cy, 2, bz, c), axis=1)
    total = sum_cube(cy * bz, both.reshape(cy * bz, c), tmp)
    return (total / 8.0).astype(BF16).reshape(cy, bz // 2, c)


def inner_body(own, w, bias, hidden, ds, pooled, wb, tmp):
    by, c = own.shape[1] - 2, own.shape[3]
    for i in range(3):
        for j in range(3):
            for k in range(3):
                wb[pl.ds((3 * i + j) * c, c), pl.ds(k * c, c)] = w[i, j, k]

    def plane(x, carry):
        hid, slope = fine_plane([own[3 * x + k] for k in range(5)], wb, bias, by)
        hidden[pl.ds(3 * x, 3)], ds[pl.ds(3 * x, 3)] = hid, slope
        return carry

    lax.fori_loop(0, hidden.shape[0] // 3, plane, 0)
    for q in range(pooled.shape[0]):
        pooled[q] = pool(hidden[2 * q + 1], hidden[2 * q + 2], tmp)


def edge_body(second, own, face, wb, bias, hid_in, pool_in, hidden, ds, pooled, out, tmp):
    bx, by, bz, c = own.shape
    cx = bx // 2
    low = bit_of("grp") == (0 if second else 1)
    halo = face[pl.ds(0, by * bz), :].reshape(by, bz, c)
    near, inside = own[jnp.where(low, 0, bx - 1)], own[jnp.where(low, 1, bx - 2)]
    three = [jnp.where(low, halo, inside), near, jnp.where(low, inside, halo)]
    hid, slope = fine_plane(three, wb, bias, by - 2)
    hidden[...], ds[...] = hid[0], slope[0]
    pooled[...] = pool(hidden[...], hid_in[jnp.where(low, 0, bx - 3)], tmp)
    out[0] = jnp.where(low, pooled[...], pool_in[cx - 3])
    out[1] = jnp.where(low, pool_in[0], pooled[...])


def taps_body(w, wb):
    c, c2 = w.shape[3], w.shape[4]
    for i in range(3):
        for j in range(3):
            for k in range(3):
                wb[pl.ds((3 * i + j) * c, c), pl.ds(k * c2, c2)] = w[i, j, k]


def cubes_body(cot, pg, bits, tmp):
    bx, by, bz, c = cot.shape
    cx, cy, cz = bx // 2, by // 2, bz // 2
    total = jnp.sum(cot[...].astype(F32).reshape(cx, 2, cy, 2, bz, c), axis=(1, 3))
    grad = sum_cube(cx * cy * bz, total.reshape(cx * cy * bz, c), tmp).astype(BF16)
    pg[...] = grad.reshape(cx, cy, cz, c)
    first = grp_bits()
    for k in range(bits.shape[0]):
        value = bit_of("grp", k) if k < first else bit_of("sub", k - first)
        bits[k] = jnp.full(bits.shape[1:], value, jnp.int32)


def pooled_of(pool_in, pool_a, pool_b):
    lo, hi = get_faces(bit_of("grp") == 1, pool_a, pool_b)
    return jnp.concatenate([lo[None], pool_in[...], hi[None]], axis=0)


def turn2_body(pool_in, pool_a, pool_b, pg, ra, rb, xa, xb, out_a, out_b):
    cy, cz, c = pool_a.shape
    pooled = pooled_of(pool_in, pool_a, pool_b)
    xlo, xhi = get_faces(bit_of("grp") == 1, ra, rb)
    _, (glo, ghi) = x_faces(xa, xb, (2 * cy + 2, 2 * cz, c), (cy, cz, c))

    def side(y, last):
        two = [jnp.concatenate([xlo[:, at], pooled[:, at], xhi[:, at]], axis=0) for at in (y, y + 1)]
        one = jnp.concatenate([glo[None, last], pg[:, last], ghi[None, last]], axis=0)
        return jnp.concatenate([*two, one], axis=0)

    put_faces(bit_of("sub") == 1, out_a, out_b, side(0, 0), side(cy - 2, cy - 1))


def reverse_bits(value, count):
    out = 0
    for _ in range(count):
        out, value = out * 2 + value % 2, value // 2
    return out


def spread(keep, send, n, blocks, piece):
    bits = n.bit_length() - 1
    half = n // 2
    for b in (0, 1):

        @pl.when(bit_of("sub") == b)
        def _():
            for s in range(n):
                target = keep if s % 2 == b else send
                for t in range(blocks):
                    value = piece(s, t)
                    size = value.shape[0]
                    target[reverse_bits(s, bits) % half, pl.ds(t * size, size)] = value


def coarse_part(taps, grads, wb, bias, wm, cz):
    c2 = wm.shape[0]
    part = jnp.dot(jnp.concatenate(taps, axis=1), wb[...], preferred_element_type=F32)
    pre = (
        part[:, c2 : 2 * c2]
        + shift_rows(part[:, :c2], 1, cz)
        + shift_rows(part[:, 2 * c2 :], -1, cz)
        + bias[...]
    )
    sig = sigmoid(pre)
    back = lax.dot_general(grads, wm[...], (((1,), (1,)), ((), ())), preferred_element_type=F32)
    return (back * (sig * (1.0 + pre * (1.0 - sig)))).astype(BF16), (pre * sig).astype(BF16)


def mid_body(pool_in, pool_a, pool_b, ra, rb, xa, xb, pg, wb, bias, wm, slope, coarse, qx, gx):
    cx, cy, cz, c = pg.shape
    c2 = wm.shape[0]
    qx[0:2], qx[cx + 2 : cx + 4] = get_faces(bit_of("grp") == 1, ra, rb)
    qx[2 : cx + 2] = pooled_of(pool_in, pool_a, pool_b)
    _, (gx[0], gx[cx + 1]) = x_faces(xa, xb, (2 * cy + 2, 2 * cz, c), (cy, cz, c))
    gx[1 : cx + 1] = pg[...]
    for first in range(0, cx + 2, 3):
        planes = range(first, first + 3)
        taps = [
            jnp.concatenate([qx[x + i, j : j + cy - 2].reshape(-1, c) for x in planes], axis=0)
            for i in range(3)
            for j in range(3)
        ]
        grads = jnp.concatenate([gx[x, 1 : cy - 1].reshape(-1, c) for x in planes], axis=0)
        out, act = coarse_part(taps, grads, wb, bias, wm, cz)
        slope[first : first + 3] = out.reshape(3, cy - 2, cz, c2)
        act = act.reshape(3, cy - 2, cz, c2)
        for h, x in enumerate(planes):
            if 1 <= x <= cx:
                coarse[x - 1] = act[h]


def coarse_body(
    n, pool_in, pool_a, pool_b, ra, rb, ua, ub, xa, xb, pg, wb, bias, wm, slope_mid, coarse_mid,
    slope, coarse, keep, send, cbias, qpad, gpad, st, acc, ct,
):
    cx, cy, cz, c = pg.shape
    c2 = wm.shape[0]
    xlo, xhi = get_faces(bit_of("grp") == 1, ra, rb)
    ylo, yhi = get_faces(bit_of("sub") == 1, ua, ub)
    qpad[2 : cx + 2, 2 : cy + 2] = pooled_of(pool_in, pool_a, pool_b)
    qpad[0:2, 2 : cy + 2] = xlo
    qpad[cx + 2 : cx + 4, 2 : cy + 2] = xhi
    wide = cx + 4
    for t in (0, 1):
        qpad[:, t] = ylo[t * wide : (t + 1) * wide]
        qpad[:, cy + 2 + t] = yhi[t * wide : (t + 1) * wide]
    gpad[1 : cx + 1, 1 : cy + 1] = pg[...]
    _, (glo, ghi) = x_faces(xa, xb, (2 * cy + 2, 2 * cz, c), (cy, cz, c))
    gpad[0, 1 : cy + 1] = glo
    gpad[cx + 1, 1 : cy + 1] = ghi
    gpad[:, 0] = ylo[2 * wide :]
    gpad[:, cy + 1] = yhi[2 * wide :]
    def both(ref, x, j):
        return jnp.concatenate([ref[x, j : j + 2], ref[x, cy + j : cy + 2 + j]], axis=0).reshape(4 * cz, -1)

    planes = range(cx + 2)
    taps = [
        jnp.concatenate([both(qpad, x + i, j) for x in planes], axis=0) for i in range(3) for j in range(3)
    ]
    grads = jnp.concatenate([both(gpad, x, 0) for x in planes], axis=0)
    out, act = coarse_part(taps, grads, wb, bias, wm, cz)
    out, act = (v.reshape(cx + 2, 4, cz, c2) for v in (out, act))
    slope[:, 0:2] = out[:, 0:2]
    slope[:, cy : cy + 2] = out[:, 2:4]
    slope[:, 2:cy] = slope_mid[...]
    coarse[:, 0] = act[1 : cx + 1, 1]
    coarse[:, cy - 1] = act[1 : cx + 1, 2]
    coarse[:, 1 : cy - 1] = coarse_mid[...]
    cells = cx * cy * cz
    mid = slope[1 : cx + 1, 1 : cy + 1].reshape(cells, c2)
    wide_mid = mid.astype(F32)
    st[pl.ds(0, c2), :] = shift_rows(wide_mid, -1, cz).astype(BF16).T
    st[pl.ds(c2, c2), :] = mid.T
    st[pl.ds(2 * c2, c2), :] = shift_rows(wide_mid, 1, cz).astype(BF16).T

    def window(t):
        if t == 9:
            return jnp.ones((cells, c), BF16)
        i, j = 1 + t // 3, 1 + t % 3
        return qpad[i : i + cx, j : j + cy].reshape(cells, c)

    for t in range(0, 10, 2):
        acc[:, pl.ds(t * c, 2 * c)] = jnp.dot(
            st[...], jnp.concatenate([window(t), window(t + 1)], axis=1), preferred_element_type=F32
        ).astype(BF16)
    ct[...] = jnp.dot(
        coarse[...].reshape(cells, c2).T, pg[...].reshape(cells, c), preferred_element_type=F32
    ).astype(BF16)
    cbias[...] = acc[pl.ds(c2, c2), pl.ds(9 * c, c)]
    per = c2 // n

    def piece(s, t):
        if t == 27:
            return ct[pl.ds(s * per, per), :]
        k, tap = t // 9, t % 9
        return acc[pl.ds(k * c2 + s * per, per), pl.ds(tap * c, c)]

    spread(keep, send, n, 28, piece)


def back_body(n, slope, w, cot, ds, ds_a, ds_b, own, xa, xb, cbias, keep, send, up, st, acc):
    bx, by, bz, c = cot.shape
    cx, cy, cz = bx // 2, by // 2, bz // 2
    c2 = slope.shape[3]
    cells = cx * cy * cz
    total = jnp.zeros((cells, 3 * c), F32)
    for i in range(3):
        for j in range(3):
            tap = slope[2 - i : 2 - i + cx, 2 - j : 2 - j + cy].reshape(cells, c2)
            total = total + lax.dot_general(
                tap,
                w[i, j].reshape(3 * c, c2),
                (((1,), (1,)), ((), ())),
                preferred_element_type=F32,
            )
    pooled = (
        total[:, c : 2 * c]
        + shift_rows(total[:, :c], -1, cz)
        + shift_rows(total[:, 2 * c :], 1, cz)
    ) * 0.125
    up[pl.ds(0, cells, stride=2), :] = pooled
    up[pl.ds(1, cells, stride=2), :] = pooled
    rows = by * bz
    edges = get_faces(bit_of("grp") == 1, ds_a, ds_b)
    halo, _ = x_faces(xa, xb, (by + 2, bz, c), (cy, cz, c))
    for x in range(bx):
        base = up[pl.ds((x // 2) * cy * bz, cy * bz), :].reshape(cy, 1, bz, c)
        fine = cot[x].astype(F32).reshape(cy, 2, bz, c) + base
        gain = ds[x - 1] if 0 < x < bx - 1 else edges[x // (bx - 1)]
        fs = (fine.reshape(rows, c) * gain.reshape(rows, c)).astype(BF16)
        wide = fs.astype(F32)
        st[pl.ds(0, c), pl.ds(x * rows, rows)] = shift_rows(wide, -1, bz).astype(BF16).T
        st[pl.ds(c, c), pl.ds(x * rows, rows)] = fs.T
        st[pl.ds(2 * c, c), pl.ds(x * rows, rows)] = shift_rows(wide, 1, bz).astype(BF16).T

    def window(t, x):
        if t == 9:
            return jnp.ones((rows, c), BF16)
        x, j = x + t // 3 - 1, t % 3
        plane = own[x, j : j + by] if 0 <= x < bx else halo[int(x == bx)][j : j + by]
        return plane.reshape(rows, c)

    for t in range(0, 10, 2):
        total = jnp.zeros((3 * c, 2 * c), F32)
        for first in range(0, bx, 1):
            pairs = [jnp.concatenate([window(t, x), window(t + 1, x)], axis=1) for x in range(first, first + 1)]
            total = total + jnp.dot(
                st[:, pl.ds(first * rows, 1 * rows)],
                jnp.concatenate(pairs, axis=0),
                preferred_element_type=F32,
            )
        acc[:, pl.ds(t * c, 2 * c)] = total.astype(BF16)
    per, cper = c // n, c2 // n
    lane = lax.broadcasted_iota(jnp.int32, (per, c), 1)

    def piece(s, t):
        if t == 27:
            bias = acc[pl.ds(c + s * per, per), pl.ds(9 * c, c)].astype(F32)
            one = cbias[pl.ds(s * cper, per), :].astype(F32)
            two = cbias[pl.ds(s * cper + per, per), :].astype(F32)
            return jnp.where(lane == 0, bias, jnp.where(lane == 1, one, two)).astype(BF16)
        k, tap = t // 9, t % 9
        return acc[pl.ds(k * c + s * per, per), pl.ds(tap * c, c)]

    spread(keep, send, n, 28, piece)


def merge_body(hidden, hid_a, hid_b, coarse, wm, out, tmp):
    bx, by, bz, c = out.shape
    cx, cy, cz = bx // 2, by // 2, bz // 2
    c2 = coarse.shape[3]
    cells = cx * cy * cz
    proj = jnp.dot(coarse[...].reshape(cells, c2), wm[...], preferred_element_type=F32)
    tmp[pl.ds(0, cells, stride=2), :] = proj
    tmp[pl.ds(1, cells, stride=2), :] = proj
    edges = get_faces(bit_of("grp") == 1, hid_a, hid_b)
    for x in range(bx):
        base = tmp[pl.ds((x // 2) * cy * bz, cy * bz), :].reshape(cy, 1, bz, c)
        hid = hidden[x - 1] if 0 < x < bx - 1 else edges[x // (bx - 1)]
        total = hid.astype(F32).reshape(cy, 2, bz, c) + base
        out[x] = total.astype(BF16).reshape(by, bz, c)


def swap_faces(first, second, axis):
    n = lax.axis_size(axis)
    one = [p for i in range(0, n - 1, 2) for p in ((i, i + 1), (i + 1, i))]
    two = [p for i in range(1, n - 1, 2) for p in ((i, i + 1), (i + 1, i))]
    got = lax.ppermute(second, axis, two)
    return lax.ppermute(first, axis, one), got


def split4_body(keep, got, own, over_sub, over_grp, over_both):
    g, s = bit_of("grp"), bit_of("sub", 1)

    def part(a, b):
        return (keep[a, :, b].astype(F32) + got[a, :, b].astype(F32)).astype(BF16)

    over_both[...] = part(1 - s, 1 - g)
    over_sub[...] = part(1 - s, g)
    over_grp[...] = part(s, 1 - g)
    own[...] = part(s, g)


def total_of(parts):
    return sum(p.astype(F32) for p in parts).astype(BF16)


def halves(pair, bit):
    return jnp.where(bit == 1, pair[1], pair[0]), jnp.where(bit == 1, pair[0], pair[1])


def partners(value, grp_mask, sub_mask):
    n_grp, n_sub = lax.axis_size("grp"), lax.axis_size("sub")
    pairs = [
        (g * n_sub + s, (g ^ grp_mask) * n_sub + (s ^ sub_mask))
        for g in range(n_grp)
        for s in range(n_sub)
    ]
    return lax.ppermute(value, ("grp", "sub"), pairs)


def split_sum(parts, bit):
    rows, c = parts[0].shape
    return halves(total_of([p.reshape(2, rows // 2, c) for p in parts]), bit)


def grp_bits():
    return lax.axis_size("grp").bit_length() - 1


def cores(send):
    return partners(send, 0, 1)


def spread_sum(keep, got):
    half, rows, c = keep.shape
    rest = half // 2
    shape = (2, rest, 2, rows // 2, c)
    out = ((rest, rows // 2, c), BF16)
    return call(split4_body, "split", (keep.reshape(shape), got.reshape(shape)), [out] * 4, (), 1)


def cross(own, over_sub, over_grp, over_both):
    return [own, partners(over_sub, 0, 2), partners(over_both, 1, 2), partners(over_grp, 1, 0)]


def split_body(count, axis, bit, *refs):
    mine = bit_of(axis, bit)

    def part(at):
        return sum(p[at].astype(F32) for p in refs[:count]).astype(BF16)

    refs[count + 1][...] = part(1 - mine)
    refs[count][...] = part(mine)


def sum_body(count, *refs):
    refs[count][...] = sum(p[...].astype(F32) for p in refs[:count]).astype(BF16)


def split_sum_kernel(parts, axis, bit, name):
    rows, c = parts[0].shape
    half = ((rows // 2, c), BF16)
    shaped = [p.reshape(2, rows // 2, c) for p in parts]
    return call(functools.partial(split_body, len(parts), axis, bit), name, shaped, [half, half], (), 0.8)


def sum_kernel(parts, name):
    out = [(parts[0].shape, BF16)]
    return call(functools.partial(sum_body, len(parts)), name, parts, out, (), 0.5)[0]


def finish_sum(parts, places, name, kernels):
    rest, rows, c = parts[0].shape
    parts = [p.reshape(rest * rows, c) for p in parts]
    for bit in range(2, lax.axis_size("sub").bit_length() - 1):
        keep, send = split_sum(parts, places[grp_bits() + bit])
        parts = [keep, partners(send, 0, 1 << bit)]
    parts = yield parts
    bits = [0]
    last = grp_bits() - 1
    for bit in range(1, last + 1):
        mask = 1 << bit
        if bit == 1 and bit < last and parts[0].shape[0] % 32 == 0:
            if "half" in kernels:
                keep, send = split_sum_kernel(parts, "grp", bit, name + "_half")
            else:
                keep, send = split_sum(parts, places[bit])
            keep, send = yield keep, send
            parts = yield keep, partners(send, mask, 0)
            bits.append(bit)
        else:
            total = sum_kernel(parts, name + "_sum") if "sum" in kernels else total_of(parts)
            total = yield total
            parts = yield total, partners(total, mask, 0)
    total = sum_kernel(parts, name + "_total") if "total" in kernels else total_of(parts)
    pieces = [total]
    for which in range(1, 2 ** len(bits)):
        pieces.append(partners(total, sum(1 << bits[b] for b in range(len(bits)) if which >> b & 1), 0))
    return pieces


def step(run, value):
    try:
        return run.send(value), None
    except StopIteration as done:
        return None, done.value


def side_by_side(ahead, behind, arrived):
    first, first_done = step(ahead, step(ahead, None)[0])
    first, arrived = lax.optimization_barrier((first, arrived))
    first, first_done = step(ahead, first)
    behind = behind(arrived)
    second, second_done = step(behind, None)
    while second_done is None:
        if first_done is None:
            first, first_done = step(ahead, first)
        if first_done is None:
            first, first_done = step(ahead, first)
        second, second_done = step(behind, second)
        if second_done is None:
            second, second_done = step(behind, second)
            if first_done is None and second_done is None:
                first, second = lax.optimization_barrier((first, second))
    return first_done, second_done


def last_body(count, *refs):
    pieces, kernel, extra, rows = refs[:count], refs[count], refs[count + 1], refs[-1]
    size = pieces[0].shape[0]
    per = extra.shape[0] if len(refs) == count + 3 else kernel.shape[3]
    mine = bit_of("grp") if count == 2 else 2 * bit_of("grp") + bit_of("grp", 1)
    for which in range(count):
        mask = which if count == 2 else 2 * (which & 1) + (which >> 1)
        rows[mine ^ mask] = pieces[which][...]

    def block(t):
        at, off = t * per // size, t * per % size
        if off + per <= size:
            return rows[at, pl.ds(off, per)].astype(F32)
        first = size - off
        return jnp.concatenate([rows[at, pl.ds(off, first)], rows[at + 1, pl.ds(0, per - first)]], axis=0).astype(F32)

    for t in range(27):
        kernel[(t // 3) % 3, t % 3, t // 9] = block(t)
    if len(refs) == count + 3:
        extra[...] = block(27)
    else:
        turned = block(27).T
        extra[...] = turned[0:1]
        refs[count + 2][:, pl.ds(0, per)] = turned[1:2]
        refs[count + 2][:, pl.ds(per, per)] = turned[2:3]


def last(pieces, per, outs, name):
    count = len(pieces)
    size, c = pieces[0].shape
    kernel, *rest = call(
        functools.partial(last_body, count),
        name,
        tuple(pieces),
        [((3, 3, 3, per, c), F32), *outs],
        [pltpu.VMEM((count, size, c), BF16)],
        1,
    )
    return jnp.swapaxes(kernel, 3, 4), *rest


def per_device(field, cotangent, fine_kernel, fine_bias, coarse_kernel, coarse_bias, merge_weight):
    n = lax.axis_size("sub")
    bx, by, bz, c = field.shape
    cx, cy, cz = bx // 2, by // 2, bz // 2
    c2 = merge_weight.shape[0]
    odd = bit_of("sub") == 1
    sa = jnp.where(odd, field[:, 0], field[:, by - 1])
    sb = jnp.where(odd, field[:, by - 1], field[:, 0])
    ya, yb = swap_faces(sa, sb, "sub")
    count = grp_bits() + n.bit_length() - 1
    pg, places = call(
        cubes_body,
        "cubes",
        (cotangent,),
        [((cx, cy, cz, c), BF16), ((count, 1, c), jnp.int32)],
        [pltpu.VMEM((cx * cy * bz, c), F32)],
    )
    face = (((by + 2) * bz + cy * cz, c), BF16)
    own, ta, tb = call(
        turn_body, "turn", (field, ya, yb, pg), [((bx, by + 2, bz, c), BF16), face, face]
    )
    xa, xb = swap_faces(ta, tb, "grp")
    bias = fine_bias.reshape(1, c)
    hidden, ds, pool_in, wb = call(
        inner_body,
        "inner",
        (own, fine_kernel, bias),
        [
            ((bx - 2, by, bz, c), BF16),
            ((bx - 2, by, bz, c), F32),
            ((cx - 2, cy, cz, c), BF16),
            ((9 * c, 3 * c), BF16),
        ],
        [pltpu.VMEM((cy * bz, c), F32)],
        6,
    )

    def edge(second, face):
        return call(
            functools.partial(edge_body, second),
            "edge",
            (own, face, wb, bias, hidden, pool_in),
            [
                ((by, bz, c), BF16),
                ((by, bz, c), F32),
                ((cy, cz, c), BF16),
                ((2, cy, cz, c), BF16),
            ],
            [pltpu.VMEM((cy * bz, c), F32)],
            1,
        )

    hid_b, ds_b, pool_b, pb = edge(True, xb)
    xa, pb = lax.optimization_barrier((xa, pb))
    hid_a, ds_a, pool_a, pa = edge(False, xa)
    pxa, pxb = swap_faces(pa, pb, "grp")
    (taps,) = call(taps_body, "taps", (coarse_kernel,), [((9 * c, 3 * c2), BF16)], (), 0.5)
    pxa, taps = lax.optimization_barrier((pxa, taps))
    face = ((2 * (cx + 4) + cx + 2, cz, c), BF16)
    pooled = (pool_in, pool_a, pool_b)
    qa, qb = call(turn2_body, "turn2", (*pooled, pg, pxa, pxb, xa, xb), [face, face])
    pya, pyb = swap_faces(qa, qb, "sub")
    bias2 = coarse_bias.reshape(1, c2)
    pyb, pya = lax.optimization_barrier((pyb, pya))
    slope_mid, coarse_mid = call(
        mid_body,
        "mid",
        (*pooled, pxa, pxb, xa, xb, pg, taps, bias2, merge_weight),
        [((cx + 2, cy - 2, cz, c2), BF16), ((cx, cy - 2, cz, c2), BF16)],
        [pltpu.VMEM((cx + 4, cy, cz, c), BF16), pltpu.VMEM((cx + 2, cy, cz, c), BF16)],
        2,
    )
    cells = cx * cy * cz
    part = (n // 2, 28 * (c2 // n), c)
    slope, coarse, ckeep, csend, cbias = call(
        functools.partial(coarse_body, n),
        "coarse",
        (*pooled, pxa, pxb, pya, pyb, xa, xb, pg, taps, bias2, merge_weight, slope_mid, coarse_mid),
        [
            ((cx + 2, cy + 2, cz, c2), BF16),
            ((cx, cy, cz, c2), BF16),
            (part, BF16),
            (part, BF16),
            ((c2, c), BF16),
        ],
        [
            pltpu.VMEM((cx + 4, cy + 4, cz, c), BF16),
            pltpu.VMEM((cx + 2, cy + 2, cz, c), BF16),
            pltpu.VMEM((3 * c2, cells), BF16),
            pltpu.VMEM((3 * c2, 10 * c), BF16),
            pltpu.VMEM((c2, c), BF16),
        ],
        6,
    )
    cgot = cores(csend)
    (output,) = call(
        merge_body,
        "merge",
        (hidden, hid_a, hid_b, coarse, merge_weight),
        [((bx, by, bz, c), BF16)],
        [pltpu.VMEM((cx * cy * bz, c), F32)],
        2,
    )
    output, cgot = lax.optimization_barrier((output, cgot))
    csent = spread_sum(ckeep, cgot)
    slope, csent = lax.optimization_barrier((slope, csent))
    cparts = cross(*csent)
    voxels = bx * by * bz
    part = (n // 2, 28 * (c // n), c)
    fkeep, fsend = call(
        functools.partial(back_body, n),
        "back",
        (slope, coarse_kernel, cotangent, ds, ds_a, ds_b, own, xa, xb, cbias),
        [(part, BF16), (part, BF16)],
        [
            pltpu.VMEM((cx * cy * bz, c), F32),
            pltpu.VMEM((3 * c, voxels), BF16),
            pltpu.VMEM((3 * c, 10 * c), BF16),
        ],
        10,
    )

    coarse_sum, fine_sum = side_by_side(
        finish_sum(cparts, places, "coarse", ("half", "sum")),
        lambda got: finish_sum(cross(*spread_sum(fkeep, jnp.stack(got))), places, "fine", ("half", "sum")),
        [cores(part) for part in fsend],
    )
    per, cper = c // n, c2 // n
    grad_coarse, grad_merge = last(coarse_sum, cper, [((cper, c), F32)], "coarse_last")
    fine_sum, grad_merge = lax.optimization_barrier((fine_sum, grad_merge))
    biases = [((1, per), F32), ((1, cper), F32)]
    grad_fine, bias, coarse_sums = last(fine_sum, per, biases, "fine_last")
    return (output, grad_fine, bias[0], grad_coarse, coarse_sums[0], grad_merge)


def solution(mesh):
    in_specs = (P("grp", "sub", None, None), P("grp", "sub", None, None), P(), P(), P(), P(), P())
    out_specs = (
        P("grp", "sub", None, None),
        P(None, None, None, None, "sub"),
        P("sub"),
        P(None, None, None, None, "sub"),
        P("sub"),
        P("sub", None),
    )
    return jax.shard_map(
        per_device, mesh=mesh, in_specs=in_specs, out_specs=out_specs, check_vma=False
    )
```
